32 devices in a mesh: groups: 2 (over x), row: 4 (over y, core), col: 4 (over z).
Axes of the slice: x: 2, y: 2, z: 4, core: 2. Of those that a mesh axis runs over, the one named last changes fastest.
Arguments:
- sender_rows: bfloat16 [2, 256, 8192], P(None, ('groups', 'row', 'col')), parts along dimension 1
- counts: int32 [2, 32], P(None, 'groups'), parts along dimension 1, may hold values from 1 to 8, as said below
- assign: int32 [2, 256], P(None, 'groups'), parts along dimension 1, may hold values from 0 to 63, as said below
- gate_w: bfloat16 [8192, 14336], P('row', 'col'), may hold values from -0.0625 to 0.0625
- up_w: bfloat16 [8192, 14336], P('row', 'col'), may hold values from -0.0625 to 0.0625
- down_w: bfloat16 [14336, 8192], P('col', 'row'), may hold values from -0.046875 to 0.046875
Outputs:
- layer_output: bfloat16 [2, 128, 8192], P(None, ('groups', 'row', 'col')), parts along dimension 1
The draws below stay inside these ranges and needn't reach their ends.
There are 2 independent parts, one for each index of `groups`. The reference program is written for one: setup_inputs(seed, part) draws one part's arguments, and reference() takes and returns one part's arrays. A program takes and returns all parts, laid end to end along the dimension named above; an argument that names none is the same for every part. Nothing has to cross between parts.
Inputs may be any that keep to these rules, and one draw needn't show every extreme that they name: In each step the counts of all senders sum to 64. `assign`: in each step the live entries carry each of 0 to 63 exactly once; the other entries hold arbitrary values of the same range.
All inputs are finite; a program needn't handle non-finite values.
Results may differ from the reference program's by a relative error of at most 0.02.
Values may be sent and summed in bfloat16 or wider, within the bound.
No kernel may reach another device: no remote copies, remote signals or barrier semaphores. Data moves between devices by JAX's collectives and lax.ppermute only.
A program may use at most 192 MiB of HBM per device.

```python
import math
import jax
import jax.numpy as jnp
from jax import lax

D = 8192
FF = 14336
STEPS = 2
MEAN = 4
CAP = 8
SENDERS = 16
ROWS = 64
N_ROW = 4


def counts_table(key):
    tables = []
    for step_index in range(STEPS):
        step_key = jax.random.fold_in(key, 101 + step_index)
        pair_key, order_key = jax.random.split(step_key)
        firsts = jax.random.randint(pair_key, ((SENDERS - 4) // 2,), 1, 2 * MEAN, dtype=jnp.int32)
        pairs = jnp.stack((firsts, 2 * MEAN - firsts), axis=1).reshape(-1)
        opening = jnp.array([2 * MEAN, MEAN // 2, MEAN - MEAN // 2, MEAN], dtype=jnp.int32)
        joined = jnp.concatenate((opening, pairs))
        ordering = jax.random.permutation(order_key, SENDERS).astype(jnp.int32)
        tables.append(joined[ordering])
    return jnp.stack(tables)


def draw_counts(key, part):
    return counts_table(key)


def draw_assign(key, part):
    table = counts_table(key)
    key = jax.random.fold_in(key, 17)
    slot_ids = lax.broadcasted_iota(jnp.int32, (SENDERS, CAP), 1)
    results = []
    for step_index in range(STEPS):
        step_key = jax.random.fold_in(key, step_index)
        perm_key, filler_key = jax.random.split(step_key)
        live_mask = (slot_ids < table[step_index][:, None]).reshape(-1)
        ranking = jnp.cumsum(live_mask.astype(jnp.int32)) - 1
        ordering = jax.random.permutation(perm_key, ROWS).astype(jnp.int32)
        filler = jax.random.randint(filler_key, (SENDERS * CAP,), 0, ROWS, dtype=jnp.int32)
        results.append(jnp.where(live_mask, ordering[jnp.clip(ranking, 0, ROWS - 1)], filler))
    return jnp.stack(results)


def draw_sender_rows(key, part):
    key = jax.random.fold_in(key, 5)
    base_key, row_key, col_key = jax.random.split(key, 3)
    shape = (STEPS, SENDERS * CAP, D)
    base = jax.random.normal(base_key, shape, jnp.float32)
    row_scale = jnp.exp(jax.random.uniform(row_key, (STEPS, SENDERS * CAP, 1), jnp.float32, 0.0, math.log(10.0)))
    col_scale = jnp.exp(jax.random.uniform(col_key, (1, 1, D), jnp.float32, math.log(0.3), math.log(3.0)))
    return (base * row_scale * col_scale).astype(jnp.bfloat16)


def shard_levels(rng, shape, shards, least, largest):
    def one(axis_at, shards_of):
        steps = jax.random.uniform(jax.random.fold_in(jax.random.fold_in(rng, 6), axis_at), (shards_of,), jnp.float32, least / len(shards), largest / len(shards))
        return jnp.repeat(jnp.exp(steps), shape[axis_at] // shards_of).reshape((-1,) + (1,) * (len(shape) - axis_at - 1))

    factor_of = one(*shards[0])
    for cut in shards[1:]:
        factor_of = factor_of * one(*cut)
    return factor_of


def normal_values(stream_key, dims, width, reach, pieces=(), kind=jnp.bfloat16):
    values = width * jax.random.normal(stream_key, dims, jnp.float32)
    if pieces:
        values = values * shard_levels(stream_key, dims, pieces, -0.22, 0.18)
    return jnp.clip(values, -reach, reach).astype(kind)


def setup_inputs(seed: int = 0, part: int = 0) -> dict:
    key_list = jax.random.split(jax.random.key(seed), 7)
    own_keys = jax.random.split(jax.random.fold_in(key_list[6], part), 7)
    sender_rows = draw_sender_rows(jax.random.fold_in(jax.random.fold_in(key_list[6], part), 71), part)
    counts = draw_counts(jax.random.fold_in(jax.random.fold_in(key_list[6], part), 71), part)
    assign = draw_assign(jax.random.fold_in(jax.random.fold_in(key_list[6], part), 71), part)
    gate_w = normal_values(key_list[3], (D, FF), D ** -0.5, 0.0625, ((0, 4), (1, 4)))
    up_w = normal_values(key_list[4], (D, FF), D ** -0.5, 0.0625, ((0, 4), (1, 4)))
    down_w = normal_values(key_list[5], (FF, D), FF ** -0.5, 0.046875, ((0, 4), (1, 4)))
    return dict(sender_rows=sender_rows, counts=counts, assign=assign, gate_w=gate_w, up_w=up_w, down_w=down_w)


epsilon = 1e-05

def reference(sender_rows, counts, assign, gate_w, up_w, down_w):
    values = sender_rows.astype(jnp.float32)
    normed = (values * lax.rsqrt(lax.optimization_barrier(jnp.mean(values * values, axis=-1, keepdims=True)) + epsilon)).astype(jnp.bfloat16)
    slot_ids = lax.broadcasted_iota(jnp.int32, (STEPS, SENDERS * CAP), 1)
    step_ids = lax.broadcasted_iota(jnp.int32, (STEPS, SENDERS * CAP), 0)
    holdings = jnp.take_along_axis(counts, slot_ids // CAP, axis=1)
    live_mask = slot_ids % CAP < holdings
    targets = jnp.where(live_mask, assign, ROWS)
    inverse = jnp.zeros((STEPS, ROWS), jnp.int32).at[step_ids, targets].set(slot_ids, mode='drop')
    picked = jax.vmap(lambda table, picks: jnp.take(table, picks, axis=0))(normed, inverse)
    all_rows = picked.reshape(STEPS * ROWS, D)
    paired = jnp.concatenate((gate_w, up_w), axis=1)
    block_width = D // N_ROW

    def add_block(carry, block_index):
        start_at = (block_index * block_width).astype(jnp.int32)
        columns = lax.dynamic_slice_in_dim(all_rows, start_at, block_width, 1)
        weights = lax.dynamic_slice_in_dim(paired, start_at, block_width, 0)
        partial_sum = lax.optimization_barrier(jnp.dot(columns, weights, preferred_element_type=jnp.float32).astype(jnp.bfloat16))
        return (carry + partial_sum.astype(jnp.float32), None)
    initial = jnp.zeros((STEPS * ROWS, 2 * FF), jnp.float32)
    gate_up, unused = lax.scan(add_block, initial, jnp.arange(N_ROW, dtype=jnp.int32))
    hidden = (jax.nn.silu(gate_up[:, :FF]) * gate_up[:, FF:]).astype(jnp.bfloat16)
    result = jnp.dot(hidden, down_w, preferred_element_type=jnp.float32).astype(jnp.bfloat16)
    return result.reshape(STEPS, ROWS, D)
```

```python
import functools

import jax
import jax.numpy as jnp
from jax import lax
from jax.experimental import pallas as pl
from jax.experimental.pallas import tpu as pltpu
from jax.sharding import PartitionSpec as P

STEPS = 2
MEAN = 4

epsilon = 1e-05

BF = jnp.bfloat16
F32 = jnp.float32
MIB = 2**20
X1 = ((0, 1), (1, 0), (2, 3), (3, 2))
X2 = ((0, 2), (1, 3), (2, 0), (3, 1))
X3 = ((0, 3), (1, 2), (2, 1), (3, 0))
Z_ORDER = (0, 3, 1, 2)


def vmem_spec():
    return pl.BlockSpec(memory_space=pltpu.VMEM)


def call(body, outs, specs, scratch=(), limit=24, cost=None):
    return pl.pallas_call(
        body,
        out_shape=outs,
        in_specs=specs,
        out_specs=jax.tree.map(lambda _: vmem_spec(), outs),
        scratch_shapes=scratch,
        compiler_params=pltpu.CompilerParams(vmem_limit_bytes=limit * MIB),
        cost_estimate=cost,
    )


def place():
    row = lax.axis_index("row")
    return row // 2, lax.rem(row, 2), lax.axis_index("col")


def norm_body(rows_ref, own_ref, core_ref, y_ref, yd_ref):
    y, c, _ = place()
    width = own_ref.shape[2]
    for step in range(rows_ref.shape[0]):
        total = jnp.sum(jnp.square(rows_ref[step].astype(F32)), axis=-1, keepdims=True)
        scale = lax.rsqrt(total / rows_ref.shape[2] + epsilon)
        for dy, dc, out in ((0, 0, own_ref), (0, 1, core_ref), (1, 0, y_ref), (1, 1, yd_ref)):
            block = lax.bitwise_xor(y, dy) * 2 + lax.bitwise_xor(c, dc)
            at = pl.ds(pl.multiple_of(block * width, width), width)
            out[step] = (rows_ref[step, :, at].astype(F32) * scale).astype(BF)


def normed_blocks(sender_rows):
    steps, slots, width = sender_rows.shape
    one = jax.ShapeDtypeStruct((steps, slots, width // 4), BF)
    return call(norm_body, (one,) * 4, [vmem_spec()])(sender_rows)


def pick_body(counts_ref, assign_ref, pick_ref):
    y, c, z = place()
    rows = pick_ref.shape[0] // 2
    slots = assign_ref.shape[1]
    arrivals = pick_ref.shape[1]
    spread = (
        lax.broadcasted_iota(jnp.int32, (slots // 8, slots), 1) // 8
        == lax.broadcasted_iota(jnp.int32, (slots // 8, slots), 0)
    ).astype(F32)
    held = jnp.dot(counts_ref[...].astype(F32), spread, preferred_element_type=F32)
    slot = lax.rem(lax.broadcasted_iota(jnp.int32, (1, slots), 1), 8).astype(F32)
    at = lax.broadcasted_iota(jnp.int32, (rows, slots), 0)
    dz = at // 16
    dz = jnp.where(dz == 0, 0, jnp.where(dz == 1, 3, dz - 1))
    target = (lax.rem(at, 16) // 4) * 16 + lax.bitwise_xor(dz, z) * 4 + lax.rem(at, 4)
    p = lax.broadcasted_iota(jnp.int32, (slots, arrivals), 1)
    bit = lambda shift: lax.rem(lax.shift_right_logical(p, shift), 2)
    row = lax.bitwise_xor(bit(5), y) * 2 + lax.bitwise_xor(bit(4), c)
    sender = row * 4 + lax.bitwise_xor(lax.shift_right_logical(p, 6), z)
    source = sender * 8 + lax.rem(p, 8)
    entry = lax.broadcasted_iota(jnp.int32, (slots, arrivals), 0)
    for step in range(2):
        live = slot < held[step : step + 1]
        chosen = jnp.where(live, assign_ref[step : step + 1, :], -1)
        placed = (chosen == target).astype(F32).astype(BF)
        moved = ((entry == source) & (bit(3) == step)).astype(F32).astype(BF)
        pick_ref[step * rows : (step + 1) * rows, :] = jnp.dot(
            placed, moved, preferred_element_type=F32
        ).astype(BF)


def pick_matrix(counts, assign):
    rows = MEAN * counts.shape[1]
    return call(
        pick_body,
        jax.ShapeDtypeStruct((2 * rows, 2 * assign.shape[1]), BF),
        [vmem_spec()] * 2,
    )(counts, assign)


def fetch_columns_body(other, w_ref, out_ref, sem):
    _, c, _ = place()
    width = out_ref.shape[1]
    half = lax.bitwise_xor(c, other)
    copy = pltpu.make_async_copy(
        w_ref.at[:, pl.ds(pl.multiple_of(half * width, 128), width)], out_ref, sem
    )
    copy.start()
    copy.wait()


def fetch_columns(w, other):
    return pl.pallas_call(
        functools.partial(fetch_columns_body, other),
        out_shape=pltpu.VMEM((w.shape[0], w.shape[1] // 2), BF),
        in_specs=[pl.BlockSpec(memory_space=pl.ANY)],
        out_specs=vmem_spec(),
        scratch_shapes=[pltpu.SemaphoreType.DMA],
        compiler_params=pltpu.CompilerParams(vmem_limit_bytes=MIB),
        cost_estimate=pl.CostEstimate(flops=0, bytes_accessed=w.size * 2, transcendentals=0),
    )(w)


def fetch_rows_body(other, w_ref, out_ref, sem):
    _, c, _ = place()
    height = out_ref.shape[0]
    half = lax.bitwise_xor(c, other)
    copy = pltpu.make_async_copy(
        w_ref.at[pl.ds(pl.multiple_of(half * height, 16), height), :], out_ref, sem
    )
    copy.start()
    copy.wait()


def fetch_rows(w, other):
    return pl.pallas_call(
        functools.partial(fetch_rows_body, other),
        out_shape=pltpu.VMEM((w.shape[0] // 2, w.shape[1]), BF),
        in_specs=[pl.BlockSpec(memory_space=pl.ANY)],
        out_specs=vmem_spec(),
        scratch_shapes=[pltpu.SemaphoreType.DMA],
        compiler_params=pltpu.CompilerParams(vmem_limit_bytes=MIB),
        cost_estimate=pl.CostEstimate(flops=0, bytes_accessed=w.size * 2, transcendentals=0),
    )(w)


def quarter(ref, dy):
    y, _, _ = place()
    width = ref.shape[1] // 2
    return ref[:, pl.ds(pl.multiple_of(lax.bitwise_xor(y, dy) * width, 128), width)]


def first_body(*refs):
    pieces, (pick_ref, gate_ref, up_ref, batch_ref, far_ref, near_ref, slots) = refs[:8], refs[8:]
    height = pieces[0].shape[0]
    for i, piece in enumerate(pieces):
        slots[i * height : (i + 1) * height, :] = piece[...]
    batch_ref[...] = jnp.dot(pick_ref[...], slots[...], preferred_element_type=F32).astype(BF)
    width = gate_ref.shape[1] // 2
    for dy, out in ((1, far_ref), (0, near_ref)):
        for i, w in enumerate((gate_ref, up_ref)):
            out[:, i * width : (i + 1) * width] = jnp.dot(
                batch_ref[...], quarter(w, dy), preferred_element_type=F32
            ).astype(BF)


def first_half(pieces, pick, gate, up):
    rows = pick.shape[0]
    out = jax.ShapeDtypeStruct((rows, gate.shape[1]), BF)
    height, width = pieces[0].shape
    return call(
        first_body,
        (jax.ShapeDtypeStruct((rows, width), BF), out, out),
        [vmem_spec()] * 11,
        scratch=[pltpu.VMEM((8 * height, width), BF)],
    )(*pieces, pick, gate, up)


def far_body(batch_ref, gate_ref, up_ref, got_ref, *outs):
    width = gate_ref.shape[1] // 2
    rows = outs[0].shape[0]
    for i, w in enumerate((gate_ref, up_ref)):
        at = slice(i * width, (i + 1) * width)
        total = jnp.dot(batch_ref[...], quarter(w, 1), preferred_element_type=F32)
        total = (total + got_ref[:, at].astype(F32)).astype(BF)
        for step, out in enumerate(outs):
            out[:, at] = total[step * rows : (step + 1) * rows]


def far_sums(batch, gate, up, got):
    out = jax.ShapeDtypeStruct((batch.shape[0] // 2, gate.shape[1]), BF)
    return call(far_body, (out, out), [vmem_spec()] * 4)(batch, gate, up, got)


def near_body(batch_ref, gate_ref, up_ref, got_ref, *outs):
    width = gate_ref.shape[1] // 2
    rows = outs[0].shape[0]
    for i, w in enumerate((gate_ref, up_ref)):
        at = slice(i * width, (i + 1) * width)
        total = jnp.dot(batch_ref[...], quarter(w, 0), preferred_element_type=F32)
        total = total + got_ref[:, at].astype(F32)
        for step, out in enumerate(outs):
            out[:, at] = total[step * rows : (step + 1) * rows]


def near_sums(batch, gate, up, got):
    out = jax.ShapeDtypeStruct((batch.shape[0] // 2, gate.shape[1]), F32)
    return call(near_body, (out, out), [vmem_spec()] * 4)(batch, gate, up, got)


def hidden_body(near_ref, got_ref, hidden_ref):
    width = hidden_ref.shape[1]
    total = near_ref[...] + got_ref[...].astype(F32)
    gate, up = total[:, :width], total[:, width:]
    hidden_ref[...] = (gate / (1.0 + jnp.exp(-gate)) * up).astype(BF)


def hidden_units(near, got):
    out = jax.ShapeDtypeStruct((near.shape[0], near.shape[1] // 2), BF)
    return call(hidden_body, out, [vmem_spec()] * 2)(near, got)


def down_body(own_ref, core_ref, y_ref, yd_ref, down0_ref, down1_ref, keep_ref, send_ref):
    y, _, _ = place()
    height = down0_ref.shape[0] // 2
    rows = keep_ref.shape[0]
    total = 0.0
    for dy, hidden, down in ((0, own_ref, down0_ref), (0, core_ref, down1_ref), (1, y_ref, down0_ref), (1, yd_ref, down1_ref)):
        at = pl.ds(pl.multiple_of(lax.bitwise_xor(y, dy) * height, 16), height)
        total = total + jnp.dot(hidden[...], down[at, :], preferred_element_type=F32)
    keep_ref[...] = total[:rows]
    send_ref[...] = total[rows:].astype(BF)


def down_sums(hidden, down):
    rows, width = hidden[0].shape[0] // 2, down[0].shape[1]
    return call(
        down_body,
        (jax.ShapeDtypeStruct((rows, width), F32), jax.ShapeDtypeStruct((rows, width), BF)),
        [vmem_spec()] * 6,
    )(*hidden, *down)


def pair_body(keep_ref, got_ref, own_ref, send_ref):
    rows = own_ref.shape[0]
    total = keep_ref[...] + got_ref[...].astype(F32)
    own_ref[...] = total[:rows]
    send_ref[...] = total[rows:].astype(BF)


def pair_sums(keep, got):
    rows, width = keep.shape[0] // 2, keep.shape[1]
    return call(
        pair_body,
        (jax.ShapeDtypeStruct((rows, width), F32), jax.ShapeDtypeStruct((rows, width), BF)),
        [vmem_spec()] * 2,
    )(keep, got)


def owner_body(keep0_ref, keep1_ref, got0_ref, got1_ref, *outs):
    y, c, _ = place()
    at = lax.broadcasted_iota(jnp.int32, (16, 16), 0)
    source = lax.bitwise_xor(at, (y * 2 + c) * 4)
    turn = (lax.broadcasted_iota(jnp.int32, (16, 16), 1) == source).astype(F32).astype(BF)
    for step, (keep, got) in enumerate(((keep0_ref, got0_ref), (keep1_ref, got1_ref))):
        total = (keep[...] + got[...].astype(F32)).astype(BF)
        turned = jnp.dot(turn, total, preferred_element_type=F32)
        for i, out in enumerate(outs):
            out[step] = turned[i * 4 : (i + 1) * 4].astype(BF)


def owner_blocks(keep, got):
    out = jax.ShapeDtypeStruct((2, 4, keep[0].shape[1]), BF)
    return call(owner_body, (out,) * 4, [vmem_spec()] * 4)(*keep, *got)


def output_body(own_ref, core_ref, y_ref, yd_ref, out_ref):
    y, c, _ = place()
    width = own_ref.shape[2]
    for dy, dc, block in ((0, 0, own_ref), (0, 1, core_ref), (1, 0, y_ref), (1, 1, yd_ref)):
        source = lax.bitwise_xor(y, dy) * 2 + lax.bitwise_xor(c, dc)
        out_ref[:, :, pl.ds(pl.multiple_of(source * width, width), width)] = block[...]


def output_rows(blocks):
    steps, rows, width = blocks[0].shape
    return call(output_body, jax.ShapeDtypeStruct((steps, rows, 4 * width), BF), [vmem_spec()] * 4)(*blocks)


def exchange(blocks):
    own, core, y, yd = blocks
    y = lax.ppermute(y, "row", X2)
    yd = lax.ppermute(yd, "row", X3)
    core = lax.ppermute(core, "row", X1)
    return own, core, y, yd


def near_plan(sender_rows, counts, assign, gate_w, up_w, down_w):
    steps, slots, _ = sender_rows.shape
    own, core, y, yd = exchange(normed_blocks(sender_rows))
    pick = pick_matrix(counts, assign)
    arrived = []
    for pair in ((own, core), (y, yd)):
        block = jnp.concatenate([p.reshape(steps * slots, -1) for p in pair], axis=0)
        far = lax.ppermute(block, "col", X3)
        near = lax.ppermute(block, "col", X1)
        arrived.append((block, near, lax.ppermute(far, "col", X1), far))
    pieces = [arrived[dy][dz] for dz in range(4) for dy in range(2)]
    gate1, up1 = fetch_columns(gate_w, 1), fetch_columns(up_w, 1)
    gate0, up0 = fetch_columns(gate_w, 0), fetch_columns(up_w, 0)
    batch, far, near = first_half(pieces, pick, gate1, up1)
    far = lax.ppermute(far, "row", X1)
    near = lax.ppermute(near, "row", X1)
    sends = far_sums(batch, gate0, up0, far)
    keeps = near_sums(batch, gate0, up0, near)
    down0, down1 = fetch_rows(down_w, 0), fetch_rows(down_w, 1)
    owns, lasts = [], []
    for step in range(steps):
        hidden = hidden_units(keeps[step], lax.ppermute(sends[step], "row", X2))
        hidden_y = lax.ppermute(hidden, "row", X2)
        hidden_core = lax.ppermute(hidden, "row", X1)
        hidden_yd = lax.ppermute(hidden_y, "row", X1)
        keep, send = down_sums((hidden, hidden_core, hidden_y, hidden_yd), (down0, down1))
        keep, send = pair_sums(keep, lax.ppermute(send, "col", X1))
        owns.append(keep)
        lasts.append(lax.ppermute(send, "col", X3))
    return output_rows(exchange(owner_blocks(owns, lasts)))


def layer_block(normed_block, counts_block, assign_block, paired, down_w, hidden_cols):
    row_devices = lax.axis_size("row")
    col_devices = lax.axis_size("col")
    step_count = normed_block.shape[0]
    capacity = normed_block.shape[1]
    rows_step = MEAN * counts_block.shape[1]
    spread = lax.all_to_all(normed_block, "row", split_axis=2, concat_axis=1, tiled=True)
    gathered = lax.all_gather(spread, "col", axis=1, tiled=True)
    slot_count = gathered.shape[1]
    stacked = gathered.reshape(step_count * slot_count, gathered.shape[2])
    targets = (
        assign_block.reshape(step_count, row_devices, col_devices, capacity)
        .transpose(0, 2, 1, 3)
        .reshape(step_count, slot_count)
    )
    holdings = counts_block.reshape(step_count, row_devices, col_devices).transpose(0, 2, 1)
    slot_grid = lax.broadcasted_iota(jnp.int32, (step_count, col_devices, row_devices, capacity), 3)
    live_mask = (slot_grid < holdings[..., None]).reshape(step_count, slot_count)
    targets = jnp.where(live_mask, targets, rows_step)
    slot_ids = lax.broadcasted_iota(jnp.int32, (step_count, slot_count), 1)
    step_ids = lax.broadcasted_iota(jnp.int32, (step_count, slot_count), 0)
    inverse = (
        jnp.zeros((step_count, rows_step), jnp.int32)
        .at[step_ids, targets]
        .set(slot_ids, mode="drop")
    )
    grid_shape = (col_devices, row_devices, step_count, MEAN)
    col_ids = lax.broadcasted_iota(jnp.int32, grid_shape, 0)
    row_ids = lax.broadcasted_iota(jnp.int32, grid_shape, 1)
    step_grid = lax.broadcasted_iota(jnp.int32, grid_shape, 2)
    member = lax.broadcasted_iota(jnp.int32, grid_shape, 3)
    row_numbers = (row_ids * col_devices + col_ids) * MEAN + member
    positions = (step_grid * slot_count + inverse[step_grid, row_numbers]).reshape(-1)
    inputs = jnp.take(stacked, positions, axis=0)
    rows_here = inputs
    gate_up = lax.psum_scatter(
        jnp.dot(rows_here, paired, preferred_element_type=jnp.float32).astype(jnp.bfloat16),
        "row",
        scatter_dimension=0,
        tiled=True,
    ).astype(jnp.float32)
    hidden = (jax.nn.silu(gate_up[:, :hidden_cols]) * gate_up[:, hidden_cols:]).astype(jnp.bfloat16)
    hidden_all = lax.all_gather(hidden, "row", axis=0, tiled=True)
    rows_here = hidden_all
    summed = lax.psum_scatter(
        jnp.dot(rows_here, down_w, preferred_element_type=jnp.float32).astype(jnp.bfloat16),
        "col",
        scatter_dimension=0,
        tiled=True,
    )
    finished = lax.all_to_all(summed, "row", split_axis=0, concat_axis=1, tiled=True)
    return finished.reshape(step_count, MEAN, finished.shape[1])


def any_plan(sender_rows, counts, assign, gate_w, up_w, down_w):
    values = sender_rows.astype(jnp.float32)
    normed = (
        values * lax.rsqrt(jnp.mean(values * values, axis=-1, keepdims=True) + epsilon)
    ).astype(jnp.bfloat16)
    paired = jnp.concatenate((gate_w, up_w), axis=1)
    hidden_cols = gate_w.shape[1]
    outputs = []
    for step_index in range(STEPS):
        outputs.append(
            layer_block(
                normed[step_index : step_index + 1],
                counts[step_index : step_index + 1],
                assign[step_index : step_index + 1],
                paired,
                down_w,
                hidden_cols,
            )
        )
    result = jnp.concatenate(outputs, axis=0)
    return result


def solution(mesh):
    near = mesh.shape["row"] == 4 and mesh.shape["col"] == 4
    return jax.shard_map(
        near_plan if near else any_plan,
        mesh=mesh,
        in_specs=(
            P(None, ("groups", "row", "col"), None),
            P(None, "groups"),
            P(None, "groups"),
            P("row", "col"),
            P("row", "col"),
            P("col", "row"),
        ),
        out_specs=P(None, ("groups", "row", "col"), None),
        check_vma=False,
    )
```

```python
import functools

import jax
import jax.numpy as jnp
from jax import lax
from jax.experimental import pallas as pl
from jax.experimental.pallas import tpu as pltpu
from jax.sharding import PartitionSpec as P

STEPS = 2
MEAN = 4

epsilon = 1e-05

BF = jnp.bfloat16
F32 = jnp.float32
MIB = 2**20
X1 = ((0, 1), (1, 0), (2, 3), (3, 2))
X2 = ((0, 2), (1, 3), (2, 0), (3, 1))
X3 = ((0, 3), (1, 2), (2, 1), (3, 0))


def vmem_spec():
    return pl.BlockSpec(memory_space=pltpu.VMEM)


def call(body, outs, specs, scratch=(), limit=24, cost=None):
    return pl.pallas_call(
        body,
        out_shape=outs,
        in_specs=specs,
        out_specs=jax.tree.map(lambda _: vmem_spec(), outs),
        scratch_shapes=scratch,
        compiler_params=pltpu.CompilerParams(vmem_limit_bytes=limit * MIB),
        cost_estimate=cost,
    )


def place():
    row = lax.axis_index("row")
    return row // 2, lax.rem(row, 2), lax.axis_index("col")


def norm_body(rows_ref, own_ref, core_ref, y_ref, yd_ref):
    y, c, _ = place()
    width = own_ref.shape[2]
    for step in range(rows_ref.shape[0]):
        total = jnp.sum(jnp.square(rows_ref[step].astype(F32)), axis=-1, keepdims=True)
        scale = lax.rsqrt(total / rows_ref.shape[2] + epsilon)
        for dy, dc, out in ((0, 0, own_ref), (0, 1, core_ref), (1, 0, y_ref), (1, 1, yd_ref)):
            block = lax.bitwise_xor(y, dy) * 2 + lax.bitwise_xor(c, dc)
            at = pl.ds(pl.multiple_of(block * width, width), width)
            out[step] = (rows_ref[step, :, at].astype(F32) * scale).astype(BF)


def normed_blocks(sender_rows):
    steps, slots, width = sender_rows.shape
    one = jax.ShapeDtypeStruct((steps, slots, width // 4), BF)
    return call(norm_body, (one,) * 4, [vmem_spec()])(sender_rows)


def pick_body(counts_ref, assign_ref, pick_ref):
    y, c, z = place()
    rows = pick_ref.shape[0] // 2
    slots = assign_ref.shape[1]
    arrivals = pick_ref.shape[1]
    spread = (
        lax.broadcasted_iota(jnp.int32, (slots // 8, slots), 1) // 8
        == lax.broadcasted_iota(jnp.int32, (slots // 8, slots), 0)
    ).astype(F32)
    held = jnp.dot(counts_ref[...].astype(F32), spread, preferred_element_type=F32)
    slot = lax.rem(lax.broadcasted_iota(jnp.int32, (1, slots), 1), 8).astype(F32)
    at = lax.broadcasted_iota(jnp.int32, (rows, slots), 0)
    target = (lax.rem(at, 16) // 4) * 16 + lax.bitwise_xor(at // 16, z) * 4 + lax.rem(at, 4)
    p = lax.broadcasted_iota(jnp.int32, (slots, arrivals), 1)
    bit = lambda shift: lax.rem(lax.shift_right_logical(p, shift), 2)
    row = lax.bitwise_xor(bit(5), y) * 2 + lax.bitwise_xor(bit(4), c)
    sender = row * 4 + lax.bitwise_xor(lax.shift_right_logical(p, 6), z)
    source = sender * 8 + lax.rem(p, 8)
    entry = lax.broadcasted_iota(jnp.int32, (slots, arrivals), 0)
    for step in range(2):
        live = slot < held[step : step + 1]
        chosen = jnp.where(live, assign_ref[step : step + 1, :], -1)
        placed = (chosen == target).astype(F32).astype(BF)
        moved = ((entry == source) & (bit(3) == step)).astype(F32).astype(BF)
        pick_ref[step * rows : (step + 1) * rows, :] = jnp.dot(
            placed, moved, preferred_element_type=F32
        ).astype(BF)


def pick_matrix(counts, assign):
    rows = MEAN * counts.shape[1]
    return call(
        pick_body,
        jax.ShapeDtypeStruct((2 * rows, 2 * assign.shape[1]), BF),
        [vmem_spec()] * 2,
    )(counts, assign)


def fetch_gate_up_body(dy, dc, gate_ref, up_ref, out_ref, token_ref, sems):
    y, c, _ = place()
    width = out_ref.shape[1] // 2
    start = (lax.bitwise_xor(c, dc) * 2 + lax.bitwise_xor(y, dy)) * width
    copies = []
    for i, w in enumerate((gate_ref, up_ref)):
        copies.append(
            pltpu.make_async_copy(
                w.at[:, pl.ds(pl.multiple_of(start, 128), width)],
                out_ref.at[:, pl.ds(i * width, width)],
                sems.at[i],
            )
        )
    for copy in copies:
        copy.start()
    token_ref[...] = jnp.zeros_like(token_ref)
    for copy in copies:
        copy.wait()


def fetch_down_body(dy, down_ref, out_ref, token_ref, sems):
    y, c, _ = place()
    height = out_ref.shape[0] // 2
    copies = []
    for dc in range(2):
        start = (lax.bitwise_xor(c, dc) * 2 + lax.bitwise_xor(y, dy)) * height
        copies.append(
            pltpu.make_async_copy(
                down_ref.at[pl.ds(pl.multiple_of(start, 16), height), :],
                out_ref.at[pl.ds(dc * height, height), :],
                sems.at[dc],
            )
        )
    for copy in copies:
        copy.start()
    token_ref[...] = jnp.zeros_like(token_ref)
    for copy in copies:
        copy.wait()


def fetch(body, shape, *weights):
    out, token = pl.pallas_call(
        body,
        out_shape=(pltpu.VMEM(shape, BF), jax.ShapeDtypeStruct((8, 128), F32)),
        in_specs=[pl.BlockSpec(memory_space=pltpu.HBM)] * len(weights),
        out_specs=(vmem_spec(), vmem_spec()),
        scratch_shapes=[pltpu.SemaphoreType.DMA((2,))],
        compiler_params=pltpu.CompilerParams(vmem_limit_bytes=MIB),
        cost_estimate=pl.CostEstimate(
            flops=0, bytes_accessed=2 * shape[0] * shape[1], transcendentals=0
        ),
    )(*(pltpu.with_memory_space_constraint(w, pltpu.HBM) for w in weights))
    return out, token


def fetch_gate_up(gate_w, up_w, dy, dc):
    shape = (gate_w.shape[0], gate_w.shape[1] // 2)
    return fetch(functools.partial(fetch_gate_up_body, dy, dc), shape, gate_w, up_w)


def fetch_down(down_w, dy):
    shape = (down_w.shape[0] // 2, down_w.shape[1])
    return fetch(functools.partial(fetch_down_body, dy), shape, down_w)


def stack_body(first_ref, second_ref, *refs):
    out_ref = refs[-1]
    for i, piece in enumerate((first_ref, second_ref)):
        for step in range(2):
            at = (i * 2 + step) * 8
            out_ref[at : at + 8, :] = piece[step]


def stack(first, second, *tokens):
    steps, slots, width = first.shape
    out = jax.ShapeDtypeStruct((2 * steps * slots, width), BF)
    return call(stack_body, out, [vmem_spec()] * (2 + len(tokens)))(first, second, *tokens)


def after_body(x_ref, *refs):
    refs[-1][...] = x_ref[...]


def after(x, *tokens):
    out = jax.ShapeDtypeStruct(x.shape, x.dtype)
    return call(after_body, out, [vmem_spec()] * (1 + len(tokens)))(x, *tokens)


def first_body(*refs):
    pieces, (pick_ref, w_ref, _, batch_ref, out_ref, slots) = refs[:8], refs[8:]
    height = pieces[0].shape[0]
    for i, piece in enumerate(pieces):
        slots[i * height : (i + 1) * height, :] = piece[...]
    batch_ref[...] = jnp.dot(pick_ref[...], slots[...], preferred_element_type=F32).astype(BF)
    out_ref[...] = jnp.dot(batch_ref[...], w_ref[...], preferred_element_type=F32).astype(BF)


def first_sums(pieces, pick, w, token):
    rows = pick.shape[0]
    height, width = pieces[0].shape
    return call(
        first_body,
        (jax.ShapeDtypeStruct((rows, width), BF), jax.ShapeDtypeStruct((rows, w.shape[1]), BF)),
        [vmem_spec()] * 11,
        scratch=[pltpu.VMEM((8 * height, width), BF)],
        cost=pl.CostEstimate(flops=2 * rows * w.size, bytes_accessed=2 * w.size, transcendentals=0),
    )(*pieces, pick, w, token)


def dot_body(x_ref, w_ref, *refs):
    out_ref = refs[-1]
    out_ref[...] = jnp.dot(x_ref[...], w_ref[...], preferred_element_type=F32).astype(out_ref.dtype)


def dot(x, w, dtype, *tokens):
    rows = x.shape[0]
    return call(
        dot_body,
        jax.ShapeDtypeStruct((rows, w.shape[1]), dtype),
        [vmem_spec()] * (2 + len(tokens)),
        cost=pl.CostEstimate(flops=2 * rows * w.size, bytes_accessed=2 * w.size, transcendentals=0),
    )(x, w, *tokens)


def far_body(own_ref, got_ref, *outs):
    rows = outs[0].shape[0]
    for step, out in enumerate(outs):
        at = slice(step * rows, (step + 1) * rows)
        out[...] = (own_ref[at, :] + got_ref[at, :].astype(F32)).astype(BF)


def far_sums(own, got):
    out = jax.ShapeDtypeStruct((own.shape[0] // 2, own.shape[1]), BF)
    return call(far_body, (out, out), [vmem_spec()] * 2)(own, got)


def hidden_body(step, own_ref, core_ref, y_ref, *refs):
    hidden_ref = refs[-1]
    rows, width = hidden_ref.shape
    at = slice(step * rows, (step + 1) * rows)
    total = own_ref[at, :] + core_ref[at, :].astype(F32) + y_ref[...].astype(F32)
    gate, up = total[:, :width], total[:, width:]
    hidden_ref[...] = (gate / (1.0 + jnp.exp(-gate)) * up).astype(BF)


def hidden_units(step, own, core, y, *tokens):
    out = jax.ShapeDtypeStruct((y.shape[0], y.shape[1] // 2), BF)
    return call(functools.partial(hidden_body, step), out, [vmem_spec()] * (3 + len(tokens)))(
        own, core, y, *tokens
    )


def down_body(own_ref, core_ref, down_ref, out_ref):
    height = down_ref.shape[0] // 2
    total = jnp.dot(own_ref[...], down_ref[:height, :], preferred_element_type=F32)
    out_ref[...] = total + jnp.dot(core_ref[...], down_ref[height:, :], preferred_element_type=F32)


def down_rest_body(y_ref, yd_ref, down_ref, part_ref, keep_ref, *outs):
    height = down_ref.shape[0] // 2
    rows = keep_ref.shape[0]
    total = part_ref[...] + jnp.dot(y_ref[...], down_ref[:height, :], preferred_element_type=F32)
    total = total + jnp.dot(yd_ref[...], down_ref[height:, :], preferred_element_type=F32)
    keep_ref[...] = total[:rows]
    for i, out in enumerate(outs):
        out[...] = total[(i + 1) * rows : (i + 2) * rows].astype(BF)


def down_cost(rows, down):
    return pl.CostEstimate(flops=2 * rows * down.size, bytes_accessed=2 * down.size, transcendentals=0)


def down_part(own, core, down):
    rows = own.shape[0]
    out = jax.ShapeDtypeStruct((rows, down.shape[1]), F32)
    return call(down_body, out, [vmem_spec()] * 3, cost=down_cost(rows, down))(own, core, down)


def down_rest(y, yd, down, part):
    rows, width = part.shape
    send = jax.ShapeDtypeStruct((rows // 4, width), BF)
    keep = jax.ShapeDtypeStruct((rows // 4, width), F32)
    return call(
        down_rest_body, (keep, send, send, send), [vmem_spec()] * 4, cost=down_cost(rows, down)
    )(y, yd, down, part)


def owner_body(*refs):
    sums, outs = refs[:8], refs[8:]
    y, c, _ = place()
    at = lax.broadcasted_iota(jnp.int32, (16, 16), 0)
    source = lax.bitwise_xor(at, (y * 2 + c) * 4)
    turn = (lax.broadcasted_iota(jnp.int32, (16, 16), 1) == source).astype(F32).astype(BF)
    for step in range(2):
        total = sums[step * 4][...]
        for got in sums[step * 4 + 1 : step * 4 + 4]:
            total = total + got[...].astype(F32)
        turned = jnp.dot(turn, total.astype(BF), preferred_element_type=F32)
        for i, out in enumerate(outs):
            out[step] = turned[i * 4 : (i + 1) * 4].astype(BF)


def owner_blocks(sums):
    out = jax.ShapeDtypeStruct((2, 4, sums[0].shape[1]), BF)
    return call(owner_body, (out,) * 4, [vmem_spec()] * 8)(*sums)


def output_body(own_ref, core_ref, y_ref, yd_ref, out_ref):
    y, c, _ = place()
    width = own_ref.shape[2]
    for dy, dc, block in ((0, 0, own_ref), (0, 1, core_ref), (1, 0, y_ref), (1, 1, yd_ref)):
        source = lax.bitwise_xor(y, dy) * 2 + lax.bitwise_xor(c, dc)
        out_ref[:, :, pl.ds(pl.multiple_of(source * width, width), width)] = block[...]


def output_rows(blocks):
    steps, rows, width = blocks[0].shape
    out = jax.ShapeDtypeStruct((steps, rows, 4 * width), BF)
    return call(output_body, out, [vmem_spec()] * 4)(*blocks)


def exchange(blocks):
    own, core, y, yd = blocks
    core = lax.ppermute(core, "row", X1)
    y = lax.ppermute(y, "row", X2)
    yd = lax.ppermute(yd, "row", X3)
    return own, core, y, yd


def near_plan(sender_rows, counts, assign, gate_w, up_w, down_w):
    pick = pick_matrix(counts, assign)
    own, core, y, yd = exchange(normed_blocks(sender_rows))
    w_first, token_first = fetch_gate_up(gate_w, up_w, 1, 1)
    w_second, token_second = fetch_gate_up(gate_w, up_w, 1, 0)
    w_third, token_third = fetch_gate_up(gate_w, up_w, 0, 1)
    arrived = []
    block_near = stack(own, core)
    block_far = stack(y, yd, block_near)
    for block, token in ((block_near, token_first), (block_far, token_second)):
        far = lax.ppermute(block, "col", X3)
        near = lax.ppermute(block, "col", X1)
        arrived.append((block, near, lax.ppermute(after(far, near, token), "col", X1), far))
    pieces = [arrived[dy][dz] for dz in range(4) for dy in range(2)]
    batch, far_core = first_sums(pieces, pick, w_first, token_third)
    far_core = lax.ppermute(far_core, "row", X1)
    sends = far_sums(dot(batch, w_second, F32), far_core)
    gots = [lax.ppermute(send, "row", X2) for send in sends]
    near_core = lax.ppermute(dot(batch, w_third, BF, sends[0]), "row", X1)
    w_fourth, _ = fetch_gate_up(gate_w, up_w, 0, 0)
    near = dot(batch, w_fourth, F32)
    down_near, token_near = fetch_down(down_w, 0)
    down_far, token_far = fetch_down(down_w, 1)
    sums = []
    tokens = [token_near]
    for step, got in enumerate(gots):
        hidden = hidden_units(step, near, near_core, got, *tokens)
        hidden_y = lax.ppermute(hidden, "row", X2)
        hidden_core = lax.ppermute(hidden, "row", X1)
        hidden_yd = lax.ppermute(hidden_y, "row", X1)
        part = down_part(hidden, hidden_core, down_near)
        tokens = [token_far, part]
        keep, send1, send2, send3 = down_rest(hidden_y, hidden_yd, down_far, part)
        sums.append(keep)
        for send, pairs in ((send3, X3), (send2, X2), (send1, X1)):
            sums.append(lax.ppermute(send, "col", pairs))
    return output_rows(exchange(owner_blocks(sums)))


def layer_block(normed_block, counts_block, assign_block, paired, down_w, hidden_cols):
    row_devices = lax.axis_size("row")
    col_devices = lax.axis_size("col")
    step_count = normed_block.shape[0]
    capacity = normed_block.shape[1]
    rows_step = MEAN * counts_block.shape[1]
    spread = lax.all_to_all(normed_block, "row", split_axis=2, concat_axis=1, tiled=True)
    gathered = lax.all_gather(spread, "col", axis=1, tiled=True)
    slot_count = gathered.shape[1]
    stacked = gathered.reshape(step_count * slot_count, gathered.shape[2])
    targets = (
        assign_block.reshape(step_count, row_devices, col_devices, capacity)
        .transpose(0, 2, 1, 3)
        .reshape(step_count, slot_count)
    )
    holdings = counts_block.reshape(step_count, row_devices, col_devices).transpose(0, 2, 1)
    slot_grid = lax.broadcasted_iota(jnp.int32, (step_count, col_devices, row_devices, capacity), 3)
    live_mask = (slot_grid < holdings[..., None]).reshape(step_count, slot_count)
    targets = jnp.where(live_mask, targets, rows_step)
    slot_ids = lax.broadcasted_iota(jnp.int32, (step_count, slot_count), 1)
    step_ids = lax.broadcasted_iota(jnp.int32, (step_count, slot_count), 0)
    inverse = (
        jnp.zeros((step_count, rows_step), jnp.int32)
        .at[step_ids, targets]
        .set(slot_ids, mode="drop")
    )
    grid_shape = (col_devices, row_devices, step_count, MEAN)
    col_ids = lax.broadcasted_iota(jnp.int32, grid_shape, 0)
    row_ids = lax.broadcasted_iota(jnp.int32, grid_shape, 1)
    step_grid = lax.broadcasted_iota(jnp.int32, grid_shape, 2)
    member = lax.broadcasted_iota(jnp.int32, grid_shape, 3)
    row_numbers = (row_ids * col_devices + col_ids) * MEAN + member
    positions = (step_grid * slot_count + inverse[step_grid, row_numbers]).reshape(-1)
    inputs = jnp.take(stacked, positions, axis=0)
    rows_here = inputs
    gate_up = lax.psum_scatter(
        jnp.dot(rows_here, paired, preferred_element_type=jnp.float32).astype(jnp.bfloat16),
        "row",
        scatter_dimension=0,
        tiled=True,
    ).astype(jnp.float32)
    hidden = (jax.nn.silu(gate_up[:, :hidden_cols]) * gate_up[:, hidden_cols:]).astype(jnp.bfloat16)
    hidden_all = lax.all_gather(hidden, "row", axis=0, tiled=True)
    rows_here = hidden_all
    summed = lax.psum_scatter(
        jnp.dot(rows_here, down_w, preferred_element_type=jnp.float32).astype(jnp.bfloat16),
        "col",
        scatter_dimension=0,
        tiled=True,
    )
    finished = lax.all_to_all(summed, "row", split_axis=0, concat_axis=1, tiled=True)
    return finished.reshape(step_count, MEAN, finished.shape[1])


def any_plan(sender_rows, counts, assign, gate_w, up_w, down_w):
    values = sender_rows.astype(jnp.float32)
    normed = (
        values * lax.rsqrt(jnp.mean(values * values, axis=-1, keepdims=True) + epsilon)
    ).astype(jnp.bfloat16)
    paired = jnp.concatenate((gate_w, up_w), axis=1)
    hidden_cols = gate_w.shape[1]
    outputs = []
    for step_index in range(STEPS):
        outputs.append(
            layer_block(
                normed[step_index : step_index + 1],
                counts[step_index : step_index + 1],
                assign[step_index : step_index + 1],
                paired,
                down_w,
                hidden_cols,
            )
        )
    result = jnp.concatenate(outputs, axis=0)
    return result


def solution(mesh):
    near = mesh.shape["row"] == 4 and mesh.shape["col"] == 4
    return jax.shard_map(
        near_plan if near else any_plan,
        mesh=mesh,
        in_specs=(
            P(None, ("groups", "row", "col"), None),
            P(None, "groups"),
            P(None, "groups"),
            P("row", "col"),
            P("row", "col"),
            P("col", "row"),
        ),
        out_specs=P(None, ("groups", "row", "col"), None),
        check_vma=False,
    )
```

```python
import functools

import jax
import jax.numpy as jnp
from jax import lax
from jax.experimental import pallas as pl
from jax.experimental.pallas import tpu as pltpu
from jax.sharding import PartitionSpec as P

STEPS = 2
MEAN = 4

epsilon = 1e-05

BF = jnp.bfloat16
F32 = jnp.float32
MIB = 2**20
PIECES = 2
X1 = ((0, 1), (1, 0), (2, 3), (3, 2))
X2 = ((0, 2), (1, 3), (2, 0), (3, 1))
X3 = ((0, 3), (1, 2), (2, 1), (3, 0))


def place():
    row = lax.axis_index("row")
    return row // 2, lax.rem(row, 2), lax.axis_index("col")


def run(body, outs, operands, token, weights=(), scratch=()):
    count, held = len(operands), len(weights)
    vmem = pl.BlockSpec(memory_space=pltpu.VMEM)
    outs = tuple(outs) + (like((8, 128), F32),)

    def wrapped(*refs):
        results = refs[count + held + 1 :]
        body(refs[:count], refs[count : count + held], results[: len(outs) - 1], results[len(outs) :])
        results[len(outs) - 1][...] = jnp.zeros((8, 128), F32)

    return pl.pallas_call(
        wrapped,
        out_shape=outs,
        in_specs=[vmem] * count
        + [pl.BlockSpec(memory_space=pltpu.HBM)] * held
        + [pl.BlockSpec(memory_space=pl.ANY)],
        out_specs=(vmem,) * len(outs),
        scratch_shapes=scratch,
        compiler_params=pltpu.CompilerParams(vmem_limit_bytes=8 * MIB),
        cost_estimate=pl.CostEstimate(flops=0, bytes_accessed=1, transcendentals=0),
    )(*operands, *(pltpu.with_memory_space_constraint(w, pltpu.HBM) for w in weights), token)


def like(shape, dtype=BF):
    return jax.ShapeDtypeStruct(shape, dtype)


def norm_body(ins, _, outs, __):
    (rows_ref,) = ins
    core_ref, sides = outs[0], outs[1:]
    y, c, _ = place()
    width = core_ref.shape[2]
    for step in range(rows_ref.shape[0]):
        total = jnp.sum(jnp.square(rows_ref[step].astype(F32)), axis=-1, keepdims=True)
        scale = lax.rsqrt(total / rows_ref.shape[2] + epsilon)
        y_ref, yd_ref, own_ref = sides[step * 3 : step * 3 + 3]
        for dy, dc, out in ((1, 0, y_ref), (1, 1, yd_ref), (0, 1, core_ref.at[step]), (0, 0, own_ref)):
            block = lax.bitwise_xor(y, dy) * 2 + lax.bitwise_xor(c, dc)
            at = pl.ds(pl.multiple_of(block * width, width), width)
            out[...] = (rows_ref[step, :, at].astype(F32) * scale).astype(BF)


def normed_blocks(sender_rows, token):
    steps, slots, width = sender_rows.shape
    core = like((steps, slots, width // 4))
    side = like((slots, width // 4))
    return run(norm_body, (core,) + (side,) * 6, (sender_rows,), token)


def pick_body(ins, _, outs, __):
    counts_ref, assign_ref = ins
    y, c, z = place()
    rows = outs[0].shape[0]
    slots = assign_ref.shape[1]
    spread = (
        lax.broadcasted_iota(jnp.int32, (slots // 8, slots), 1) // 8
        == lax.broadcasted_iota(jnp.int32, (slots // 8, slots), 0)
    ).astype(F32)
    held = jnp.dot(counts_ref[...].astype(F32), spread, preferred_element_type=F32)
    slot = lax.rem(lax.broadcasted_iota(jnp.int32, (1, slots), 1), 8).astype(F32)
    at = lax.broadcasted_iota(jnp.int32, (rows, slots), 0)
    target = (lax.rem(at, 16) // 4) * 16 + lax.bitwise_xor(at // 16, z) * 4 + lax.rem(at, 4)
    p = lax.broadcasted_iota(jnp.int32, (slots, slots), 1)
    bit = lambda shift: lax.rem(lax.shift_right_logical(p, shift), 2)
    row = lax.bitwise_xor(bit(4), y) * 2 + lax.bitwise_xor(bit(3), c)
    sender = row * 4 + lax.bitwise_xor(lax.shift_right_logical(p, 5), z)
    source = sender * 8 + lax.rem(p, 8)
    moved = (lax.broadcasted_iota(jnp.int32, (slots, slots), 0) == source).astype(F32).astype(BF)
    for step, out in enumerate(outs):
        live = slot < held[step : step + 1]
        chosen = jnp.where(live, assign_ref[step : step + 1, :], -1)
        placed = (chosen == target).astype(F32).astype(BF)
        out[...] = jnp.dot(placed, moved, preferred_element_type=F32).astype(BF)


def pick_matrices(counts, assign, token):
    one = like((MEAN * counts.shape[1], assign.shape[1]))
    return run(pick_body, (one, one), (counts, assign), token)


def chunk_shape(chunk, gate_w, down_w):
    if chunk[0] == "down":
        return (down_w.shape[0] // 4, down_w.shape[1])
    return (gate_w.shape[0] // 2, gate_w.shape[1] // 2)


def chunk_copies(chunk, weights, out_ref, sems):
    y, c, _ = place()
    kind, dy, dc, half = chunk
    quarter = lax.bitwise_xor(c, dc) * 2 + lax.bitwise_xor(y, dy)
    if kind == "down":
        height = out_ref.shape[0]
        at = pl.ds(pl.multiple_of(quarter * height, 16), height)
        return [pltpu.make_async_copy(weights[0].at[at, :], out_ref, sems.at[0])]
    height, width = out_ref.shape[0], out_ref.shape[1] // 2
    at = pl.ds(pl.multiple_of(quarter * width, 128), width)
    return [
        pltpu.make_async_copy(
            w.at[pl.ds(half * height, height), at],
            out_ref.at[:, pl.ds(i * width, width)],
            sems.at[i],
        )
        for i, w in enumerate(weights)
    ]


def with_chunk(chunk, body):
    def wrapped(ins, weights, outs, scratch):
        copies = chunk_copies(chunk, weights, outs[-1], scratch[-1])
        for copy in copies:
            copy.start()
        body(ins, weights, outs[:-1], scratch[:-1])
        for copy in copies:
            copy.wait()

    return wrapped


def meet(token):
    return lax.ppermute(token, "row", X1)


def run_with(chunk, model, body, outs, operands, token, scratch=()):
    if chunk is None:
        return run(body, outs, operands, token, (), scratch)
    gate_w, up_w, down_w = model
    weights = (down_w,) if chunk[0] == "down" else (gate_w, up_w)
    return run(
        with_chunk(chunk, body),
        tuple(outs) + (pltpu.VMEM(chunk_shape(chunk, gate_w, down_w), BF),),
        operands,
        token,
        weights,
        tuple(scratch) + (pltpu.SemaphoreType.DMA((2,)),),
    )


def fetch_body(_, __, ___, ____):
    pass


def stack_step_body(step, ins, _, outs, __):
    own_ref, core_ref, y_ref, yd_ref = ins
    slots = own_ref.shape[0]
    pairs = ((own_ref[...], core_ref[step]), (y_ref[...], yd_ref[...]))
    for i, pair in enumerate(pairs):
        joined = jnp.concatenate([x.astype(F32) for x in pair], axis=0).astype(BF)
        outs[0][2 * i * slots : 2 * (i + 1) * slots, :] = joined


def after_body(ins, _, outs, __):
    outs[0][...] = ins[0][...]


def halves_dot(x_ref, w_refs):
    height = w_refs[0].shape[0]
    total = jnp.dot(x_ref[:, :height], w_refs[0][...], preferred_element_type=F32)
    return total + jnp.dot(x_ref[:, height:], w_refs[1][...], preferred_element_type=F32)


def store_rows(outs, value):
    rows = outs[0].shape[0]
    for i, out in enumerate(outs):
        out[...] = value[i * rows : (i + 1) * rows].astype(out.dtype)


def load_rows(refs):
    return jnp.concatenate([ref[...].astype(F32) for ref in refs], axis=0)


def first_body(ins, _, outs, scratch):
    pieces, pick_ref, w_refs = ins[:4], ins[4], ins[5:]
    batch_ref, pieces_out = outs[0], outs[1:]
    slots = scratch[0]
    height = pieces[0].shape[0]
    for i, piece in enumerate(pieces):
        slots[i * height : (i + 1) * height, :] = piece[...]
    batch_ref[...] = jnp.dot(pick_ref[...], slots[...], preferred_element_type=F32).astype(BF)
    store_rows(pieces_out, halves_dot(batch_ref, w_refs))


def dot_body(ins, _, outs, __):
    store_rows(outs, halves_dot(ins[0], ins[1:]))


def far_body(ins, _, outs, __):
    outs[0][...] = (ins[0][...] + load_rows(ins[1:])).astype(BF)


def hidden_body(ins, _, outs, __):
    width = outs[0].shape[1]
    total = ins[0][...] + ins[1][...].astype(F32) + load_rows(ins[2:])
    gate, up = total[:, :width], total[:, width:]
    outs[0][...] = (gate / (1.0 + jnp.exp(-gate)) * up).astype(BF)


def down_part_body(ins, _, outs, __):
    own_ref, core_ref, own_w, core_w = ins
    total = jnp.dot(own_ref[...], own_w[...], preferred_element_type=F32)
    outs[0][...] = total + jnp.dot(core_ref[...], core_w[...], preferred_element_type=F32)


def down_rest_body(ins, _, outs, __):
    y_ref, yd_ref, y_w, yd_w, part_ref = ins
    rows = outs[0].shape[0]
    total = part_ref[...] + jnp.dot(y_ref[...], y_w[...], preferred_element_type=F32)
    total = total + jnp.dot(yd_ref[...], yd_w[...], preferred_element_type=F32)
    for i, out in enumerate(outs):
        out[...] = total[i * rows : (i + 1) * rows].astype(out.dtype)


def owner_body(ins, _, outs, __):
    y, c, _ = place()
    at = lax.broadcasted_iota(jnp.int32, (16, 16), 0)
    source = lax.bitwise_xor(at, (y * 2 + c) * 4)
    turn = (lax.broadcasted_iota(jnp.int32, (16, 16), 1) == source).astype(F32).astype(BF)
    for step in range(2):
        total = ins[step * 4][...]
        for got in ins[step * 4 + 1 : step * 4 + 4]:
            total = total + got[...].astype(F32)
        turned = jnp.dot(turn, total.astype(BF), preferred_element_type=F32)
        for i, out in enumerate(outs):
            out[step] = turned[i * 4 : (i + 1) * 4].astype(BF)


def output_body(ins, _, outs, __):
    y, c, _ = place()
    width = ins[0].shape[2]
    for dy, dc, block in ((0, 0, ins[0]), (0, 1, ins[1]), (1, 0, ins[2]), (1, 1, ins[3])):
        source = lax.bitwise_xor(y, dy) * 2 + lax.bitwise_xor(c, dc)
        outs[0][:, :, pl.ds(pl.multiple_of(source * width, width), width)] = block[...]


def near_plan(sender_rows, counts, assign, gate_w, up_w, down_w):
    steps, slots, width = sender_rows.shape
    model = (gate_w, up_w, down_w)
    width //= 4
    units = gate_w.shape[1] // 4
    rows = MEAN * counts.shape[1]
    part = rows // 4
    held = {}

    def bring(chunk, token):
        held[chunk], token = run_with(chunk, model, fetch_body, (), (), token)
        return token

    def quarter(dy, dc):
        return held["gu", dy, dc, 0], held["gu", dy, dc, 1]

    def carry(chunk, body, outs, operands, token, scratch=()):
        results = run_with(chunk, model, body, outs, operands, token, scratch)
        if chunk is not None:
            held[chunk] = results[-2]
        return results[: len(outs)] + (results[-1],)

    core, y0, yd0, own0, y1, yd1, own1, token = normed_blocks(sender_rows, counts)
    sides = []
    for own, y, yd in ((own0, y0, yd0), (own1, y1, yd1)):
        sides.append((own, lax.ppermute(y, "row", X2), lax.ppermute(yd, "row", X3)))
    core_got = lax.ppermute(core, "row", X1)
    *picks, token = pick_matrices(counts, assign, token)
    token = bring(("gu", 1, 1, 0), token)

    blocks, far, near, onward = [], [], [], []
    for step, (own, y, yd) in enumerate(sides):
        block, token = run(
            functools.partial(stack_step_body, step),
            (like((4 * slots, width)),),
            (own, core_got, y, yd),
            token,
        )
        blocks.append(block)
        far.append(lax.ppermute(block, "col", X3))
        near.append(lax.ppermute(block, "col", X1))
    token = bring(("gu", 1, 1, 1), meet(token))
    for step in range(steps):
        passed, token = run(after_body, (like(far[step].shape),), (far[step],), token)
        onward.append(lax.ppermute(passed, "col", X1))
        token = meet(token)
        if step == 0:
            token = bring(("gu", 1, 0, 0), token)
            token = bring(("gu", 1, 0, 1), token)

    carried = (
        (("gu", 0, 1, 0), ("gu", 0, 1, 1), ("gu", 0, 0, 0), ("down", 0, 0, 0)),
        (("down", 0, 1, 0), ("down", 1, 0, 0), ("down", 1, 1, 0), None),
    )
    gots, nears, near_cores, hidden, sums = [], [], [], [], []
    both = like((rows, 2 * units))
    bits = (like((rows // PIECES, 2 * units)),) * PIECES
    both_wide = like((rows, 2 * units), F32)

    def activate(step, token):
        result, token = run(
            hidden_body, (like((rows, units)),), (nears[step], gots[step]) + near_cores[step], token
        )
        y = lax.ppermute(result, "row", X2)
        hidden.append((result, lax.ppermute(result, "row", X1), y))
        return token

    for step in range(steps):
        first, second, third, fourth = carried[step]
        pieces = (blocks[step], near[step], onward[step], far[step])
        batch, *out, token = carry(
            first,
            first_body,
            (like((rows, width)),) + bits,
            pieces + (picks[step],) + quarter(1, 1),
            token,
            (pltpu.VMEM((16 * slots, width), BF),),
        )
        core = tuple(lax.ppermute(o, "row", X1) for o in out)
        own, token = carry(second, dot_body, (both_wide,), (batch,) + quarter(1, 0), token)
        send, token = run(far_body, (both,), (own,) + core, token)
        gots.append(lax.ppermute(send, "row", X2))
        *out, token = carry(third, dot_body, bits, (batch,) + quarter(0, 1), meet(token))
        near_cores.append(tuple(lax.ppermute(o, "row", X1) for o in out))
        if step == 0:
            token = bring(("gu", 0, 0, 1), token)
        own, token = carry(fourth, dot_body, (both_wide,), (batch,) + quarter(0, 0), token)
        nears.append(own)

    def down_part(step, token):
        weights = (held["down", 0, 0, 0], held["down", 0, 1, 0])
        return run(
            down_part_body, (like((rows, width), F32),), hidden[step][:2] + weights, token
        )

    def down_rest(step, part_sum, yd, token):
        weights = (held["down", 1, 0, 0], held["down", 1, 1, 0])
        outs = (like((part, width), F32),) + (like((part, width)),) * 3
        operands = (hidden[step][2], yd) + weights + (part_sum,)
        keep, send1, send2, send3, token = run(down_rest_body, outs, operands, token)
        got = [lax.ppermute(s, "col", x) for s, x in ((send3, X3), (send2, X2), (send1, X1))]
        sums.extend([keep] + got)
        return token

    token = activate(0, token)
    part0, token = down_part(0, token)
    token = activate(1, token)
    passed, token = run(after_body, (like(hidden[0][2].shape),), (hidden[0][2],), token)
    token = down_rest(0, part0, lax.ppermute(passed, "row", X1), token)
    part1, token = down_part(1, meet(token))
    passed, token = run(after_body, (like(hidden[1][2].shape),), (hidden[1][2],), token)
    token = down_rest(1, part1, lax.ppermute(passed, "row", X1), token)
    own, core, y, yd, token = run(owner_body, (like((steps, MEAN, width)),) * 4, tuple(sums), token)
    blocks = (own, lax.ppermute(core, "row", X1), lax.ppermute(y, "row", X2), lax.ppermute(yd, "row", X3))
    result, _ = run(output_body, (like((steps, MEAN, 4 * width)),), blocks, token)
    return result


def layer_block(normed_block, counts_block, assign_block, paired, down_w, hidden_cols):
    row_devices = lax.axis_size("row")
    col_devices = lax.axis_size("col")
    step_count = normed_block.shape[0]
    capacity = normed_block.shape[1]
    rows_step = MEAN * counts_block.shape[1]
    spread = lax.all_to_all(normed_block, "row", split_axis=2, concat_axis=1, tiled=True)
    gathered = lax.all_gather(spread, "col", axis=1, tiled=True)
    slot_count = gathered.shape[1]
    stacked = gathered.reshape(step_count * slot_count, gathered.shape[2])
    targets = (
        assign_block.reshape(step_count, row_devices, col_devices, capacity)
        .transpose(0, 2, 1, 3)
        .reshape(step_count, slot_count)
    )
    holdings = counts_block.reshape(step_count, row_devices, col_devices).transpose(0, 2, 1)
    slot_grid = lax.broadcasted_iota(jnp.int32, (step_count, col_devices, row_devices, capacity), 3)
    live_mask = (slot_grid < holdings[..., None]).reshape(step_count, slot_count)
    targets = jnp.where(live_mask, targets, rows_step)
    slot_ids = lax.broadcasted_iota(jnp.int32, (step_count, slot_count), 1)
    step_ids = lax.broadcasted_iota(jnp.int32, (step_count, slot_count), 0)
    inverse = (
        jnp.zeros((step_count, rows_step), jnp.int32)
        .at[step_ids, targets]
        .set(slot_ids, mode="drop")
    )
    grid_shape = (col_devices, row_devices, step_count, MEAN)
    col_ids = lax.broadcasted_iota(jnp.int32, grid_shape, 0)
    row_ids = lax.broadcasted_iota(jnp.int32, grid_shape, 1)
    step_grid = lax.broadcasted_iota(jnp.int32, grid_shape, 2)
    member = lax.broadcasted_iota(jnp.int32, grid_shape, 3)
    row_numbers = (row_ids * col_devices + col_ids) * MEAN + member
    positions = (step_grid * slot_count + inverse[step_grid, row_numbers]).reshape(-1)
    inputs = jnp.take(stacked, positions, axis=0)
    rows_here = inputs
    gate_up = lax.psum_scatter(
        jnp.dot(rows_here, paired, preferred_element_type=jnp.float32).astype(jnp.bfloat16),
        "row",
        scatter_dimension=0,
        tiled=True,
    ).astype(jnp.float32)
    hidden = (jax.nn.silu(gate_up[:, :hidden_cols]) * gate_up[:, hidden_cols:]).astype(jnp.bfloat16)
    hidden_all = lax.all_gather(hidden, "row", axis=0, tiled=True)
    rows_here = hidden_all
    summed = lax.psum_scatter(
        jnp.dot(rows_here, down_w, preferred_element_type=jnp.float32).astype(jnp.bfloat16),
        "col",
        scatter_dimension=0,
        tiled=True,
    )
    finished = lax.all_to_all(summed, "row", split_axis=0, concat_axis=1, tiled=True)
    return finished.reshape(step_count, MEAN, finished.shape[1])


def any_plan(sender_rows, counts, assign, gate_w, up_w, down_w):
    values = sender_rows.astype(jnp.float32)
    normed = (
        values * lax.rsqrt(jnp.mean(values * values, axis=-1, keepdims=True) + epsilon)
    ).astype(jnp.bfloat16)
    paired = jnp.concatenate((gate_w, up_w), axis=1)
    hidden_cols = gate_w.shape[1]
    outputs = []
    for step_index in range(STEPS):
        outputs.append(
            layer_block(
                normed[step_index : step_index + 1],
                counts[step_index : step_index + 1],
                assign[step_index : step_index + 1],
                paired,
                down_w,
                hidden_cols,
            )
        )
    result = jnp.concatenate(outputs, axis=0)
    return result


def solution(mesh):
    near = mesh.shape["row"] == 4 and mesh.shape["col"] == 4
    return jax.shard_map(
        near_plan if near else any_plan,
        mesh=mesh,
        in_specs=(
            P(None, ("groups", "row", "col"), None),
            P(None, "groups"),
            P(None, "groups"),
            P("row", "col"),
            P("row", "col"),
            P("col", "row"),
        ),
        out_specs=P(None, ("groups", "row", "col"), None),
        check_vma=False,
    )
```

```python
import functools

import jax
import jax.numpy as jnp
from jax import lax
from jax.experimental import pallas as pl
from jax.experimental.pallas import tpu as pltpu
from jax.sharding import PartitionSpec as P

STEPS = 2
MEAN = 4

epsilon = 1e-05

BF = jnp.bfloat16
F32 = jnp.float32
MIB = 2**20
PIECES = 2
X1 = ((0, 1), (1, 0), (2, 3), (3, 2))
X2 = ((0, 2), (1, 3), (2, 0), (3, 1))
X3 = ((0, 3), (1, 2), (2, 1), (3, 0))


def place():
    row = lax.axis_index("row")
    return row // 2, lax.rem(row, 2), lax.axis_index("col")


def run(body, outs, operands, token, weights=(), scratch=(), cost=1, spec=None):
    count, held = len(operands), len(weights)
    skip = count + held + (token is not None)
    vmem = pl.BlockSpec(memory_space=pltpu.VMEM)
    outs = tuple(outs) + (like((8, 128), F32),)

    def wrapped(*refs):
        results = refs[skip:]
        body(refs[:count], refs[count : count + held], results[: len(outs) - 1], results[len(outs) :])
        results[len(outs) - 1][...] = jnp.zeros((8, 128), F32)

    return pl.pallas_call(
        wrapped,
        out_shape=outs,
        in_specs=[spec or vmem] * count
        + [pl.BlockSpec(memory_space=pltpu.HBM)] * held
        + [pl.BlockSpec(memory_space=pl.ANY)] * (token is not None),
        out_specs=(vmem,) * len(outs),
        scratch_shapes=scratch,
        compiler_params=pltpu.CompilerParams(vmem_limit_bytes=8 * MIB),
        cost_estimate=pl.CostEstimate(flops=0, bytes_accessed=cost, transcendentals=0),
    )(*operands, *(pltpu.with_memory_space_constraint(w, pltpu.HBM) for w in weights), *(() if token is None else (token,)))


def like(shape, dtype=BF):
    return jax.ShapeDtypeStruct(shape, dtype)


def norm_body(ins, _, outs, __):
    (rows_ref,) = ins
    y, c, _ = place()
    width = outs[0].shape[2]
    for step in range(rows_ref.shape[0]):
        total = jnp.sum(jnp.square(rows_ref[step].astype(F32)), axis=-1, keepdims=True)
        scale = lax.rsqrt(total / rows_ref.shape[2] + epsilon)
        for out, (dy, dc) in zip(outs, ((1, 0), (1, 1), (0, 1), (0, 0))):
            block = lax.bitwise_xor(y, dy) * 2 + lax.bitwise_xor(c, dc)
            at = pl.ds(pl.multiple_of(block * width, width), width)
            out[step] = (rows_ref[step, :, at].astype(F32) * scale).astype(BF)


def normed_blocks(sender_rows):
    steps, slots, width = sender_rows.shape
    return run(norm_body, (like((steps, slots, width // 4)),) * 4, (sender_rows,), None)


def pick_body(ins, _, outs, __):
    counts_ref, assign_ref = ins
    (pick_ref,) = outs
    y, c, z = place()
    rows = pick_ref.shape[0] // 2
    slots = assign_ref.shape[1]
    arrivals = pick_ref.shape[1]
    spread = (
        lax.broadcasted_iota(jnp.int32, (slots // 8, slots), 1) // 8
        == lax.broadcasted_iota(jnp.int32, (slots // 8, slots), 0)
    ).astype(F32)
    held = jnp.dot(counts_ref[...].astype(F32), spread, preferred_element_type=F32)
    slot = lax.rem(lax.broadcasted_iota(jnp.int32, (1, slots), 1), 8).astype(F32)
    at = lax.broadcasted_iota(jnp.int32, (rows, slots), 0)
    target = (lax.rem(at, 16) // 4) * 16 + lax.bitwise_xor(at // 16, z) * 4 + lax.rem(at, 4)
    p = lax.broadcasted_iota(jnp.int32, (slots, arrivals), 1)
    bit = lambda shift: lax.rem(lax.shift_right_logical(p, shift), 2)
    row = lax.bitwise_xor(bit(5), y) * 2 + lax.bitwise_xor(bit(4), c)
    sender = row * 4 + lax.bitwise_xor(lax.shift_right_logical(p, 6), z)
    source = sender * 8 + lax.rem(p, 8)
    entry = lax.broadcasted_iota(jnp.int32, (slots, arrivals), 0)
    for step in range(2):
        live = slot < held[step : step + 1]
        chosen = jnp.where(live, assign_ref[step : step + 1, :], -1)
        placed = (chosen == target).astype(F32).astype(BF)
        moved = ((entry == source) & (bit(3) == step)).astype(F32).astype(BF)
        pick_ref[step * rows : (step + 1) * rows, :] = jnp.dot(
            placed, moved, preferred_element_type=F32
        ).astype(BF)


def quarter_body(dy, dc, half, ins, weights, outs, scratch):
    y, c, _ = place()
    (out_ref,) = outs
    height, width = out_ref.shape[0], out_ref.shape[1] // 2
    start = (lax.bitwise_xor(c, dc) * 2 + lax.bitwise_xor(y, dy)) * width
    at = pl.ds(pl.multiple_of(start, 128), width)
    copies = [
        pltpu.make_async_copy(
            w.at[pl.ds(half * height, height), at],
            out_ref.at[:, pl.ds(i * width, width)],
            scratch[0].at[i],
        )
        for i, w in enumerate(weights)
    ]
    for copy in copies:
        copy.start()
    for copy in copies:
        copy.wait()


def fetch_quarter(gate_w, up_w, dy, dc, half, parts, token):
    shape = pltpu.VMEM((gate_w.shape[0] // parts, gate_w.shape[1] // 2), BF)
    return run(
        functools.partial(quarter_body, dy, dc, half),
        (shape,),
        (),
        token,
        (gate_w, up_w),
        (pltpu.SemaphoreType.DMA((2,)),),
    )


def down_rows_body(dy, ins, _, outs, scratch):
    y, c, _ = place()
    (out_ref,) = outs
    height = out_ref.shape[0] // 2
    copies = []
    for dc in range(2):
        start = (lax.bitwise_xor(c, dc) * 2 + lax.bitwise_xor(y, dy)) * height
        copies.append(
            pltpu.make_async_copy(
                ins[0].at[pl.ds(pl.multiple_of(start, 16), height), :],
                out_ref.at[pl.ds(dc * height, height), :],
                scratch[0].at[dc],
            )
        )
    for copy in copies:
        copy.start()
    for copy in copies:
        copy.wait()


def meet(token):
    return lax.ppermute(token, "row", X1)


def stack_body(ins, _, outs, __):
    for i, piece in enumerate(ins):
        joined = jnp.concatenate([piece[step].astype(F32) for step in range(2)], axis=0)
        outs[0][i * 16 : (i + 1) * 16, :] = joined.astype(BF)


def after_body(ins, _, outs, __):
    outs[0][...] = ins[0][...]


def halves_dot(x_ref, w_refs):
    total = 0.0
    height = w_refs[0].shape[0]
    for i, w_ref in enumerate(w_refs):
        at = slice(i * height, (i + 1) * height)
        total = total + jnp.dot(x_ref[:, at], w_ref[...], preferred_element_type=F32)
    return total


def store_rows(outs, value):
    rows = outs[0].shape[0]
    for i, out in enumerate(outs):
        out[...] = value[i * rows : (i + 1) * rows].astype(out.dtype)


def load_rows(refs):
    return jnp.concatenate([ref[...].astype(F32) for ref in refs], axis=0)


def first_body(ins, _, outs, scratch):
    pieces, pick_ref, w_refs = ins[:8], ins[8], ins[9:]
    batch_ref, pieces_out = outs[0], outs[1:]
    slots = scratch[0]
    height = pieces[0].shape[0]
    for i, piece in enumerate(pieces):
        slots[i * height : (i + 1) * height, :] = piece[...]
    batch_ref[...] = jnp.dot(pick_ref[...], slots[...], preferred_element_type=F32).astype(BF)
    store_rows(pieces_out, halves_dot(batch_ref, w_refs))


def dot_body(ins, _, outs, __):
    store_rows(outs, halves_dot(ins[0], ins[1:]))


def far_body(ins, _, outs, __):
    store_rows(outs, ins[0][...] + load_rows(ins[1:]))


def hidden_body(step, ins, _, outs, __):
    rows, width = outs[0].shape
    total = ins[0][step * rows : (step + 1) * rows, :] + ins[1][...].astype(F32) + load_rows(ins[2:])
    gate, up = total[:, :width], total[:, width:]
    outs[0][...] = (gate / (1.0 + jnp.exp(-gate)) * up).astype(BF)


def down_part_body(ins, _, outs, __):
    own_ref, core_ref, w_ref = ins
    height = w_ref.shape[0] // 2
    total = jnp.dot(own_ref[...], w_ref[:height, :], preferred_element_type=F32)
    outs[0][...] = total + jnp.dot(core_ref[...], w_ref[height:, :], preferred_element_type=F32)


def down_rest_body(ins, _, outs, __):
    y_ref, yd_ref, w_ref, part_ref = ins
    rows = outs[0].shape[0]
    height = w_ref.shape[0] // 2
    total = part_ref[...] + jnp.dot(y_ref[...], w_ref[:height, :], preferred_element_type=F32)
    total = total + jnp.dot(yd_ref[...], w_ref[height:, :], preferred_element_type=F32)
    for i, out in enumerate(outs):
        out[...] = total[i * rows : (i + 1) * rows].astype(out.dtype)


def owner_body(ins, _, outs, __):
    y, c, _ = place()
    at = lax.broadcasted_iota(jnp.int32, (16, 16), 0)
    source = lax.bitwise_xor(at, (y * 2 + c) * 4)
    turn = (lax.broadcasted_iota(jnp.int32, (16, 16), 1) == source).astype(F32).astype(BF)
    for step in range(2):
        total = ins[step * 4][...]
        for got in ins[step * 4 + 1 : step * 4 + 4]:
            total = total + got[...].astype(F32)
        turned = jnp.dot(turn, total.astype(BF), preferred_element_type=F32)
        for i, out in enumerate(outs):
            out[step] = turned[i * 4 : (i + 1) * 4].astype(BF)


def output_body(ins, _, outs, __):
    y, c, _ = place()
    width = ins[0].shape[2]
    for dy, dc, block in ((0, 0, ins[0]), (0, 1, ins[1]), (1, 0, ins[2]), (1, 1, ins[3])):
        source = lax.bitwise_xor(y, dy) * 2 + lax.bitwise_xor(c, dc)
        outs[0][:, :, pl.ds(pl.multiple_of(source * width, width), width)] = block[...]


def near_plan(sender_rows, counts, assign, gate_w, up_w, down_w):
    steps, slots, width = sender_rows.shape
    width //= 4
    units = gate_w.shape[1] // 4
    rows = MEAN * counts.shape[1]
    part = rows // 4

    def down_rows(dy, token):
        shape = pltpu.VMEM((down_w.shape[0] // 2, down_w.shape[1]), BF)
        scratch = (pltpu.SemaphoreType.DMA((2,)),)
        spec = pl.BlockSpec(memory_space=pl.ANY)
        return run(functools.partial(down_rows_body, dy), (shape,), (down_w,), token, (), scratch, spec=spec)

    y, yd, core, own, token = normed_blocks(sender_rows)
    y, yd = lax.ppermute(y, "row", X2), lax.ppermute(yd, "row", X3)
    core = lax.ppermute(core, "row", X1)
    pick, token = run(pick_body, (like((steps * rows, steps * assign.shape[1])),), (counts, assign), token)
    quarters = {}

    def bring(dy, dc, half, parts, token):
        w, token = fetch_quarter(gate_w, up_w, dy, dc, half, parts, token)
        quarters.setdefault((dy, dc), []).append(w)
        return token

    block = like((4 * slots, width))
    near_block, token = run(stack_body, (block,), (own, core), token)
    near_sent = [lax.ppermute(near_block, "col", X3), lax.ppermute(near_block, "col", X1)]
    token = meet(token)
    token = bring(1, 1, 0, 2, token)
    far_block, token = run(stack_body, (block,), (y, yd), token)
    far_sent = [lax.ppermute(far_block, "col", X3), lax.ppermute(far_block, "col", X1)]
    token = meet(token)
    token = bring(1, 1, 1, 2, token)
    passed, token = run(after_body, (block,), (near_sent[0],), token)
    near_sent.append(lax.ppermute(passed, "col", X1))
    token = meet(token)
    token = bring(1, 0, 0, 2, token)
    passed, token = run(after_body, (block,), (far_sent[0],), token)
    far_sent.append(lax.ppermute(passed, "col", X1))
    token = meet(token)
    token = bring(1, 0, 1, 2, token)
    token = bring(0, 1, 0, 1, token)
    pieces = []
    for dz in range(4):
        for own_block, sent in ((near_block, near_sent), (far_block, far_sent)):
            pieces.append((own_block, sent[1], sent[2], sent[0])[dz])

    bits = (like((steps * rows // PIECES, 2 * units)),) * PIECES
    wide = like((steps * rows, 2 * units), F32)
    batch, *out, token = run(
        first_body,
        (like((steps * rows, width)),) + bits,
        tuple(pieces) + (pick, *quarters[1, 1]),
        token,
        (),
        (pltpu.VMEM((32 * slots, width), BF),),
    )
    cores = tuple(lax.ppermute(o, "row", X1) for o in out)
    own_far, token = run(dot_body, (wide,), (batch, *quarters[1, 0]), token)
    *sends, token = run(far_body, (like((rows, 2 * units)),) * steps, (own_far,) + cores, token)
    gots = [lax.ppermute(send, "row", X2) for send in sends]
    token = meet(token)
    *out, token = run(dot_body, bits, (batch, *quarters[0, 1]), token)
    cores = tuple(lax.ppermute(o, "row", X1) for o in out)
    token = bring(0, 0, 0, 1, token)
    own_near, token = run(dot_body, (wide,), (batch, *quarters[0, 0]), token)
    down_near, token = down_rows(0, token)
    hidden, sums = [], []

    def activate(step, token):
        each = PIECES // steps
        near = cores[step * each : (step + 1) * each]
        operands = (own_near, gots[step]) + near
        body = functools.partial(hidden_body, step)
        result, token = run(body, (like((rows, units)),), operands, token)
        y = lax.ppermute(result, "row", X2)
        hidden.append((result, lax.ppermute(result, "row", X1), y))
        return token

    def down_part(step, token):
        return run(down_part_body, (like((rows, width), F32),), hidden[step][:2] + (down_near,), token)

    def down_rest(step, part_sum, token):
        passed, token = run(after_body, (like((rows, units)),), (hidden[step][2],), token)
        outs = (like((part, width), F32),) + (like((part, width)),) * 3
        operands = (hidden[step][2], lax.ppermute(passed, "row", X1), down_far, part_sum)
        keep, send1, send2, send3, token = run(down_rest_body, outs, operands, token)
        got = [lax.ppermute(s, "col", x) for s, x in ((send3, X3), (send2, X2), (send1, X1))]
        sums.extend([keep] + got)
        return token

    token = activate(0, token)
    down_far, token = down_rows(1, token)
    part0, token = down_part(0, token)
    token = activate(1, token)
    token = down_rest(0, part0, token)
    part1, token = down_part(1, meet(token))
    token = down_rest(1, part1, token)
    own, core, y, yd, token = run(owner_body, (like((steps, MEAN, width)),) * 4, tuple(sums), token)
    blocks = (own, lax.ppermute(core, "row", X1), lax.ppermute(y, "row", X2), lax.ppermute(yd, "row", X3))
    result, _ = run(output_body, (like((steps, MEAN, 4 * width)),), blocks, token)
    return result


def layer_block(normed_block, counts_block, assign_block, paired, down_w, hidden_cols):
    row_devices = lax.axis_size("row")
    col_devices = lax.axis_size("col")
    step_count = normed_block.shape[0]
    capacity = normed_block.shape[1]
    rows_step = MEAN * counts_block.shape[1]
    spread = lax.all_to_all(normed_block, "row", split_axis=2, concat_axis=1, tiled=True)
    gathered = lax.all_gather(spread, "col", axis=1, tiled=True)
    slot_count = gathered.shape[1]
    stacked = gathered.reshape(step_count * slot_count, gathered.shape[2])
    targets = (
        assign_block.reshape(step_count, row_devices, col_devices, capacity)
        .transpose(0, 2, 1, 3)
        .reshape(step_count, slot_count)
    )
    holdings = counts_block.reshape(step_count, row_devices, col_devices).transpose(0, 2, 1)
    slot_grid = lax.broadcasted_iota(jnp.int32, (step_count, col_devices, row_devices, capacity), 3)
    live_mask = (slot_grid < holdings[..., None]).reshape(step_count, slot_count)
    targets = jnp.where(live_mask, targets, rows_step)
    slot_ids = lax.broadcasted_iota(jnp.int32, (step_count, slot_count), 1)
    step_ids = lax.broadcasted_iota(jnp.int32, (step_count, slot_count), 0)
    inverse = (
        jnp.zeros((step_count, rows_step), jnp.int32)
        .at[step_ids, targets]
        .set(slot_ids, mode="drop")
    )
    grid_shape = (col_devices, row_devices, step_count, MEAN)
    col_ids = lax.broadcasted_iota(jnp.int32, grid_shape, 0)
    row_ids = lax.broadcasted_iota(jnp.int32, grid_shape, 1)
    step_grid = lax.broadcasted_iota(jnp.int32, grid_shape, 2)
    member = lax.broadcasted_iota(jnp.int32, grid_shape, 3)
    row_numbers = (row_ids * col_devices + col_ids) * MEAN + member
    positions = (step_grid * slot_count + inverse[step_grid, row_numbers]).reshape(-1)
    inputs = jnp.take(stacked, positions, axis=0)
    rows_here = inputs
    gate_up = lax.psum_scatter(
        jnp.dot(rows_here, paired, preferred_element_type=jnp.float32).astype(jnp.bfloat16),
        "row",
        scatter_dimension=0,
        tiled=True,
    ).astype(jnp.float32)
    hidden = (jax.nn.silu(gate_up[:, :hidden_cols]) * gate_up[:, hidden_cols:]).astype(jnp.bfloat16)
    hidden_all = lax.all_gather(hidden, "row", axis=0, tiled=True)
    rows_here = hidden_all
    summed = lax.psum_scatter(
        jnp.dot(rows_here, down_w, preferred_element_type=jnp.float32).astype(jnp.bfloat16),
        "col",
        scatter_dimension=0,
        tiled=True,
    )
    finished = lax.all_to_all(summed, "row", split_axis=0, concat_axis=1, tiled=True)
    return finished.reshape(step_count, MEAN, finished.shape[1])


def any_plan(sender_rows, counts, assign, gate_w, up_w, down_w):
    values = sender_rows.astype(jnp.float32)
    normed = (
        values * lax.rsqrt(jnp.mean(values * values, axis=-1, keepdims=True) + epsilon)
    ).astype(jnp.bfloat16)
    paired = jnp.concatenate((gate_w, up_w), axis=1)
    hidden_cols = gate_w.shape[1]
    outputs = []
    for step_index in range(STEPS):
        outputs.append(
            layer_block(
                normed[step_index : step_index + 1],
                counts[step_index : step_index + 1],
                assign[step_index : step_index + 1],
                paired,
                down_w,
                hidden_cols,
            )
        )
    result = jnp.concatenate(outputs, axis=0)
    return result


def solution(mesh):
    near = mesh.shape["row"] == 4 and mesh.shape["col"] == 4
    return jax.shard_map(
        near_plan if near else any_plan,
        mesh=mesh,
        in_specs=(
            P(None, ("groups", "row", "col"), None),
            P(None, "groups"),
            P(None, "groups"),
            P("row", "col"),
            P("row", "col"),
            P("col", "row"),
        ),
        out_specs=P(None, ("groups", "row", "col"), None),
        check_vma=False,
    )
```

```python
import functools

import jax
import jax.numpy as jnp
from jax import lax
from jax.experimental import pallas as pl
from jax.experimental.pallas import tpu as pltpu
from jax.sharding import PartitionSpec as P

STEPS = 2
MEAN = 4

epsilon = 1e-05

BF = jnp.bfloat16
F32 = jnp.float32
MIB = 2**20
PIECES = 2
X1 = ((0, 1), (1, 0), (2, 3), (3, 2))
X2 = ((0, 2), (1, 3), (2, 0), (3, 1))
X3 = ((0, 3), (1, 2), (2, 1), (3, 0))


def place():
    row = lax.axis_index("row")
    return row // 2, lax.rem(row, 2), lax.axis_index("col")


def run(body, outs, operands, token, weights=(), scratch=(), cost=1, spec=None):
    count, held = len(operands), len(weights)
    skip = count + held + (token is not None)
    vmem = pl.BlockSpec(memory_space=pltpu.VMEM)
    outs = tuple(outs) + (like((8, 128), F32),)

    def wrapped(*refs):
        results = refs[skip:]
        body(refs[:count], refs[count : count + held], results[: len(outs) - 1], results[len(outs) :])
        results[len(outs) - 1][...] = jnp.zeros((8, 128), F32)

    return pl.pallas_call(
        wrapped,
        out_shape=outs,
        in_specs=[spec or vmem] * count
        + [pl.BlockSpec(memory_space=pltpu.HBM)] * held
        + [pl.BlockSpec(memory_space=pl.ANY)] * (token is not None),
        out_specs=(vmem,) * len(outs),
        scratch_shapes=scratch,
        compiler_params=pltpu.CompilerParams(vmem_limit_bytes=8 * MIB),
        cost_estimate=pl.CostEstimate(flops=0, bytes_accessed=cost, transcendentals=0),
    )(*operands, *(pltpu.with_memory_space_constraint(w, pltpu.HBM) for w in weights), *(() if token is None else (token,)))


def like(shape, dtype=BF):
    return jax.ShapeDtypeStruct(shape, dtype)


def norm_body(ins, _, outs, __):
    (rows_ref,) = ins
    y, c, _ = place()
    width = outs[0].shape[2]
    for step in range(rows_ref.shape[0]):
        total = jnp.sum(jnp.square(rows_ref[step].astype(F32)), axis=-1, keepdims=True)
        scale = lax.rsqrt(total / rows_ref.shape[2] + epsilon)
        for out, (dy, dc) in zip(outs, ((1, 0), (1, 1), (0, 1), (0, 0))):
            block = lax.bitwise_xor(y, dy) * 2 + lax.bitwise_xor(c, dc)
            at = pl.ds(pl.multiple_of(block * width, width), width)
            out[step] = (rows_ref[step, :, at].astype(F32) * scale).astype(BF)


def normed_blocks(sender_rows):
    steps, slots, width = sender_rows.shape
    return run(norm_body, (like((steps, slots, width // 4)),) * 4, (sender_rows,), None)


def pick_body(ins, _, outs, __):
    counts_ref, assign_ref = ins
    (pick_ref,) = outs
    y, c, z = place()
    rows = pick_ref.shape[0] // 2
    slots = assign_ref.shape[1]
    arrivals = pick_ref.shape[1]
    spread = (
        lax.broadcasted_iota(jnp.int32, (slots // 8, slots), 1) // 8
        == lax.broadcasted_iota(jnp.int32, (slots // 8, slots), 0)
    ).astype(F32)
    held = jnp.dot(counts_ref[...].astype(F32), spread, preferred_element_type=F32)
    slot = lax.rem(lax.broadcasted_iota(jnp.int32, (1, slots), 1), 8).astype(F32)
    at = lax.broadcasted_iota(jnp.int32, (rows, slots), 0)
    target = (lax.rem(at, 16) // 4) * 16 + lax.bitwise_xor(at // 16, z) * 4 + lax.rem(at, 4)
    p = lax.broadcasted_iota(jnp.int32, (slots, arrivals), 1)
    bit = lambda shift: lax.rem(lax.shift_right_logical(p, shift), 2)
    row = lax.bitwise_xor(bit(5), y) * 2 + lax.bitwise_xor(bit(4), c)
    sender = row * 4 + lax.bitwise_xor(lax.shift_right_logical(p, 6), z)
    source = sender * 8 + lax.rem(p, 8)
    entry = lax.broadcasted_iota(jnp.int32, (slots, arrivals), 0)
    for step in range(2):
        live = slot < held[step : step + 1]
        chosen = jnp.where(live, assign_ref[step : step + 1, :], -1)
        placed = (chosen == target).astype(F32).astype(BF)
        moved = ((entry == source) & (bit(3) == step)).astype(F32).astype(BF)
        pick_ref[step * rows : (step + 1) * rows, :] = jnp.dot(
            placed, moved, preferred_element_type=F32
        ).astype(BF)


def quarter_copies(dy, dc, weights, out_ref, sems):
    y, c, _ = place()
    width = out_ref.shape[1] // 2
    start = (lax.bitwise_xor(c, dc) * 2 + lax.bitwise_xor(y, dy)) * width
    at = pl.ds(pl.multiple_of(start, 128), width)
    return [
        pltpu.make_async_copy(w.at[:, at], out_ref.at[:, pl.ds(i * width, width)], sems.at[i])
        for i, w in enumerate(weights)
    ]


def quarter_body(dy, dc, ins, weights, outs, scratch):
    copies = quarter_copies(dy, dc, weights, outs[0], scratch[0])
    for copy in copies:
        copy.start()
    for copy in copies:
        copy.wait()


def dot_and_quarter_body(dy, dc, ins, weights, outs, scratch):
    copies = quarter_copies(dy, dc, weights, outs[-1], scratch[0])
    for copy in copies:
        copy.start()
    x_ref, w_ref = ins
    rows = outs[0].shape[0]

    @pl.loop(0, w_ref.shape[1] // 256)
    def _(i):
        at = pl.ds(pl.multiple_of(i * 256, 256), 256)
        total = jnp.dot(x_ref[...], w_ref[:, at], preferred_element_type=F32).astype(BF)
        for k, out in enumerate(outs[:-1]):
            out[:, at] = total[k * rows : (k + 1) * rows]

    for copy in copies:
        copy.wait()


def fetch_quarter(gate_w, up_w, dy, dc, token):
    shape = pltpu.VMEM((gate_w.shape[0], gate_w.shape[1] // 2), BF)
    return run(
        functools.partial(quarter_body, dy, dc),
        (shape,),
        (),
        token,
        (gate_w, up_w),
        (pltpu.SemaphoreType.DMA((2,)),),
    )


def down_rows_body(dy, ins, _, outs, scratch):
    y, c, _ = place()
    (out_ref,) = outs
    height = out_ref.shape[0] // 2
    copies = []
    for dc in range(2):
        start = (lax.bitwise_xor(c, dc) * 2 + lax.bitwise_xor(y, dy)) * height
        copies.append(
            pltpu.make_async_copy(
                ins[0].at[pl.ds(pl.multiple_of(start, 16), height), :],
                out_ref.at[pl.ds(dc * height, height), :],
                scratch[0].at[dc],
            )
        )
    for copy in copies:
        copy.start()
    for copy in copies:
        copy.wait()


def meet(token):
    return lax.ppermute(token, "row", X1)


def stack_body(ins, _, outs, __):
    for i, piece in enumerate(ins):
        joined = jnp.concatenate([piece[step].astype(F32) for step in range(2)], axis=0)
        outs[0][i * 16 : (i + 1) * 16, :] = joined.astype(BF)


def after_body(ins, _, outs, __):
    rows = outs[0].shape[0]
    for i, out in enumerate(outs):
        out[...] = ins[0][i * rows : (i + 1) * rows, :]


def halves_dot(x_ref, w_refs):
    total = 0.0
    height = w_refs[0].shape[0]
    for i, w_ref in enumerate(w_refs):
        at = slice(i * height, (i + 1) * height)
        total = total + jnp.dot(x_ref[:, at], w_ref[...], preferred_element_type=F32)
    return total


def store_rows(outs, value):
    rows = outs[0].shape[0]
    for i, out in enumerate(outs):
        out[...] = value[i * rows : (i + 1) * rows].astype(out.dtype)


def load_rows(refs):
    return jnp.concatenate([ref[...].astype(F32) for ref in refs], axis=0)


def first_body(ins, _, outs, scratch):
    pieces, pick_ref, w_refs = ins[:8], ins[8], ins[9:]
    batch_ref, pieces_out = outs[0], outs[1:]
    slots = scratch[0]
    height = pieces[0].shape[0]
    for i, piece in enumerate(pieces):
        slots[i * height : (i + 1) * height, :] = piece[...]
    batch_ref[...] = jnp.dot(pick_ref[...], slots[...], preferred_element_type=F32).astype(BF)
    store_rows(pieces_out, halves_dot(batch_ref, w_refs))


def dot_body(ins, _, outs, __):
    store_rows(outs, halves_dot(ins[0], ins[1:]))


def far_body(ins, _, outs, __):
    store_rows(outs, ins[0][...] + load_rows(ins[1:]))


def hidden_body(step, ins, _, outs, __):
    rows, width = outs[0].shape
    total = ins[0][step * rows : (step + 1) * rows, :] + ins[1][...].astype(F32) + load_rows(ins[2:])
    gate, up = total[:, :width], total[:, width:]
    outs[0][...] = (gate / (1.0 + jnp.exp(-gate)) * up).astype(BF)


def down_part_body(ins, _, outs, __):
    own_ref, core_ref, w_ref = ins
    height = w_ref.shape[0] // 2
    total = jnp.dot(own_ref[...], w_ref[:height, :], preferred_element_type=F32)
    outs[0][...] = total + jnp.dot(core_ref[...], w_ref[height:, :], preferred_element_type=F32)


def down_rest_body(ins, _, outs, __):
    y_ref, w_ref, part_ref, yd_refs = *ins[:3], ins[3:]
    rows = outs[0].shape[0]
    height = w_ref.shape[0] // 2
    total = part_ref[...] + jnp.dot(y_ref[...], w_ref[:height, :], preferred_element_type=F32)
    total = total + jnp.dot(load_rows(yd_refs).astype(BF), w_ref[height:, :], preferred_element_type=F32)
    for i, out in enumerate(outs):
        out[...] = total[i * rows : (i + 1) * rows].astype(out.dtype)


def owner_body(ins, _, outs, __):
    y, c, _ = place()
    at = lax.broadcasted_iota(jnp.int32, (16, 16), 0)
    source = lax.bitwise_xor(at, (y * 2 + c) * 4)
    turn = (lax.broadcasted_iota(jnp.int32, (16, 16), 1) == source).astype(F32).astype(BF)
    for step in range(2):
        total = ins[step * 4][...]
        for got in ins[step * 4 + 1 : step * 4 + 4]:
            total = total + got[...].astype(F32)
        turned = jnp.dot(turn, total.astype(BF), preferred_element_type=F32)
        for i, out in enumerate(outs):
            out[step] = turned[i * 4 : (i + 1) * 4].astype(BF)


def output_body(ins, _, outs, __):
    y, c, _ = place()
    width = ins[0].shape[2]
    for dy, dc, block in ((0, 0, ins[0]), (0, 1, ins[1]), (1, 0, ins[2]), (1, 1, ins[3])):
        source = lax.bitwise_xor(y, dy) * 2 + lax.bitwise_xor(c, dc)
        outs[0][:, :, pl.ds(pl.multiple_of(source * width, width), width)] = block[...]


def near_plan(sender_rows, counts, assign, gate_w, up_w, down_w):
    steps, slots, width = sender_rows.shape
    width //= 4
    units = gate_w.shape[1] // 4
    rows = MEAN * counts.shape[1]
    part = rows // 4

    def down_rows(dy, token):
        shape = pltpu.VMEM((down_w.shape[0] // 2, down_w.shape[1]), BF)
        scratch = (pltpu.SemaphoreType.DMA((2,)),)
        spec = pl.BlockSpec(memory_space=pl.ANY)
        return run(functools.partial(down_rows_body, dy), (shape,), (down_w,), token, (), scratch, spec=spec)

    y, yd, core, own, token = normed_blocks(sender_rows)
    y, yd = lax.ppermute(y, "row", X2), lax.ppermute(yd, "row", X3)
    core = lax.ppermute(core, "row", X1)
    quarters = {}

    def bring(dy, dc, token):
        w, token = fetch_quarter(gate_w, up_w, dy, dc, token)
        quarters.setdefault((dy, dc), []).append(w)
        return token

    block = like((4 * slots, width))
    near_block, token = run(stack_body, (block,), (own, core), token)
    near_sent = [lax.ppermute(near_block, "col", X3), lax.ppermute(near_block, "col", X1)]
    token = meet(token)
    far_block, token = run(stack_body, (block,), (y, yd), token)
    far_sent = [lax.ppermute(far_block, "col", X3), lax.ppermute(far_block, "col", X1)]
    token = meet(token)
    token = bring(1, 1, token)
    passed, token = run(after_body, (block,), (near_sent[0], near_sent[1]), token)
    near_sent.append(lax.ppermute(passed, "col", X1))
    token = meet(token)
    token = bring(1, 0, token)
    pick, token = run(pick_body, (like((steps * rows, steps * assign.shape[1])),), (counts, assign), token)
    passed, token = run(after_body, (block,), (far_sent[0], far_sent[1]), token)
    far_sent.append(lax.ppermute(passed, "col", X1))
    token = meet(token)
    token = bring(0, 1, token)
    pieces = []
    for dz in range(4):
        for own_block, sent in ((near_block, near_sent), (far_block, far_sent)):
            pieces.append((own_block, sent[1], sent[2], sent[0])[dz])

    bits = (like((steps * rows // PIECES, 2 * units)),) * PIECES
    wide = like((steps * rows, 2 * units), F32)
    batch, *out, token = run(
        first_body,
        (like((steps * rows, width)),) + bits,
        tuple(pieces) + (pick, *quarters[1, 1]),
        token,
        (),
        (pltpu.VMEM((32 * slots, width), BF),),
    )
    cores = tuple(lax.ppermute(o, "row", X1) for o in out)
    own_far, token = run(dot_body, (wide,), (batch, *quarters[1, 0]), token)
    *sends, token = run(far_body, (like((rows, 2 * units)),) * steps, (own_far,) + cores, token)
    gots = [lax.ppermute(send, "row", X2) for send in sends]
    token = meet(token)
    last = pltpu.VMEM((gate_w.shape[0], gate_w.shape[1] // 2), BF)
    *out, last, token = run(
        functools.partial(dot_and_quarter_body, 0, 0),
        bits + (last,),
        (batch, *quarters[0, 1]),
        token,
        (gate_w, up_w),
        (pltpu.SemaphoreType.DMA((2,)),),
    )
    cores = tuple(lax.ppermute(o, "row", X1) for o in out)
    own_near, token = run(dot_body, (wide,), (batch, last), token)
    down_near, token = down_rows(0, token)
    hidden, sums = [], []

    def activate(step, token):
        each = PIECES // steps
        near = cores[step * each : (step + 1) * each]
        operands = (own_near, gots[step]) + near
        body = functools.partial(hidden_body, step)
        result, token = run(body, (like((rows, units)),), operands, token)
        y = lax.ppermute(result, "row", X2)
        hidden.append((result, lax.ppermute(result, "row", X1), y))
        return token

    def down_part(step, token):
        return run(down_part_body, (like((rows, width), F32),), hidden[step][:2] + (down_near,), token)

    def down_rest(step, part_sum, token):
        cut = (like((16, units)),) * (rows // 16)
        *passed, token = run(after_body, cut, (hidden[step][2],), token)
        passed = tuple(lax.ppermute(p, "row", X1) for p in passed)
        outs = (like((part, width), F32),) + (like((part, width)),) * 3
        operands = (hidden[step][2], down_far, part_sum) + passed
        keep, send1, send2, send3, token = run(down_rest_body, outs, operands, token)
        got = [lax.ppermute(s, "col", x) for s, x in ((send3, X3), (send2, X2), (send1, X1))]
        sums.extend([keep] + got)
        return token

    token = activate(0, token)
    down_far, token = down_rows(1, token)
    part0, token = down_part(0, token)
    token = activate(1, token)
    token = down_rest(0, part0, token)
    part1, token = down_part(1, meet(token))
    token = down_rest(1, part1, token)
    own, core, y, yd, token = run(owner_body, (like((steps, MEAN, width)),) * 4, tuple(sums), token)
    blocks = (own, lax.ppermute(core, "row", X1), lax.ppermute(y, "row", X2), lax.ppermute(yd, "row", X3))
    result, _ = run(output_body, (like((steps, MEAN, 4 * width)),), blocks, token)
    return result


def layer_block(normed_block, counts_block, assign_block, paired, down_w, hidden_cols):
    row_devices = lax.axis_size("row")
    col_devices = lax.axis_size("col")
    step_count = normed_block.shape[0]
    capacity = normed_block.shape[1]
    rows_step = MEAN * counts_block.shape[1]
    spread = lax.all_to_all(normed_block, "row", split_axis=2, concat_axis=1, tiled=True)
    gathered = lax.all_gather(spread, "col", axis=1, tiled=True)
    slot_count = gathered.shape[1]
    stacked = gathered.reshape(step_count * slot_count, gathered.shape[2])
    targets = (
        assign_block.reshape(step_count, row_devices, col_devices, capacity)
        .transpose(0, 2, 1, 3)
        .reshape(step_count, slot_count)
    )
    holdings = counts_block.reshape(step_count, row_devices, col_devices).transpose(0, 2, 1)
    slot_grid = lax.broadcasted_iota(jnp.int32, (step_count, col_devices, row_devices, capacity), 3)
    live_mask = (slot_grid < holdings[..., None]).reshape(step_count, slot_count)
    targets = jnp.where(live_mask, targets, rows_step)
    slot_ids = lax.broadcasted_iota(jnp.int32, (step_count, slot_count), 1)
    step_ids = lax.broadcasted_iota(jnp.int32, (step_count, slot_count), 0)
    inverse = (
        jnp.zeros((step_count, rows_step), jnp.int32)
        .at[step_ids, targets]
        .set(slot_ids, mode="drop")
    )
    grid_shape = (col_devices, row_devices, step_count, MEAN)
    col_ids = lax.broadcasted_iota(jnp.int32, grid_shape, 0)
    row_ids = lax.broadcasted_iota(jnp.int32, grid_shape, 1)
    step_grid = lax.broadcasted_iota(jnp.int32, grid_shape, 2)
    member = lax.broadcasted_iota(jnp.int32, grid_shape, 3)
    row_numbers = (row_ids * col_devices + col_ids) * MEAN + member
    positions = (step_grid * slot_count + inverse[step_grid, row_numbers]).reshape(-1)
    inputs = jnp.take(stacked, positions, axis=0)
    rows_here = inputs
    gate_up = lax.psum_scatter(
        jnp.dot(rows_here, paired, preferred_element_type=jnp.float32).astype(jnp.bfloat16),
        "row",
        scatter_dimension=0,
        tiled=True,
    ).astype(jnp.float32)
    hidden = (jax.nn.silu(gate_up[:, :hidden_cols]) * gate_up[:, hidden_cols:]).astype(jnp.bfloat16)
    hidden_all = lax.all_gather(hidden, "row", axis=0, tiled=True)
    rows_here = hidden_all
    summed = lax.psum_scatter(
        jnp.dot(rows_here, down_w, preferred_element_type=jnp.float32).astype(jnp.bfloat16),
        "col",
        scatter_dimension=0,
        tiled=True,
    )
    finished = lax.all_to_all(summed, "row", split_axis=0, concat_axis=1, tiled=True)
    return finished.reshape(step_count, MEAN, finished.shape[1])


def any_plan(sender_rows, counts, assign, gate_w, up_w, down_w):
    values = sender_rows.astype(jnp.float32)
    normed = (
        values * lax.rsqrt(jnp.mean(values * values, axis=-1, keepdims=True) + epsilon)
    ).astype(jnp.bfloat16)
    paired = jnp.concatenate((gate_w, up_w), axis=1)
    hidden_cols = gate_w.shape[1]
    outputs = []
    for step_index in range(STEPS):
        outputs.append(
            layer_block(
                normed[step_index : step_index + 1],
                counts[step_index : step_index + 1],
                assign[step_index : step_index + 1],
                paired,
                down_w,
                hidden_cols,
            )
        )
    result = jnp.concatenate(outputs, axis=0)
    return result


def solution(mesh):
    near = mesh.shape["row"] == 4 and mesh.shape["col"] == 4
    return jax.shard_map(
        near_plan if near else any_plan,
        mesh=mesh,
        in_specs=(
            P(None, ("groups", "row", "col"), None),
            P(None, "groups"),
            P(None, "groups"),
            P("row", "col"),
            P("row", "col"),
            P("col", "row"),
        ),
        out_specs=P(None, ("groups", "row", "col"), None),
        check_vma=False,
    )
```

```python
import functools

import jax
import jax.numpy as jnp
from jax import lax
from jax.experimental import pallas as pl
from jax.experimental.pallas import tpu as pltpu
from jax.sharding import PartitionSpec as P

STEPS = 2
MEAN = 4

epsilon = 1e-05

BF = jnp.bfloat16
F32 = jnp.float32
MIB = 2**20
PIECES = 2
CUTS = 1
X1 = ((0, 1), (1, 0), (2, 3), (3, 2))
X2 = ((0, 2), (1, 3), (2, 0), (3, 1))
X3 = ((0, 3), (1, 2), (2, 1), (3, 0))


def place():
    row = lax.axis_index("row")
    return row // 2, lax.rem(row, 2), lax.axis_index("col")


def run(body, outs, operands, token, weights=(), scratch=(), cost=1, spec=None):
    count, held = len(operands), len(weights)
    skip = count + held + (token is not None)
    vmem = pl.BlockSpec(memory_space=pltpu.VMEM)
    outs = tuple(outs) + (like((8, 128), F32),)

    def wrapped(*refs):
        results = refs[skip:]
        body(refs[:count], refs[count : count + held], results[: len(outs) - 1], results[len(outs) :])
        results[len(outs) - 1][...] = jnp.zeros((8, 128), F32)

    return pl.pallas_call(
        wrapped,
        out_shape=outs,
        in_specs=[spec or vmem] * count
        + [pl.BlockSpec(memory_space=pltpu.HBM)] * held
        + [pl.BlockSpec(memory_space=pl.ANY)] * (token is not None),
        out_specs=(vmem,) * len(outs),
        scratch_shapes=scratch,
        compiler_params=pltpu.CompilerParams(vmem_limit_bytes=8 * MIB),
        cost_estimate=pl.CostEstimate(flops=0, bytes_accessed=cost, transcendentals=0),
    )(*operands, *(pltpu.with_memory_space_constraint(w, pltpu.HBM) for w in weights), *(() if token is None else (token,)))


def like(shape, dtype=BF):
    return jax.ShapeDtypeStruct(shape, dtype)


def norm_body(ins, _, outs, __):
    (rows_ref,) = ins
    y, c, _ = place()
    width = outs[0].shape[2]
    for step in range(rows_ref.shape[0]):
        total = jnp.sum(jnp.square(rows_ref[step].astype(F32)), axis=-1, keepdims=True)
        scale = lax.rsqrt(total / rows_ref.shape[2] + epsilon)
        for out, (dy, dc) in zip(outs, ((1, 0), (1, 1), (0, 1), (0, 0))):
            block = lax.bitwise_xor(y, dy) * 2 + lax.bitwise_xor(c, dc)
            at = pl.ds(pl.multiple_of(block * width, width), width)
            out[step] = (rows_ref[step, :, at].astype(F32) * scale).astype(BF)


def normed_blocks(sender_rows):
    steps, slots, width = sender_rows.shape
    return run(norm_body, (like((steps, slots, width // 4)),) * 4, (sender_rows,), None)


def pick_body(ins, _, outs, __):
    counts_ref, assign_ref = ins
    (pick_ref,) = outs
    y, c, z = place()
    rows = pick_ref.shape[0] // 2
    slots = assign_ref.shape[1]
    arrivals = pick_ref.shape[1]
    spread = (
        lax.broadcasted_iota(jnp.int32, (slots // 8, slots), 1) // 8
        == lax.broadcasted_iota(jnp.int32, (slots // 8, slots), 0)
    ).astype(F32)
    held = jnp.dot(counts_ref[...].astype(F32), spread, preferred_element_type=F32)
    slot = lax.rem(lax.broadcasted_iota(jnp.int32, (1, slots), 1), 8).astype(F32)
    at = lax.broadcasted_iota(jnp.int32, (rows, slots), 0)
    target = (lax.rem(at, 16) // 4) * 16 + lax.bitwise_xor(at // 16, z) * 4 + lax.rem(at, 4)
    p = lax.broadcasted_iota(jnp.int32, (slots, arrivals), 1)
    bit = lambda shift: lax.rem(lax.shift_right_logical(p, shift), 2)
    row = lax.bitwise_xor(bit(5), y) * 2 + lax.bitwise_xor(bit(4), c)
    sender = row * 4 + lax.bitwise_xor(lax.shift_right_logical(p, 6), z)
    source = sender * 8 + lax.rem(p, 8)
    entry = lax.broadcasted_iota(jnp.int32, (slots, arrivals), 0)
    for step in range(2):
        live = slot < held[step : step + 1]
        chosen = jnp.where(live, assign_ref[step : step + 1, :], -1)
        placed = (chosen == target).astype(F32).astype(BF)
        moved = ((entry == source) & (bit(3) == step)).astype(F32).astype(BF)
        pick_ref[step * rows : (step + 1) * rows, :] = jnp.dot(
            placed, moved, preferred_element_type=F32
        ).astype(BF)


def quarter_copies(dy, dc, weights, out_ref, sems):
    y, c, _ = place()
    width = out_ref.shape[1] // 2
    start = (lax.bitwise_xor(c, dc) * 2 + lax.bitwise_xor(y, dy)) * width
    at = pl.ds(pl.multiple_of(start, 128), width)
    return [
        pltpu.make_async_copy(w.at[:, at], out_ref.at[:, pl.ds(i * width, width)], sems.at[i])
        for i, w in enumerate(weights)
    ]


def quarter_body(dy, dc, ins, weights, outs, scratch):
    copies = quarter_copies(dy, dc, weights, outs[0], scratch[0])
    for copy in copies:
        copy.start()
    for copy in copies:
        copy.wait()


def dot_and_quarter_body(dy, dc, ins, weights, outs, scratch):
    copies = quarter_copies(dy, dc, weights, outs[-1], scratch[0])
    for copy in copies:
        copy.start()
    x_ref, w_ref = ins
    rows = outs[0].shape[0]

    @pl.loop(0, w_ref.shape[1] // 256)
    def _(i):
        at = pl.ds(pl.multiple_of(i * 256, 256), 256)
        total = jnp.dot(x_ref[...], w_ref[:, at], preferred_element_type=F32).astype(BF)
        for k, out in enumerate(outs[:-1]):
            out[:, at] = total[k * rows : (k + 1) * rows]

    for copy in copies:
        copy.wait()


def fetch_quarter(gate_w, up_w, dy, dc, token):
    shape = pltpu.VMEM((gate_w.shape[0], gate_w.shape[1] // 2), BF)
    return run(
        functools.partial(quarter_body, dy, dc),
        (shape,),
        (),
        token,
        (gate_w, up_w),
        (pltpu.SemaphoreType.DMA((2,)),),
    )


def down_rows_body(dy, ins, _, outs, scratch):
    y, c, _ = place()
    (out_ref,) = outs
    height = out_ref.shape[0] // 2
    copies = []
    for dc in range(2):
        start = (lax.bitwise_xor(c, dc) * 2 + lax.bitwise_xor(y, dy)) * height
        copies.append(
            pltpu.make_async_copy(
                ins[0].at[pl.ds(pl.multiple_of(start, 16), height), :],
                out_ref.at[pl.ds(dc * height, height), :],
                scratch[0].at[dc],
            )
        )
    for copy in copies:
        copy.start()
    for copy in copies:
        copy.wait()


def stack_body(ins, _, outs, __):
    for i, piece in enumerate(ins):
        joined = jnp.concatenate([piece[step].astype(F32) for step in range(2)], axis=0)
        outs[0][i * 16 : (i + 1) * 16, :] = joined.astype(BF)


def after_body(ins, _, outs, __):
    rows = outs[0].shape[0]
    for i, out in enumerate(outs):
        out[...] = ins[0][i * rows : (i + 1) * rows, :]


def halves_dot(x_ref, w_refs):
    total = 0.0
    height = w_refs[0].shape[0]
    for i, w_ref in enumerate(w_refs):
        at = slice(i * height, (i + 1) * height)
        total = total + jnp.dot(x_ref[:, at], w_ref[...], preferred_element_type=F32)
    return total


def store_rows(outs, value):
    rows = outs[0].shape[0]
    for i, out in enumerate(outs):
        out[...] = value[i * rows : (i + 1) * rows].astype(out.dtype)


def load_rows(refs):
    return jnp.concatenate([ref[...].astype(F32) for ref in refs], axis=0)


def first_body(ins, _, outs, scratch):
    pieces, pick_ref, w_refs = ins[:8], ins[8], ins[9:]
    batch_ref, pieces_out = outs[0], outs[1:]
    slots = scratch[0]
    height = pieces[0].shape[0]
    for i, piece in enumerate(pieces):
        slots[i * height : (i + 1) * height, :] = piece[...]
    batch_ref[...] = jnp.dot(pick_ref[...], slots[...], preferred_element_type=F32).astype(BF)
    store_rows(pieces_out, halves_dot(batch_ref, w_refs))


def dot_body(ins, _, outs, __):
    store_rows(outs, halves_dot(ins[0], ins[1:]))


def far_body(ins, _, outs, __):
    store_rows(outs, ins[0][...] + load_rows(ins[1:]))


def hidden_body(step, ins, _, outs, __):
    rows, width = outs[0].shape
    total = ins[0][step * rows : (step + 1) * rows, :] + ins[1][...].astype(F32) + load_rows(ins[2:])
    gate, up = total[:, :width], total[:, width:]
    outs[0][...] = (gate / (1.0 + jnp.exp(-gate)) * up).astype(BF)


def down_part_body(ins, _, outs, __):
    w_ref, hidden = ins[0], ins[1:]
    height = w_ref.shape[0] // 2
    own, core = (jnp.concatenate([x[...] for x in hidden[i : i + 2]], axis=0) for i in (0, 2))
    total = jnp.dot(own, w_ref[:height, :], preferred_element_type=F32)
    outs[0][...] = total + jnp.dot(core, w_ref[height:, :], preferred_element_type=F32)


def down_rest_body(ins, _, outs, __):
    w_ref, part_ref, y0_ref, y1_ref = ins[:4]
    steps, rows, _ = outs[0].shape
    height = w_ref.shape[0] // 2
    y = jnp.concatenate([y0_ref[...], y1_ref[...]], axis=0)
    total = part_ref[...] + jnp.dot(y, w_ref[:height, :], preferred_element_type=F32)
    yd = load_rows(ins[4:]).astype(BF)
    total = total + jnp.dot(yd, w_ref[height:, :], preferred_element_type=F32)
    for i, out in enumerate(outs):
        for step in range(steps):
            at = (step * len(outs) + i) * rows
            out[step] = total[at : at + rows].astype(out.dtype)


def owner_body(ins, _, outs, __):
    y, c, _ = place()
    at = lax.broadcasted_iota(jnp.int32, (16, 16), 0)
    source = lax.bitwise_xor(at, (y * 2 + c) * 4)
    turn = (lax.broadcasted_iota(jnp.int32, (16, 16), 1) == source).astype(F32).astype(BF)
    for step in range(2):
        total = ins[0][step]
        for got in ins[1:]:
            total = total + got[step].astype(F32)
        turned = jnp.dot(turn, total.astype(BF), preferred_element_type=F32)
        for i, out in enumerate(outs):
            out[step] = turned[i * 4 : (i + 1) * 4].astype(BF)


def output_body(ins, _, outs, __):
    y, c, _ = place()
    width = ins[0].shape[2]
    for dy, dc, block in ((0, 0, ins[0]), (0, 1, ins[1]), (1, 0, ins[2]), (1, 1, ins[3])):
        source = lax.bitwise_xor(y, dy) * 2 + lax.bitwise_xor(c, dc)
        outs[0][:, :, pl.ds(pl.multiple_of(source * width, width), width)] = block[...]


def near_plan(sender_rows, counts, assign, gate_w, up_w, down_w):
    steps, slots, width = sender_rows.shape
    width //= 4
    units = gate_w.shape[1] // 4
    rows = MEAN * counts.shape[1]
    part = rows // 4

    def down_rows(dy, token):
        shape = pltpu.VMEM((down_w.shape[0] // 2, down_w.shape[1]), BF)
        scratch = (pltpu.SemaphoreType.DMA((2,)),)
        spec = pl.BlockSpec(memory_space=pl.ANY)
        return run(functools.partial(down_rows_body, dy), (shape,), (down_w,), token, (), scratch, spec=spec)

    y, yd, core, own, token = normed_blocks(sender_rows)
    y, yd = lax.ppermute(y, "row", X2), lax.ppermute(yd, "row", X3)
    core = lax.ppermute(core, "row", X1)
    quarters = {}

    def bring(dy, dc, token):
        w, token = fetch_quarter(gate_w, up_w, dy, dc, token)
        quarters.setdefault((dy, dc), []).append(w)
        return token

    block = like((4 * slots, width))
    near_block, token = run(stack_body, (block,), (own, core), token)
    near_sent = [lax.ppermute(near_block, "col", X3), lax.ppermute(near_block, "col", X1)]
    far_block, token = run(stack_body, (block,), (y, yd), token)
    far_sent = [lax.ppermute(far_block, "col", X3), lax.ppermute(far_block, "col", X1)]
    token = bring(1, 1, token)
    passed, token = run(after_body, (block,), (near_sent[0], near_sent[1]), token)
    near_sent.append(lax.ppermute(passed, "col", X1))
    token = bring(1, 0, token)
    pick, token = run(pick_body, (like((steps * rows, steps * assign.shape[1])),), (counts, assign), token)
    passed, token = run(after_body, (block,), (far_sent[0], far_sent[1]), token)
    far_sent.append(lax.ppermute(passed, "col", X1))
    token = bring(0, 1, token)
    pieces = []
    for dz in range(4):
        for own_block, sent in ((near_block, near_sent), (far_block, far_sent)):
            pieces.append((own_block, sent[1], sent[2], sent[0])[dz])

    bits = (like((steps * rows // PIECES, 2 * units)),) * PIECES
    wide = like((steps * rows, 2 * units), F32)
    batch, *out, token = run(
        first_body,
        (like((steps * rows, width)),) + bits,
        tuple(pieces) + (pick, *quarters[1, 1]),
        token,
        (),
        (pltpu.VMEM((32 * slots, width), BF),),
    )
    cores = tuple(lax.ppermute(o, "row", X1) for o in out)
    own_far, token = run(dot_body, (wide,), (batch, *quarters[1, 0]), token)
    *sends, token = run(far_body, (like((rows, 2 * units)),) * steps, (own_far,) + cores, token)
    gots = [lax.ppermute(send, "row", X2) for send in sends]
    last = pltpu.VMEM((gate_w.shape[0], gate_w.shape[1] // 2), BF)
    *out, last, token = run(
        functools.partial(dot_and_quarter_body, 0, 0),
        bits + (last,),
        (batch, *quarters[0, 1]),
        token,
        (gate_w, up_w),
        (pltpu.SemaphoreType.DMA((2,)),),
    )
    cores = tuple(lax.ppermute(o, "row", X1) for o in out)
    own_near, token = run(dot_body, (wide,), (batch, last), token)
    down_near, token = down_rows(0, token)
    hidden = []

    def activate(step, token):
        each = PIECES // steps
        near = cores[step * each : (step + 1) * each]
        operands = (own_near, gots[step]) + near
        body = functools.partial(hidden_body, step)
        result, token = run(body, (like((rows, units)),), operands, token)
        y = lax.ppermute(result, "row", X2)
        hidden.append((result, lax.ppermute(result, "row", X1), y))
        return token

    def shared(step, token):
        cut = (like((rows // CUTS, units)),) * CUTS
        *passed, token = run(after_body, cut, (hidden[step][2],), token)
        return tuple(lax.ppermute(p, "row", X1) for p in passed), token

    token = activate(0, token)
    down_far, token = down_rows(1, token)
    token = activate(1, token)
    yd0, token = shared(0, token)
    (own0, core0, y0), (own1, core1, y1) = hidden
    wide = like((steps * rows, width), F32)
    part_sum, token = run(down_part_body, (wide,), (down_near, own0, own1, core0, core1), token)
    yd1, token = shared(1, token)
    outs = (like((steps, part, width), F32),) + (like((steps, part, width)),) * 3
    operands = (down_far, part_sum, y0, y1) + yd0 + yd1
    keep, send1, send2, send3, token = run(down_rest_body, outs, operands, token)
    sums = [keep] + [lax.ppermute(s, "col", x) for s, x in ((send3, X3), (send2, X2), (send1, X1))]
    own, core, y, yd, token = run(owner_body, (like((steps, MEAN, width)),) * 4, tuple(sums), token)
    blocks = (own, lax.ppermute(core, "row", X1), lax.ppermute(y, "row", X2), lax.ppermute(yd, "row", X3))
    result, _ = run(output_body, (like((steps, MEAN, 4 * width)),), blocks, token)
    return result


def layer_block(normed_block, counts_block, assign_block, paired, down_w, hidden_cols):
    row_devices = lax.axis_size("row")
    col_devices = lax.axis_size("col")
    step_count = normed_block.shape[0]
    capacity = normed_block.shape[1]
    rows_step = MEAN * counts_block.shape[1]
    spread = lax.all_to_all(normed_block, "row", split_axis=2, concat_axis=1, tiled=True)
    gathered = lax.all_gather(spread, "col", axis=1, tiled=True)
    slot_count = gathered.shape[1]
    stacked = gathered.reshape(step_count * slot_count, gathered.shape[2])
    targets = (
        assign_block.reshape(step_count, row_devices, col_devices, capacity)
        .transpose(0, 2, 1, 3)
        .reshape(step_count, slot_count)
    )
    holdings = counts_block.reshape(step_count, row_devices, col_devices).transpose(0, 2, 1)
    slot_grid = lax.broadcasted_iota(jnp.int32, (step_count, col_devices, row_devices, capacity), 3)
    live_mask = (slot_grid < holdings[..., None]).reshape(step_count, slot_count)
    targets = jnp.where(live_mask, targets, rows_step)
    slot_ids = lax.broadcasted_iota(jnp.int32, (step_count, slot_count), 1)
    step_ids = lax.broadcasted_iota(jnp.int32, (step_count, slot_count), 0)
    inverse = (
        jnp.zeros((step_count, rows_step), jnp.int32)
        .at[step_ids, targets]
        .set(slot_ids, mode="drop")
    )
    grid_shape = (col_devices, row_devices, step_count, MEAN)
    col_ids = lax.broadcasted_iota(jnp.int32, grid_shape, 0)
    row_ids = lax.broadcasted_iota(jnp.int32, grid_shape, 1)
    step_grid = lax.broadcasted_iota(jnp.int32, grid_shape, 2)
    member = lax.broadcasted_iota(jnp.int32, grid_shape, 3)
    row_numbers = (row_ids * col_devices + col_ids) * MEAN + member
    positions = (step_grid * slot_count + inverse[step_grid, row_numbers]).reshape(-1)
    inputs = jnp.take(stacked, positions, axis=0)
    rows_here = inputs
    gate_up = lax.psum_scatter(
        jnp.dot(rows_here, paired, preferred_element_type=jnp.float32).astype(jnp.bfloat16),
        "row",
        scatter_dimension=0,
        tiled=True,
    ).astype(jnp.float32)
    hidden = (jax.nn.silu(gate_up[:, :hidden_cols]) * gate_up[:, hidden_cols:]).astype(jnp.bfloat16)
    hidden_all = lax.all_gather(hidden, "row", axis=0, tiled=True)
    rows_here = hidden_all
    summed = lax.psum_scatter(
        jnp.dot(rows_here, down_w, preferred_element_type=jnp.float32).astype(jnp.bfloat16),
        "col",
        scatter_dimension=0,
        tiled=True,
    )
    finished = lax.all_to_all(summed, "row", split_axis=0, concat_axis=1, tiled=True)
    return finished.reshape(step_count, MEAN, finished.shape[1])


def any_plan(sender_rows, counts, assign, gate_w, up_w, down_w):
    values = sender_rows.astype(jnp.float32)
    normed = (
        values * lax.rsqrt(jnp.mean(values * values, axis=-1, keepdims=True) + epsilon)
    ).astype(jnp.bfloat16)
    paired = jnp.concatenate((gate_w, up_w), axis=1)
    hidden_cols = gate_w.shape[1]
    outputs = []
    for step_index in range(STEPS):
        outputs.append(
            layer_block(
                normed[step_index : step_index + 1],
                counts[step_index : step_index + 1],
                assign[step_index : step_index + 1],
                paired,
                down_w,
                hidden_cols,
            )
        )
    result = jnp.concatenate(outputs, axis=0)
    return result


def solution(mesh):
    near = mesh.shape["row"] == 4 and mesh.shape["col"] == 4
    return jax.shard_map(
        near_plan if near else any_plan,
        mesh=mesh,
        in_specs=(
            P(None, ("groups", "row", "col"), None),
            P(None, "groups"),
            P(None, "groups"),
            P("row", "col"),
            P("row", "col"),
            P("col", "row"),
        ),
        out_specs=P(None, ("groups", "row", "col"), None),
        check_vma=False,
    )
```

```python
import functools

import jax
import jax.numpy as jnp
from jax import lax
from jax.experimental import pallas as pl
from jax.experimental.pallas import tpu as pltpu
from jax.sharding import PartitionSpec as P

STEPS = 2
MEAN = 4

epsilon = 1e-05

BF = jnp.bfloat16
F32 = jnp.float32
MIB = 2**20
PIECES = 2
CUTS = 2
X1 = ((0, 1), (1, 0), (2, 3), (3, 2))
X2 = ((0, 2), (1, 3), (2, 0), (3, 1))
X3 = ((0, 3), (1, 2), (2, 1), (3, 0))


def place():
    row = lax.axis_index("row")
    return row // 2, lax.rem(row, 2), lax.axis_index("col")


def run(body, outs, operands, token, weights=(), scratch=(), cost=1, spec=None):
    count, held = len(operands), len(weights)
    skip = count + held + (token is not None)
    vmem = pl.BlockSpec(memory_space=pltpu.VMEM)
    outs = tuple(outs) + (like((8, 128), F32),)

    def wrapped(*refs):
        results = refs[skip:]
        body(refs[:count], refs[count : count + held], results[: len(outs) - 1], results[len(outs) :])
        results[len(outs) - 1][...] = jnp.zeros((8, 128), F32)

    return pl.pallas_call(
        wrapped,
        out_shape=outs,
        in_specs=[spec or vmem] * count
        + [pl.BlockSpec(memory_space=pltpu.HBM)] * held
        + [pl.BlockSpec(memory_space=pl.ANY)] * (token is not None),
        out_specs=(vmem,) * len(outs),
        scratch_shapes=scratch,
        compiler_params=pltpu.CompilerParams(vmem_limit_bytes=8 * MIB),
        cost_estimate=pl.CostEstimate(flops=0, bytes_accessed=cost, transcendentals=0),
    )(*operands, *(pltpu.with_memory_space_constraint(w, pltpu.HBM) for w in weights), *(() if token is None else (token,)))


def like(shape, dtype=BF):
    return jax.ShapeDtypeStruct(shape, dtype)


def norm_body(ins, _, outs, __):
    (rows_ref,) = ins
    y, c, _ = place()
    width = outs[0].shape[2]
    for step in range(rows_ref.shape[0]):
        total = jnp.sum(jnp.square(rows_ref[step].astype(F32)), axis=-1, keepdims=True)
        scale = lax.rsqrt(total / rows_ref.shape[2] + epsilon)
        for out, (dy, dc) in zip(outs, ((1, 0), (1, 1), (0, 1), (0, 0))):
            block = lax.bitwise_xor(y, dy) * 2 + lax.bitwise_xor(c, dc)
            at = pl.ds(pl.multiple_of(block * width, width), width)
            out[step] = (rows_ref[step, :, at].astype(F32) * scale).astype(BF)


def normed_blocks(sender_rows):
    steps, slots, width = sender_rows.shape
    return run(norm_body, (like((steps, slots, width // 4)),) * 4, (sender_rows,), None)


def pick_body(ins, _, outs, __):
    counts_ref, assign_ref = ins
    (pick_ref,) = outs
    y, c, z = place()
    rows = pick_ref.shape[0] // 2
    slots = assign_ref.shape[1]
    arrivals = pick_ref.shape[1]
    spread = (
        lax.broadcasted_iota(jnp.int32, (slots // 8, slots), 1) // 8
        == lax.broadcasted_iota(jnp.int32, (slots // 8, slots), 0)
    ).astype(F32)
    held = jnp.dot(counts_ref[...].astype(F32), spread, preferred_element_type=F32)
    slot = lax.rem(lax.broadcasted_iota(jnp.int32, (1, slots), 1), 8).astype(F32)
    at = lax.broadcasted_iota(jnp.int32, (rows, slots), 0)
    target = (lax.rem(at, 16) // 4) * 16 + lax.bitwise_xor(at // 16, z) * 4 + lax.rem(at, 4)
    p = lax.broadcasted_iota(jnp.int32, (slots, arrivals), 1)
    bit = lambda shift: lax.rem(lax.shift_right_logical(p, shift), 2)
    row = lax.bitwise_xor(bit(5), y) * 2 + lax.bitwise_xor(bit(4), c)
    sender = row * 4 + lax.bitwise_xor(lax.shift_right_logical(p, 6), z)
    source = sender * 8 + lax.rem(p, 8)
    entry = lax.broadcasted_iota(jnp.int32, (slots, arrivals), 0)
    for step in range(2):
        live = slot < held[step : step + 1]
        chosen = jnp.where(live, assign_ref[step : step + 1, :], -1)
        placed = (chosen == target).astype(F32).astype(BF)
        moved = ((entry == source) & (bit(3) == step)).astype(F32).astype(BF)
        pick_ref[step * rows : (step + 1) * rows, :] = jnp.dot(
            placed, moved, preferred_element_type=F32
        ).astype(BF)


def quarter_copies(dy, dc, weights, out_ref, sems):
    y, c, _ = place()
    width = out_ref.shape[1] // 2
    start = (lax.bitwise_xor(c, dc) * 2 + lax.bitwise_xor(y, dy)) * width
    at = pl.ds(pl.multiple_of(start, 128), width)
    return [
        pltpu.make_async_copy(w.at[:, at], out_ref.at[:, pl.ds(i * width, width)], sems.at[i])
        for i, w in enumerate(weights)
    ]


def quarter_body(dy, dc, ins, weights, outs, scratch):
    copies = quarter_copies(dy, dc, weights, outs[0], scratch[0])
    for copy in copies:
        copy.start()
    for copy in copies:
        copy.wait()


def dot_and_quarter_body(dy, dc, ins, weights, outs, scratch):
    copies = quarter_copies(dy, dc, weights, outs[-1], scratch[0])
    for copy in copies:
        copy.start()
    x_ref, w_ref = ins
    rows = outs[0].shape[0]

    @pl.loop(0, w_ref.shape[1] // 256)
    def _(i):
        at = pl.ds(pl.multiple_of(i * 256, 256), 256)
        total = jnp.dot(x_ref[...], w_ref[:, at], preferred_element_type=F32).astype(BF)
        for k, out in enumerate(outs[:-1]):
            out[:, at] = total[k * rows : (k + 1) * rows]

    for copy in copies:
        copy.wait()


def fetch_quarter(gate_w, up_w, dy, dc, token):
    shape = pltpu.VMEM((gate_w.shape[0], gate_w.shape[1] // 2), BF)
    return run(
        functools.partial(quarter_body, dy, dc),
        (shape,),
        (),
        token,
        (gate_w, up_w),
        (pltpu.SemaphoreType.DMA((2,)),),
    )


def down_rows_body(dy, ins, _, outs, scratch):
    y, c, _ = place()
    (out_ref,) = outs
    height = out_ref.shape[0] // 2
    copies = []
    for dc in range(2):
        start = (lax.bitwise_xor(c, dc) * 2 + lax.bitwise_xor(y, dy)) * height
        copies.append(
            pltpu.make_async_copy(
                ins[0].at[pl.ds(pl.multiple_of(start, 16), height), :],
                out_ref.at[pl.ds(dc * height, height), :],
                scratch[0].at[dc],
            )
        )
    for copy in copies:
        copy.start()
    for copy in copies:
        copy.wait()


def stack_body(ins, _, outs, __):
    for i, piece in enumerate(ins):
        joined = jnp.concatenate([piece[step].astype(F32) for step in range(2)], axis=0)
        outs[0][i * 16 : (i + 1) * 16, :] = joined.astype(BF)


def after_body(ins, _, outs, __):
    rows = outs[0].shape[0]
    for i, out in enumerate(outs):
        out[...] = ins[0][i * rows : (i + 1) * rows, :]


def halves_dot(x_ref, w_refs):
    total = 0.0
    height = w_refs[0].shape[0]
    for i, w_ref in enumerate(w_refs):
        at = slice(i * height, (i + 1) * height)
        total = total + jnp.dot(x_ref[:, at], w_ref[...], preferred_element_type=F32)
    return total


def store_rows(outs, value):
    rows = outs[0].shape[0]
    for i, out in enumerate(outs):
        out[...] = value[i * rows : (i + 1) * rows].astype(out.dtype)


def load_rows(refs):
    return jnp.concatenate([ref[...].astype(F32) for ref in refs], axis=0)


def first_body(ins, _, outs, scratch):
    pieces, pick_ref, w_refs = ins[:8], ins[8], ins[9:]
    batch_ref, pieces_out = outs[0], outs[1:]
    slots = scratch[0]
    height = pieces[0].shape[0]
    for i, piece in enumerate(pieces):
        slots[i * height : (i + 1) * height, :] = piece[...]
    batch_ref[...] = jnp.dot(pick_ref[...], slots[...], preferred_element_type=F32).astype(BF)
    store_rows(pieces_out, halves_dot(batch_ref, w_refs))


def dot_body(ins, _, outs, __):
    store_rows(outs, halves_dot(ins[0], ins[1:]))


def far_body(ins, _, outs, __):
    store_rows(outs, ins[0][...] + load_rows(ins[1:]))


def hidden_body(step, ins, _, outs, __):
    rows, width = outs[0].shape
    total = ins[0][step * rows : (step + 1) * rows, :] + ins[1][...].astype(F32) + load_rows(ins[2:])
    gate, up = total[:, :width], total[:, width:]
    outs[0][...] = (gate / (1.0 + jnp.exp(-gate)) * up).astype(BF)


def down_part_body(ins, _, outs, __):
    w_ref, own_ref, core_ref = ins
    height = w_ref.shape[0] // 2
    total = jnp.dot(own_ref[...], w_ref[:height, :], preferred_element_type=F32)
    outs[0][...] = total + jnp.dot(core_ref[...], w_ref[height:, :], preferred_element_type=F32)


def down_rest_body(ins, _, outs, __):
    w_ref, part_ref, y_ref = ins[:3]
    rows = outs[0].shape[0]
    height = w_ref.shape[0] // 2
    total = part_ref[...] + jnp.dot(y_ref[...], w_ref[:height, :], preferred_element_type=F32)
    yd = load_rows(ins[3:]).astype(BF)
    total = total + jnp.dot(yd, w_ref[height:, :], preferred_element_type=F32)
    for i, out in enumerate(outs):
        out[...] = total[i * rows : (i + 1) * rows].astype(out.dtype)


def owner_body(ins, _, outs, __):
    y, c, _ = place()
    at = lax.broadcasted_iota(jnp.int32, (16, 16), 0)
    source = lax.bitwise_xor(at, (y * 2 + c) * 4)
    turn = (lax.broadcasted_iota(jnp.int32, (16, 16), 1) == source).astype(F32).astype(BF)
    for step in range(2):
        total = ins[step * 4][...]
        for got in ins[step * 4 + 1 : step * 4 + 4]:
            total = total + got[...].astype(F32)
        turned = jnp.dot(turn, total.astype(BF), preferred_element_type=F32)
        for i, out in enumerate(outs):
            out[step] = turned[i * 4 : (i + 1) * 4].astype(BF)


def output_body(ins, _, outs, __):
    y, c, _ = place()
    width = ins[0].shape[2]
    for dy, dc, block in ((0, 0, ins[0]), (0, 1, ins[1]), (1, 0, ins[2]), (1, 1, ins[3])):
        source = lax.bitwise_xor(y, dy) * 2 + lax.bitwise_xor(c, dc)
        outs[0][:, :, pl.ds(pl.multiple_of(source * width, width), width)] = block[...]


def near_plan(sender_rows, counts, assign, gate_w, up_w, down_w):
    steps, slots, width = sender_rows.shape
    width //= 4
    units = gate_w.shape[1] // 4
    rows = MEAN * counts.shape[1]
    part = rows // 4

    def down_rows(dy, token):
        shape = pltpu.VMEM((down_w.shape[0] // 2, down_w.shape[1]), BF)
        scratch = (pltpu.SemaphoreType.DMA((2,)),)
        spec = pl.BlockSpec(memory_space=pl.ANY)
        return run(functools.partial(down_rows_body, dy), (shape,), (down_w,), token, (), scratch, spec=spec)

    y, yd, core, own, token = normed_blocks(sender_rows)
    y, yd = lax.ppermute(y, "row", X2), lax.ppermute(yd, "row", X3)
    core = lax.ppermute(core, "row", X1)
    quarters = {}

    def bring(dy, dc, token):
        w, token = fetch_quarter(gate_w, up_w, dy, dc, token)
        quarters.setdefault((dy, dc), []).append(w)
        return token

    block = like((4 * slots, width))
    near_block, token = run(stack_body, (block,), (own, core), token)
    near_sent = [lax.ppermute(near_block, "col", X3), lax.ppermute(near_block, "col", X1)]
    far_block, token = run(stack_body, (block,), (y, yd), token)
    far_sent = [lax.ppermute(far_block, "col", X3), lax.ppermute(far_block, "col", X1)]
    token = bring(1, 1, token)
    passed, token = run(after_body, (block,), (near_sent[0], near_sent[1]), token)
    near_sent.append(lax.ppermute(passed, "col", X1))
    token = bring(1, 0, token)
    pick, token = run(pick_body, (like((steps * rows, steps * assign.shape[1])),), (counts, assign), token)
    passed, token = run(after_body, (block,), (far_sent[0], far_sent[1]), token)
    far_sent.append(lax.ppermute(passed, "col", X1))
    token = bring(0, 1, token)
    pieces = []
    for dz in range(4):
        for own_block, sent in ((near_block, near_sent), (far_block, far_sent)):
            pieces.append((own_block, sent[1], sent[2], sent[0])[dz])

    bits = (like((steps * rows // PIECES, 2 * units)),) * PIECES
    wide = like((steps * rows, 2 * units), F32)
    batch, *out, token = run(
        first_body,
        (like((steps * rows, width)),) + bits,
        tuple(pieces) + (pick, *quarters[1, 1]),
        token,
        (),
        (pltpu.VMEM((32 * slots, width), BF),),
    )
    cores = tuple(lax.ppermute(o, "row", X1) for o in out)
    own_far, token = run(dot_body, (wide,), (batch, *quarters[1, 0]), token)
    *sends, token = run(far_body, (like((rows, 2 * units)),) * steps, (own_far,) + cores, token)
    gots = [lax.ppermute(send, "row", X2) for send in sends]
    last = pltpu.VMEM((gate_w.shape[0], gate_w.shape[1] // 2), BF)
    *out, last, token = run(
        functools.partial(dot_and_quarter_body, 0, 0),
        bits + (last,),
        (batch, *quarters[0, 1]),
        token,
        (gate_w, up_w),
        (pltpu.SemaphoreType.DMA((2,)),),
    )
    cores = tuple(lax.ppermute(o, "row", X1) for o in out)
    own_near, token = run(dot_body, (wide,), (batch, last), token)
    down_near, token = down_rows(0, token)
    hidden = []

    def activate(step, token):
        each = PIECES // steps
        near = cores[step * each : (step + 1) * each]
        operands = (own_near, gots[step]) + near
        body = functools.partial(hidden_body, step)
        result, token = run(body, (like((rows, units)),), operands, token)
        y = lax.ppermute(result, "row", X2)
        hidden.append((result, lax.ppermute(result, "row", X1), y))
        return token

    def shared(step, token):
        cut = (like((rows // CUTS, units)),) * CUTS
        *passed, token = run(after_body, cut, (hidden[step][2],), token)
        return tuple(lax.ppermute(p, "row", X1) for p in passed), token

    def shared(step, token):
        cut = (like((rows // CUTS, units)),) * CUTS
        *passed, token = run(after_body, cut, (hidden[step][2],), token)
        return tuple(lax.ppermute(p, "row", X1) for p in passed), token

    def down_part(step, token):
        own, core, _ = hidden[step]
        return run(down_part_body, (like((rows, width), F32),), (down_near, own, core), token)

    def down_rest(step, part_sum, yd, token):
        outs = (like((part, width), F32),) + (like((part, width)),) * 3
        operands = (down_far, part_sum, hidden[step][2]) + yd
        keep, send1, send2, send3, token = run(down_rest_body, outs, operands, token)
        sent = ((send3, X3), (send2, X2), (send1, X1))
        return (keep,) + tuple(lax.ppermute(s, "col", x) for s, x in sent), token

    token = activate(0, token)
    down_far, token = down_rows(1, token)
    part0, token = down_part(0, token)
    token = activate(1, token)
    yd0, token = shared(0, token)
    sums0, token = down_rest(0, part0, yd0, token)
    part1, token = down_part(1, token)
    yd1, token = shared(1, token)
    sums1, token = down_rest(1, part1, yd1, token)
    sums = sums0 + sums1
    own, core, y, yd, token = run(owner_body, (like((steps, MEAN, width)),) * 4, tuple(sums), token)
    blocks = (own, lax.ppermute(core, "row", X1), lax.ppermute(y, "row", X2), lax.ppermute(yd, "row", X3))
    result, _ = run(output_body, (like((steps, MEAN, 4 * width)),), blocks, token)
    return result


def layer_block(normed_block, counts_block, assign_block, paired, down_w, hidden_cols):
    row_devices = lax.axis_size("row")
    col_devices = lax.axis_size("col")
    step_count = normed_block.shape[0]
    capacity = normed_block.shape[1]
    rows_step = MEAN * counts_block.shape[1]
    spread = lax.all_to_all(normed_block, "row", split_axis=2, concat_axis=1, tiled=True)
    gathered = lax.all_gather(spread, "col", axis=1, tiled=True)
    slot_count = gathered.shape[1]
    stacked = gathered.reshape(step_count * slot_count, gathered.shape[2])
    targets = (
        assign_block.reshape(step_count, row_devices, col_devices, capacity)
        .transpose(0, 2, 1, 3)
        .reshape(step_count, slot_count)
    )
    holdings = counts_block.reshape(step_count, row_devices, col_devices).transpose(0, 2, 1)
    slot_grid = lax.broadcasted_iota(jnp.int32, (step_count, col_devices, row_devices, capacity), 3)
    live_mask = (slot_grid < holdings[..., None]).reshape(step_count, slot_count)
    targets = jnp.where(live_mask, targets, rows_step)
    slot_ids = lax.broadcasted_iota(jnp.int32, (step_count, slot_count), 1)
    step_ids = lax.broadcasted_iota(jnp.int32, (step_count, slot_count), 0)
    inverse = (
        jnp.zeros((step_count, rows_step), jnp.int32)
        .at[step_ids, targets]
        .set(slot_ids, mode="drop")
    )
    grid_shape = (col_devices, row_devices, step_count, MEAN)
    col_ids = lax.broadcasted_iota(jnp.int32, grid_shape, 0)
    row_ids = lax.broadcasted_iota(jnp.int32, grid_shape, 1)
    step_grid = lax.broadcasted_iota(jnp.int32, grid_shape, 2)
    member = lax.broadcasted_iota(jnp.int32, grid_shape, 3)
    row_numbers = (row_ids * col_devices + col_ids) * MEAN + member
    positions = (step_grid * slot_count + inverse[step_grid, row_numbers]).reshape(-1)
    inputs = jnp.take(stacked, positions, axis=0)
    rows_here = inputs
    gate_up = lax.psum_scatter(
        jnp.dot(rows_here, paired, preferred_element_type=jnp.float32).astype(jnp.bfloat16),
        "row",
        scatter_dimension=0,
        tiled=True,
    ).astype(jnp.float32)
    hidden = (jax.nn.silu(gate_up[:, :hidden_cols]) * gate_up[:, hidden_cols:]).astype(jnp.bfloat16)
    hidden_all = lax.all_gather(hidden, "row", axis=0, tiled=True)
    rows_here = hidden_all
    summed = lax.psum_scatter(
        jnp.dot(rows_here, down_w, preferred_element_type=jnp.float32).astype(jnp.bfloat16),
        "col",
        scatter_dimension=0,
        tiled=True,
    )
    finished = lax.all_to_all(summed, "row", split_axis=0, concat_axis=1, tiled=True)
    return finished.reshape(step_count, MEAN, finished.shape[1])


def any_plan(sender_rows, counts, assign, gate_w, up_w, down_w):
    values = sender_rows.astype(jnp.float32)
    normed = (
        values * lax.rsqrt(jnp.mean(values * values, axis=-1, keepdims=True) + epsilon)
    ).astype(jnp.bfloat16)
    paired = jnp.concatenate((gate_w, up_w), axis=1)
    hidden_cols = gate_w.shape[1]
    outputs = []
    for step_index in range(STEPS):
        outputs.append(
            layer_block(
                normed[step_index : step_index + 1],
                counts[step_index : step_index + 1],
                assign[step_index : step_index + 1],
                paired,
                down_w,
                hidden_cols,
            )
        )
    result = jnp.concatenate(outputs, axis=0)
    return result


def solution(mesh):
    near = mesh.shape["row"] == 4 and mesh.shape["col"] == 4
    return jax.shard_map(
        near_plan if near else any_plan,
        mesh=mesh,
        in_specs=(
            P(None, ("groups", "row", "col"), None),
            P(None, "groups"),
            P(None, "groups"),
            P("row", "col"),
            P("row", "col"),
            P("col", "row"),
        ),
        out_specs=P(None, ("groups", "row", "col"), None),
        check_vma=False,
    )
```

```python
import functools

import jax
import jax.numpy as jnp
from jax import lax
from jax.experimental import pallas as pl
from jax.experimental.pallas import tpu as pltpu
from jax.sharding import PartitionSpec as P

STEPS = 2
MEAN = 4

epsilon = 1e-05

BF = jnp.bfloat16
F32 = jnp.float32
MIB = 2**20
PIECES = 2
CUTS = 2
X1 = ((0, 1), (1, 0), (2, 3), (3, 2))
X2 = ((0, 2), (1, 3), (2, 0), (3, 1))
X3 = ((0, 3), (1, 2), (2, 1), (3, 0))


def place():
    row = lax.axis_index("row")
    return row // 2, lax.rem(row, 2), lax.axis_index("col")


def run(body, outs, operands, token, weights=(), scratch=(), cost=1, spec=None):
    count, held = len(operands), len(weights)
    skip = count + held + (token is not None)
    vmem = pl.BlockSpec(memory_space=pltpu.VMEM)
    outs = tuple(outs) + (like((8, 128), F32),)

    def wrapped(*refs):
        results = refs[skip:]
        body(refs[:count], refs[count : count + held], results[: len(outs) - 1], results[len(outs) :])
        results[len(outs) - 1][...] = jnp.zeros((8, 128), F32)

    return pl.pallas_call(
        wrapped,
        out_shape=outs,
        in_specs=[spec or vmem] * count
        + [pl.BlockSpec(memory_space=pltpu.HBM)] * held
        + [pl.BlockSpec(memory_space=pl.ANY)] * (token is not None),
        out_specs=(vmem,) * len(outs),
        scratch_shapes=scratch,
        compiler_params=pltpu.CompilerParams(vmem_limit_bytes=8 * MIB),
        cost_estimate=pl.CostEstimate(flops=0, bytes_accessed=cost, transcendentals=0),
    )(*operands, *(pltpu.with_memory_space_constraint(w, pltpu.HBM) for w in weights), *(() if token is None else (token,)))


def like(shape, dtype=BF):
    return jax.ShapeDtypeStruct(shape, dtype)


def norm_body(ins, _, outs, __):
    (rows_ref,) = ins
    y, c, _ = place()
    width = outs[0].shape[2]
    for step in range(rows_ref.shape[0]):
        total = jnp.sum(jnp.square(rows_ref[step].astype(F32)), axis=-1, keepdims=True)
        scale = lax.rsqrt(total / rows_ref.shape[2] + epsilon)
        for out, (dy, dc) in zip(outs, ((1, 0), (1, 1), (0, 1), (0, 0))):
            block = lax.bitwise_xor(y, dy) * 2 + lax.bitwise_xor(c, dc)
            at = pl.ds(pl.multiple_of(block * width, width), width)
            out[step] = (rows_ref[step, :, at].astype(F32) * scale).astype(BF)


def normed_blocks(sender_rows):
    steps, slots, width = sender_rows.shape
    return run(norm_body, (like((steps, slots, width // 4)),) * 4, (sender_rows,), None)


def pick_body(ins, _, outs, __):
    counts_ref, assign_ref = ins
    (pick_ref,) = outs
    y, c, z = place()
    rows = pick_ref.shape[0] // 2
    slots = assign_ref.shape[1]
    arrivals = pick_ref.shape[1]
    spread = (
        lax.broadcasted_iota(jnp.int32, (slots // 8, slots), 1) // 8
        == lax.broadcasted_iota(jnp.int32, (slots // 8, slots), 0)
    ).astype(F32)
    held = jnp.dot(counts_ref[...].astype(F32), spread, preferred_element_type=F32)
    slot = lax.rem(lax.broadcasted_iota(jnp.int32, (1, slots), 1), 8).astype(F32)
    at = lax.broadcasted_iota(jnp.int32, (rows, slots), 0)
    target = (lax.rem(at, 16) // 4) * 16 + lax.bitwise_xor(at // 16, z) * 4 + lax.rem(at, 4)
    p = lax.broadcasted_iota(jnp.int32, (slots, arrivals), 1)
    bit = lambda shift: lax.rem(lax.shift_right_logical(p, shift), 2)
    row = lax.bitwise_xor(bit(5), y) * 2 + lax.bitwise_xor(bit(4), c)
    sender = row * 4 + lax.bitwise_xor(lax.shift_right_logical(p, 6), z)
    source = sender * 8 + lax.rem(p, 8)
    entry = lax.broadcasted_iota(jnp.int32, (slots, arrivals), 0)
    for step in range(2):
        live = slot < held[step : step + 1]
        chosen = jnp.where(live, assign_ref[step : step + 1, :], -1)
        placed = (chosen == target).astype(F32).astype(BF)
        moved = ((entry == source) & (bit(3) == step)).astype(F32).astype(BF)
        pick_ref[step * rows : (step + 1) * rows, :] = jnp.dot(
            placed, moved, preferred_element_type=F32
        ).astype(BF)


def quarter_copies(dy, dc, weights, out_ref, sems):
    y, c, _ = place()
    width = out_ref.shape[1] // 2
    start = (lax.bitwise_xor(c, dc) * 2 + lax.bitwise_xor(y, dy)) * width
    at = pl.ds(pl.multiple_of(start, 128), width)
    return [
        pltpu.make_async_copy(w.at[:, at], out_ref.at[:, pl.ds(i * width, width)], sems.at[i])
        for i, w in enumerate(weights)
    ]


def quarter_body(dy, dc, ins, weights, outs, scratch):
    copies = quarter_copies(dy, dc, weights, outs[0], scratch[0])
    for copy in copies:
        copy.start()
    for copy in copies:
        copy.wait()


def dot_and_quarter_body(dy, dc, ins, weights, outs, scratch):
    copies = quarter_copies(dy, dc, weights, outs[-1], scratch[0])
    for copy in copies:
        copy.start()
    x_ref, w_ref = ins
    rows = outs[0].shape[0]

    @pl.loop(0, w_ref.shape[1] // 256)
    def _(i):
        at = pl.ds(pl.multiple_of(i * 256, 256), 256)
        total = jnp.dot(x_ref[...], w_ref[:, at], preferred_element_type=F32).astype(BF)
        for k, out in enumerate(outs[:-1]):
            out[:, at] = total[k * rows : (k + 1) * rows]

    for copy in copies:
        copy.wait()


def fetch_quarter(gate_w, up_w, dy, dc, token):
    shape = pltpu.VMEM((gate_w.shape[0], gate_w.shape[1] // 2), BF)
    return run(
        functools.partial(quarter_body, dy, dc),
        (shape,),
        (),
        token,
        (gate_w, up_w),
        (pltpu.SemaphoreType.DMA((2,)),),
    )


def down_rows_body(dy, ins, _, outs, scratch):
    y, c, _ = place()
    (out_ref,) = outs
    height = out_ref.shape[0] // 2
    copies = []
    for dc in range(2):
        start = (lax.bitwise_xor(c, dc) * 2 + lax.bitwise_xor(y, dy)) * height
        copies.append(
            pltpu.make_async_copy(
                ins[0].at[pl.ds(pl.multiple_of(start, 16), height), :],
                out_ref.at[pl.ds(dc * height, height), :],
                scratch[0].at[dc],
            )
        )
    for copy in copies:
        copy.start()
    for copy in copies:
        copy.wait()


def stack_body(ins, _, outs, __):
    for i, piece in enumerate(ins):
        joined = jnp.concatenate([piece[step].astype(F32) for step in range(2)], axis=0)
        outs[0][i * 16 : (i + 1) * 16, :] = joined.astype(BF)


def after_body(ins, _, outs, __):
    rows = outs[0].shape[0]
    for i, out in enumerate(outs):
        out[...] = ins[0][i * rows : (i + 1) * rows, :]


def halves_dot(x_ref, w_refs):
    total = 0.0
    height = w_refs[0].shape[0]
    for i, w_ref in enumerate(w_refs):
        at = slice(i * height, (i + 1) * height)
        total = total + jnp.dot(x_ref[:, at], w_ref[...], preferred_element_type=F32)
    return total


def store_rows(outs, value):
    rows = outs[0].shape[0]
    for i, out in enumerate(outs):
        out[...] = value[i * rows : (i + 1) * rows].astype(out.dtype)


def load_rows(refs):
    return jnp.concatenate([ref[...].astype(F32) for ref in refs], axis=0)


def first_body(ins, _, outs, scratch):
    pieces, pick_ref, w_refs = ins[:8], ins[8], ins[9:]
    batch_ref, pieces_out = outs[0], outs[1:]
    slots = scratch[0]
    height = pieces[0].shape[0]
    for i, piece in enumerate(pieces):
        slots[i * height : (i + 1) * height, :] = piece[...]
    batch_ref[...] = jnp.dot(pick_ref[...], slots[...], preferred_element_type=F32).astype(BF)
    store_rows(pieces_out, halves_dot(batch_ref, w_refs))


def dot_body(ins, _, outs, __):
    store_rows(outs, halves_dot(ins[0], ins[1:]))


def far_body(ins, _, outs, __):
    store_rows(outs, ins[0][...] + load_rows(ins[1:]))


def hidden_body(step, ins, _, outs, __):
    rows, width = outs[0].shape
    total = ins[0][step * rows : (step + 1) * rows, :] + ins[1][...].astype(F32) + load_rows(ins[2:])
    gate, up = total[:, :width], total[:, width:]
    outs[0][...] = (gate / (1.0 + jnp.exp(-gate)) * up).astype(BF)


def down_part_body(ins, _, outs, __):
    w_ref, own_ref, core_ref = ins
    height = w_ref.shape[0] // 2
    total = jnp.dot(own_ref[...], w_ref[:height, :], preferred_element_type=F32)
    outs[0][...] = total + jnp.dot(core_ref[...], w_ref[height:, :], preferred_element_type=F32)


def down_rest_body(count, ins, _, outs, __):
    w_ref, part_ref, y_ref = ins[:3]
    rows = outs[0].shape[0]
    height = w_ref.shape[0] // 2
    total = part_ref[...] + jnp.dot(y_ref[...], w_ref[:height, :], preferred_element_type=F32)
    yd = load_rows(ins[3 + count :]).astype(BF)
    total = total + jnp.dot(yd, w_ref[height:, :], preferred_element_type=F32)
    for i, out in enumerate(outs[:4]):
        out[...] = total[i * rows : (i + 1) * rows].astype(out.dtype)
    for given, out in zip(ins[3 : 3 + count], outs[4:]):
        out[...] = given[...]


def owner_body(ins, _, outs, __):
    y, c, _ = place()
    at = lax.broadcasted_iota(jnp.int32, (16, 16), 0)
    source = lax.bitwise_xor(at, (y * 2 + c) * 4)
    turn = (lax.broadcasted_iota(jnp.int32, (16, 16), 1) == source).astype(F32).astype(BF)
    for step in range(2):
        total = ins[step * 3][...]
        for got in (ins[step * 3 + 1], ins[step * 3 + 2], ins[7 - step]):
            total = total + got[...].astype(F32)
        turned = jnp.dot(turn, total.astype(BF), preferred_element_type=F32)
        for i, out in enumerate(outs):
            out[step] = turned[i * 4 : (i + 1) * 4].astype(BF)


def output_body(ins, _, outs, __):
    y, c, _ = place()
    width = ins[0].shape[2]
    for dy, dc, block in ((0, 0, ins[0]), (0, 1, ins[1]), (1, 0, ins[2]), (1, 1, ins[3])):
        source = lax.bitwise_xor(y, dy) * 2 + lax.bitwise_xor(c, dc)
        outs[0][:, :, pl.ds(pl.multiple_of(source * width, width), width)] = block[...]


def near_plan(sender_rows, counts, assign, gate_w, up_w, down_w):
    steps, slots, width = sender_rows.shape
    width //= 4
    units = gate_w.shape[1] // 4
    rows = MEAN * counts.shape[1]
    part = rows // 4

    def down_rows(dy, token):
        shape = pltpu.VMEM((down_w.shape[0] // 2, down_w.shape[1]), BF)
        scratch = (pltpu.SemaphoreType.DMA((2,)),)
        spec = pl.BlockSpec(memory_space=pl.ANY)
        return run(functools.partial(down_rows_body, dy), (shape,), (down_w,), token, (), scratch, spec=spec)

    y, yd, core, own, token = normed_blocks(sender_rows)
    y, yd = lax.ppermute(y, "row", X2), lax.ppermute(yd, "row", X3)
    core = lax.ppermute(core, "row", X1)
    quarters = {}

    def bring(dy, dc, token):
        w, token = fetch_quarter(gate_w, up_w, dy, dc, token)
        quarters.setdefault((dy, dc), []).append(w)
        return token

    block = like((4 * slots, width))
    near_block, token = run(stack_body, (block,), (own, core), token)
    near_sent = [lax.ppermute(near_block, "col", X3), lax.ppermute(near_block, "col", X1)]
    far_block, token = run(stack_body, (block,), (y, yd), token)
    far_sent = [lax.ppermute(far_block, "col", X3), lax.ppermute(far_block, "col", X1)]
    token = bring(1, 1, token)
    passed, token = run(after_body, (block,), (near_sent[0], near_sent[1]), token)
    near_sent.append(lax.ppermute(passed, "col", X1))
    token = bring(1, 0, token)
    passed, token = run(after_body, (block,), (far_sent[0], far_sent[1]), token)
    far_sent.append(lax.ppermute(passed, "col", X1))
    pick, token = run(pick_body, (like((steps * rows, steps * assign.shape[1])),), (counts, assign), token)
    token = bring(0, 1, token)
    pieces = []
    for dz in range(4):
        for own_block, sent in ((near_block, near_sent), (far_block, far_sent)):
            pieces.append((own_block, sent[1], sent[2], sent[0])[dz])

    bits = (like((steps * rows // PIECES, 2 * units)),) * PIECES
    wide = like((steps * rows, 2 * units), F32)
    batch, *out, token = run(
        first_body,
        (like((steps * rows, width)),) + bits,
        tuple(pieces) + (pick, *quarters[1, 1]),
        token,
        (),
        (pltpu.VMEM((32 * slots, width), BF),),
    )
    cores = tuple(lax.ppermute(o, "row", X1) for o in out)
    own_far, token = run(dot_body, (wide,), (batch, *quarters[1, 0]), token)
    *sends, token = run(far_body, (like((rows, 2 * units)),) * steps, (own_far,) + cores, token)
    gots = [lax.ppermute(send, "row", X2) for send in sends]
    last = pltpu.VMEM((gate_w.shape[0], gate_w.shape[1] // 2), BF)
    *out, last, token = run(
        functools.partial(dot_and_quarter_body, 0, 0),
        bits + (last,),
        (batch, *quarters[0, 1]),
        token,
        (gate_w, up_w),
        (pltpu.SemaphoreType.DMA((2,)),),
    )
    cores = tuple(lax.ppermute(o, "row", X1) for o in out)
    own_near, token = run(dot_body, (wide,), (batch, last), token)
    down_near, token = down_rows(0, token)
    hidden = []

    def activate(step, token):
        each = PIECES // steps
        near = cores[step * each : (step + 1) * each]
        operands = (own_near, gots[step]) + near
        body = functools.partial(hidden_body, step)
        result, token = run(body, (like((rows, units)),), operands, token)
        y = lax.ppermute(result, "row", X2)
        hidden.append((result, lax.ppermute(result, "row", X1), y))
        return token

    def shared(step, token):
        cut = (like((rows // CUTS, units)),) * CUTS
        *passed, token = run(after_body, cut, (hidden[step][2],), token)
        return tuple(lax.ppermute(p, "row", X1) for p in passed), token

    def shared(step, token):
        cut = (like((rows // CUTS, units)),) * CUTS
        *passed, token = run(after_body, cut, (hidden[step][2],), token)
        return tuple(lax.ppermute(p, "row", X1) for p in passed), token

    def down_part(step, token):
        own, core, _ = hidden[step]
        return run(down_part_body, (like((rows, width), F32),), (down_near, own, core), token)

    def down_rest(step, part_sum, yd, first, token):
        outs = (like((part, width), F32),) + (like((part, width)),) * (3 + len(first))
        operands = (down_far, part_sum, hidden[step][2]) + first + yd
        body = functools.partial(down_rest_body, len(first))
        keep, send1, send2, send3, *passed, token = run(body, outs, operands, token)
        sent = [keep, lax.ppermute(send3, "col", X3), lax.ppermute(send2, "col", X2)]
        return sent, send1, passed, token

    token = activate(0, token)
    down_far, token = down_rows(1, token)
    part0, token = down_part(0, token)
    token = activate(1, token)
    yd0, token = shared(0, token)
    part1, token = down_part(1, token)
    sums0, first, _, token = down_rest(0, part0, yd0, (), token)
    yd1, token = shared(1, token)
    sums1, second, passed, token = down_rest(1, part1, yd1, (first,), token)
    sums = sums0 + sums1 + [lax.ppermute(s, "col", X1) for s in (second, passed[0])]
    own, core, y, yd, token = run(owner_body, (like((steps, MEAN, width)),) * 4, tuple(sums), token)
    blocks = (own, lax.ppermute(core, "row", X1), lax.ppermute(y, "row", X2), lax.ppermute(yd, "row", X3))
    result, _ = run(output_body, (like((steps, MEAN, 4 * width)),), blocks, token)
    return result


def layer_block(normed_block, counts_block, assign_block, paired, down_w, hidden_cols):
    row_devices = lax.axis_size("row")
    col_devices = lax.axis_size("col")
    step_count = normed_block.shape[0]
    capacity = normed_block.shape[1]
    rows_step = MEAN * counts_block.shape[1]
    spread = lax.all_to_all(normed_block, "row", split_axis=2, concat_axis=1, tiled=True)
    gathered = lax.all_gather(spread, "col", axis=1, tiled=True)
    slot_count = gathered.shape[1]
    stacked = gathered.reshape(step_count * slot_count, gathered.shape[2])
    targets = (
        assign_block.reshape(step_count, row_devices, col_devices, capacity)
        .transpose(0, 2, 1, 3)
        .reshape(step_count, slot_count)
    )
    holdings = counts_block.reshape(step_count, row_devices, col_devices).transpose(0, 2, 1)
    slot_grid = lax.broadcasted_iota(jnp.int32, (step_count, col_devices, row_devices, capacity), 3)
    live_mask = (slot_grid < holdings[..., None]).reshape(step_count, slot_count)
    targets = jnp.where(live_mask, targets, rows_step)
    slot_ids = lax.broadcasted_iota(jnp.int32, (step_count, slot_count), 1)
    step_ids = lax.broadcasted_iota(jnp.int32, (step_count, slot_count), 0)
    inverse = (
        jnp.zeros((step_count, rows_step), jnp.int32)
        .at[step_ids, targets]
        .set(slot_ids, mode="drop")
    )
    grid_shape = (col_devices, row_devices, step_count, MEAN)
    col_ids = lax.broadcasted_iota(jnp.int32, grid_shape, 0)
    row_ids = lax.broadcasted_iota(jnp.int32, grid_shape, 1)
    step_grid = lax.broadcasted_iota(jnp.int32, grid_shape, 2)
    member = lax.broadcasted_iota(jnp.int32, grid_shape, 3)
    row_numbers = (row_ids * col_devices + col_ids) * MEAN + member
    positions = (step_grid * slot_count + inverse[step_grid, row_numbers]).reshape(-1)
    inputs = jnp.take(stacked, positions, axis=0)
    rows_here = inputs
    gate_up = lax.psum_scatter(
        jnp.dot(rows_here, paired, preferred_element_type=jnp.float32).astype(jnp.bfloat16),
        "row",
        scatter_dimension=0,
        tiled=True,
    ).astype(jnp.float32)
    hidden = (jax.nn.silu(gate_up[:, :hidden_cols]) * gate_up[:, hidden_cols:]).astype(jnp.bfloat16)
    hidden_all = lax.all_gather(hidden, "row", axis=0, tiled=True)
    rows_here = hidden_all
    summed = lax.psum_scatter(
        jnp.dot(rows_here, down_w, preferred_element_type=jnp.float32).astype(jnp.bfloat16),
        "col",
        scatter_dimension=0,
        tiled=True,
    )
    finished = lax.all_to_all(summed, "row", split_axis=0, concat_axis=1, tiled=True)
    return finished.reshape(step_count, MEAN, finished.shape[1])


def any_plan(sender_rows, counts, assign, gate_w, up_w, down_w):
    values = sender_rows.astype(jnp.float32)
    normed = (
        values * lax.rsqrt(jnp.mean(values * values, axis=-1, keepdims=True) + epsilon)
    ).astype(jnp.bfloat16)
    paired = jnp.concatenate((gate_w, up_w), axis=1)
    hidden_cols = gate_w.shape[1]
    outputs = []
    for step_index in range(STEPS):
        outputs.append(
            layer_block(
                normed[step_index : step_index + 1],
                counts[step_index : step_index + 1],
                assign[step_index : step_index + 1],
                paired,
                down_w,
                hidden_cols,
            )
        )
    result = jnp.concatenate(outputs, axis=0)
    return result


def solution(mesh):
    near = mesh.shape["row"] == 4 and mesh.shape["col"] == 4
    return jax.shard_map(
        near_plan if near else any_plan,
        mesh=mesh,
        in_specs=(
            P(None, ("groups", "row", "col"), None),
            P(None, "groups"),
            P(None, "groups"),
            P("row", "col"),
            P("row", "col"),
            P("col", "row"),
        ),
        out_specs=P(None, ("groups", "row", "col"), None),
        check_vma=False,
    )
```

```python
import functools

import jax
import jax.numpy as jnp
from jax import lax
from jax.experimental import pallas as pl
from jax.experimental.pallas import tpu as pltpu
from jax.sharding import PartitionSpec as P

STEPS = 2
MEAN = 4

epsilon = 1e-05

BF = jnp.bfloat16
F32 = jnp.float32
MIB = 2**20
PIECES = 2
CUTS = 2
X1 = ((0, 1), (1, 0), (2, 3), (3, 2))
X2 = ((0, 2), (1, 3), (2, 0), (3, 1))
X3 = ((0, 3), (1, 2), (2, 1), (3, 0))


def place():
    row = lax.axis_index("row")
    return row // 2, lax.rem(row, 2), lax.axis_index("col")


def run(body, outs, operands, token, weights=(), scratch=(), cost=1, spec=None):
    count, held = len(operands), len(weights)
    skip = count + held + (token is not None)
    vmem = pl.BlockSpec(memory_space=pltpu.VMEM)
    outs = tuple(outs) + (like((8, 128), F32),)

    def wrapped(*refs):
        results = refs[skip:]
        body(refs[:count], refs[count : count + held], results[: len(outs) - 1], results[len(outs) :])
        results[len(outs) - 1][...] = jnp.zeros((8, 128), F32)

    return pl.pallas_call(
        wrapped,
        out_shape=outs,
        in_specs=[spec or vmem] * count
        + [pl.BlockSpec(memory_space=pltpu.HBM)] * held
        + [pl.BlockSpec(memory_space=pl.ANY)] * (token is not None),
        out_specs=(vmem,) * len(outs),
        scratch_shapes=scratch,
        compiler_params=pltpu.CompilerParams(vmem_limit_bytes=8 * MIB),
        cost_estimate=pl.CostEstimate(flops=0, bytes_accessed=cost, transcendentals=0),
    )(*operands, *(pltpu.with_memory_space_constraint(w, pltpu.HBM) for w in weights), *(() if token is None else (token,)))


def like(shape, dtype=BF):
    return jax.ShapeDtypeStruct(shape, dtype)


def norm_body(ins, _, outs, __):
    (rows_ref,) = ins
    y, c, _ = place()
    width = outs[0].shape[2]
    for step in range(rows_ref.shape[0]):
        total = jnp.sum(jnp.square(rows_ref[step].astype(F32)), axis=-1, keepdims=True)
        scale = lax.rsqrt(total / rows_ref.shape[2] + epsilon)
        for out, (dy, dc) in zip(outs, ((1, 0), (1, 1), (0, 1), (0, 0))):
            block = lax.bitwise_xor(y, dy) * 2 + lax.bitwise_xor(c, dc)
            at = pl.ds(pl.multiple_of(block * width, width), width)
            out[step] = (rows_ref[step, :, at].astype(F32) * scale).astype(BF)


def normed_blocks(sender_rows):
    steps, slots, width = sender_rows.shape
    return run(norm_body, (like((steps, slots, width // 4)),) * 4, (sender_rows,), None)


def pick_body(ins, _, outs, __):
    counts_ref, assign_ref = ins
    (pick_ref,) = outs
    y, c, z = place()
    rows = pick_ref.shape[0] // 2
    slots = assign_ref.shape[1]
    arrivals = pick_ref.shape[1]
    spread = (
        lax.broadcasted_iota(jnp.int32, (slots // 8, slots), 1) // 8
        == lax.broadcasted_iota(jnp.int32, (slots // 8, slots), 0)
    ).astype(F32)
    held = jnp.dot(counts_ref[...].astype(F32), spread, preferred_element_type=F32)
    slot = lax.rem(lax.broadcasted_iota(jnp.int32, (1, slots), 1), 8).astype(F32)
    at = lax.broadcasted_iota(jnp.int32, (rows, slots), 0)
    target = (lax.rem(at, 16) // 4) * 16 + lax.bitwise_xor(at // 16, z) * 4 + lax.rem(at, 4)
    p = lax.broadcasted_iota(jnp.int32, (slots, arrivals), 1)
    bit = lambda shift: lax.rem(lax.shift_right_logical(p, shift), 2)
    row = lax.bitwise_xor(bit(5), y) * 2 + lax.bitwise_xor(bit(4), c)
    sender = row * 4 + lax.bitwise_xor(lax.shift_right_logical(p, 6), z)
    source = sender * 8 + lax.rem(p, 8)
    entry = lax.broadcasted_iota(jnp.int32, (slots, arrivals), 0)
    for step in range(2):
        live = slot < held[step : step + 1]
        chosen = jnp.where(live, assign_ref[step : step + 1, :], -1)
        placed = (chosen == target).astype(F32).astype(BF)
        moved = ((entry == source) & (bit(3) == step)).astype(F32).astype(BF)
        pick_ref[step * rows : (step + 1) * rows, :] = jnp.dot(
            placed, moved, preferred_element_type=F32
        ).astype(BF)


def quarter_copies(dy, dc, weights, out_ref, sems):
    y, c, _ = place()
    width = out_ref.shape[1] // 2
    start = (lax.bitwise_xor(c, dc) * 2 + lax.bitwise_xor(y, dy)) * width
    at = pl.ds(pl.multiple_of(start, 128), width)
    return [
        pltpu.make_async_copy(w.at[:, at], out_ref.at[:, pl.ds(i * width, width)], sems.at[i])
        for i, w in enumerate(weights)
    ]


def quarter_body(dy, dc, ins, weights, outs, scratch):
    copies = quarter_copies(dy, dc, weights, outs[0], scratch[0])
    for copy in copies:
        copy.start()
    for copy in copies:
        copy.wait()


def dot_and_quarter_body(dy, dc, ins, weights, outs, scratch):
    copies = quarter_copies(dy, dc, weights, outs[-1], scratch[0])
    for copy in copies:
        copy.start()
    x_ref, w_ref = ins
    rows = outs[0].shape[0]

    @pl.loop(0, w_ref.shape[1] // 256)
    def _(i):
        at = pl.ds(pl.multiple_of(i * 256, 256), 256)
        total = jnp.dot(x_ref[...], w_ref[:, at], preferred_element_type=F32).astype(BF)
        for k, out in enumerate(outs[:-1]):
            out[:, at] = total[k * rows : (k + 1) * rows]

    for copy in copies:
        copy.wait()


def fetch_quarter(gate_w, up_w, dy, dc, token):
    shape = pltpu.VMEM((gate_w.shape[0], gate_w.shape[1] // 2), BF)
    return run(
        functools.partial(quarter_body, dy, dc),
        (shape,),
        (),
        token,
        (gate_w, up_w),
        (pltpu.SemaphoreType.DMA((2,)),),
    )


def down_rows_body(dy, ins, _, outs, scratch):
    y, c, _ = place()
    (out_ref,) = outs
    height = out_ref.shape[0] // 2
    copies = []
    for dc in range(2):
        start = (lax.bitwise_xor(c, dc) * 2 + lax.bitwise_xor(y, dy)) * height
        copies.append(
            pltpu.make_async_copy(
                ins[0].at[pl.ds(pl.multiple_of(start, 16), height), :],
                out_ref.at[pl.ds(dc * height, height), :],
                scratch[0].at[dc],
            )
        )
    for copy in copies:
        copy.start()
    for copy in copies:
        copy.wait()


def stack_body(ins, _, outs, __):
    for i, piece in enumerate(ins):
        joined = jnp.concatenate([piece[step].astype(F32) for step in range(2)], axis=0)
        outs[0][i * 16 : (i + 1) * 16, :] = joined.astype(BF)


def after_body(ins, _, outs, __):
    rows = outs[0].shape[0]
    for i, out in enumerate(outs):
        out[...] = ins[0][i * rows : (i + 1) * rows, :]


def two_body(ins, _, outs, __):
    for x, out in zip(ins, outs):
        out[...] = x[...]


def halves_dot(x_ref, w_refs):
    total = 0.0
    height = w_refs[0].shape[0]
    for i, w_ref in enumerate(w_refs):
        at = slice(i * height, (i + 1) * height)
        total = total + jnp.dot(x_ref[:, at], w_ref[...], preferred_element_type=F32)
    return total


def store_rows(outs, value):
    rows = outs[0].shape[0]
    for i, out in enumerate(outs):
        out[...] = value[i * rows : (i + 1) * rows].astype(out.dtype)


def load_rows(refs):
    return jnp.concatenate([ref[...].astype(F32) for ref in refs], axis=0)


def first_body(ins, _, outs, scratch):
    pieces, pick_ref, w_refs = ins[:8], ins[8], ins[9:]
    batch_ref, pieces_out = outs[0], outs[1:]
    slots = scratch[0]
    height = pieces[0].shape[0]
    for i, piece in enumerate(pieces):
        slots[i * height : (i + 1) * height, :] = piece[...]
    batch_ref[...] = jnp.dot(pick_ref[...], slots[...], preferred_element_type=F32).astype(BF)
    store_rows(pieces_out, halves_dot(batch_ref, w_refs))


def dot_body(ins, _, outs, __):
    store_rows(outs, halves_dot(ins[0], ins[1:]))


def far_body(ins, _, outs, __):
    store_rows(outs, ins[0][...] + load_rows(ins[1:]))


def hidden_body(step, ins, _, outs, __):
    rows, width = outs[0].shape
    total = ins[0][step * rows : (step + 1) * rows, :] + ins[1][...].astype(F32) + load_rows(ins[2:])
    gate, up = total[:, :width], total[:, width:]
    outs[0][...] = (gate / (1.0 + jnp.exp(-gate)) * up).astype(BF)


def down_part_body(ins, _, outs, __):
    w_ref, own_ref, core_ref = ins
    height = w_ref.shape[0] // 2
    total = jnp.dot(own_ref[...], w_ref[:height, :], preferred_element_type=F32)
    outs[0][...] = total + jnp.dot(core_ref[...], w_ref[height:, :], preferred_element_type=F32)


def down_rest_body(count, ins, _, outs, __):
    w_ref, part_ref, y_ref = ins[:3]
    rows = outs[0].shape[0]
    height = w_ref.shape[0] // 2
    total = part_ref[...] + jnp.dot(y_ref[...], w_ref[:height, :], preferred_element_type=F32)
    yd = load_rows(ins[3 + count :]).astype(BF)
    total = total + jnp.dot(yd, w_ref[height:, :], preferred_element_type=F32)
    for i, out in enumerate(outs[:4]):
        out[...] = total[i * rows : (i + 1) * rows].astype(out.dtype)
    for given, out in zip(ins[3 : 3 + count], outs[4:]):
        out[...] = given[...]


def owner_body(ins, _, outs, __):
    y, c, _ = place()
    at = lax.broadcasted_iota(jnp.int32, (16, 16), 0)
    source = lax.bitwise_xor(at, (y * 2 + c) * 4)
    turn = (lax.broadcasted_iota(jnp.int32, (16, 16), 1) == source).astype(F32).astype(BF)
    for step in range(2):
        total = ins[step * 3][...]
        for got in (ins[step * 3 + 1], ins[step * 3 + 2], ins[7 - step]):
            total = total + got[...].astype(F32)
        turned = jnp.dot(turn, total.astype(BF), preferred_element_type=F32)
        for i, out in enumerate(outs):
            out[step] = turned[i * 4 : (i + 1) * 4].astype(BF)


def output_body(ins, _, outs, __):
    y, c, _ = place()
    width = ins[0].shape[2]
    for dy, dc, block in ((0, 0, ins[0]), (0, 1, ins[1]), (1, 0, ins[2]), (1, 1, ins[3])):
        source = lax.bitwise_xor(y, dy) * 2 + lax.bitwise_xor(c, dc)
        outs[0][:, :, pl.ds(pl.multiple_of(source * width, width), width)] = block[...]


def near_plan(sender_rows, counts, assign, gate_w, up_w, down_w):
    steps, slots, width = sender_rows.shape
    width //= 4
    units = gate_w.shape[1] // 4
    rows = MEAN * counts.shape[1]
    part = rows // 4

    def down_rows(dy, token):
        shape = pltpu.VMEM((down_w.shape[0] // 2, down_w.shape[1]), BF)
        scratch = (pltpu.SemaphoreType.DMA((2,)),)
        spec = pl.BlockSpec(memory_space=pl.ANY)
        return run(functools.partial(down_rows_body, dy), (shape,), (down_w,), token, (), scratch, spec=spec)

    y, yd, core, own, token = normed_blocks(sender_rows)
    y, yd = lax.ppermute(y, "row", X2), lax.ppermute(yd, "row", X3)
    core = lax.ppermute(core, "row", X1)
    quarters = {}

    def bring(dy, dc, token):
        w, token = fetch_quarter(gate_w, up_w, dy, dc, token)
        quarters.setdefault((dy, dc), []).append(w)
        return token

    block = like((4 * slots, width))
    near_block, token = run(stack_body, (block,), (own, core), token)
    near_sent = [lax.ppermute(near_block, "col", X3), lax.ppermute(near_block, "col", X1)]
    pick, token = run(pick_body, (like((steps * rows, steps * assign.shape[1])),), (counts, assign), token)
    far_block, token = run(stack_body, (block,), (y, yd), token)
    far_sent = [lax.ppermute(far_block, "col", X3)]
    token = bring(1, 1, token)
    passed, late, token = run(two_body, (block, block), (near_sent[0], far_block, near_sent[1]), token)
    near_sent.append(lax.ppermute(passed, "col", X1))
    far_sent.append(lax.ppermute(late, "col", X1))
    token = bring(1, 0, token)
    passed, token = run(after_body, (block,), (far_sent[0],), token)
    far_sent.append(lax.ppermute(passed, "col", X1))
    token = bring(0, 1, token)
    pieces = []
    for dz in range(4):
        for own_block, sent in ((near_block, near_sent), (far_block, far_sent)):
            pieces.append((own_block, sent[1], sent[2], sent[0])[dz])

    bits = (like((steps * rows // PIECES, 2 * units)),) * PIECES
    wide = like((steps * rows, 2 * units), F32)
    batch, *out, token = run(
        first_body,
        (like((steps * rows, width)),) + bits,
        tuple(pieces) + (pick, *quarters[1, 1]),
        token,
        (),
        (pltpu.VMEM((32 * slots, width), BF),),
    )
    cores = tuple(lax.ppermute(o, "row", X1) for o in out)
    own_far, token = run(dot_body, (wide,), (batch, *quarters[1, 0]), token)
    *sends, token = run(far_body, (like((rows, 2 * units)),) * steps, (own_far,) + cores, token)
    gots = [lax.ppermute(send, "row", X2) for send in sends]
    last = pltpu.VMEM((gate_w.shape[0], gate_w.shape[1] // 2), BF)
    *out, last, token = run(
        functools.partial(dot_and_quarter_body, 0, 0),
        bits + (last,),
        (batch, *quarters[0, 1]),
        token,
        (gate_w, up_w),
        (pltpu.SemaphoreType.DMA((2,)),),
    )
    cores = tuple(lax.ppermute(o, "row", X1) for o in out)
    own_near, token = run(dot_body, (wide,), (batch, last), token)
    down_near, token = down_rows(0, token)
    hidden = []

    def activate(step, token):
        each = PIECES // steps
        near = cores[step * each : (step + 1) * each]
        operands = (own_near, gots[step]) + near
        body = functools.partial(hidden_body, step)
        result, token = run(body, (like((rows, units)),), operands, token)
        y = lax.ppermute(result, "row", X2)
        hidden.append((result, lax.ppermute(result, "row", X1), y))
        return token

    def shared(step, token):
        cut = (like((rows // CUTS, units)),) * CUTS
        *passed, token = run(after_body, cut, (hidden[step][2],), token)
        return tuple(lax.ppermute(p, "row", X1) for p in passed), token

    def shared(step, token):
        cut = (like((rows // CUTS, units)),) * CUTS
        *passed, token = run(after_body, cut, (hidden[step][2],), token)
        return tuple(lax.ppermute(p, "row", X1) for p in passed), token

    def down_part(step, token):
        own, core, _ = hidden[step]
        return run(down_part_body, (like((rows, width), F32),), (down_near, own, core), token)

    def down_rest(step, part_sum, yd, first, token):
        outs = (like((part, width), F32),) + (like((part, width)),) * (3 + len(first))
        operands = (down_far, part_sum, hidden[step][2]) + first + yd
        body = functools.partial(down_rest_body, len(first))
        keep, send1, send2, send3, *passed, token = run(body, outs, operands, token)
        sent = [keep, lax.ppermute(send3, "col", X3), lax.ppermute(send2, "col", X2)]
        return sent, send1, passed, token

    token = activate(0, token)
    down_far, token = down_rows(1, token)
    part0, token = down_part(0, token)
    token = activate(1, token)
    yd0, token = shared(0, token)
    part1, token = down_part(1, token)
    sums0, first, _, token = down_rest(0, part0, yd0, (), token)
    yd1, token = shared(1, token)
    sums1, second, passed, token = down_rest(1, part1, yd1, (first,), token)
    sums = sums0 + sums1 + [lax.ppermute(s, "col", X1) for s in (second, passed[0])]
    own, core, y, yd, token = run(owner_body, (like((steps, MEAN, width)),) * 4, tuple(sums), token)
    blocks = (own, lax.ppermute(core, "row", X1), lax.ppermute(y, "row", X2), lax.ppermute(yd, "row", X3))
    result, _ = run(output_body, (like((steps, MEAN, 4 * width)),), blocks, token)
    return result


def layer_block(normed_block, counts_block, assign_block, paired, down_w, hidden_cols):
    row_devices = lax.axis_size("row")
    col_devices = lax.axis_size("col")
    step_count = normed_block.shape[0]
    capacity = normed_block.shape[1]
    rows_step = MEAN * counts_block.shape[1]
    spread = lax.all_to_all(normed_block, "row", split_axis=2, concat_axis=1, tiled=True)
    gathered = lax.all_gather(spread, "col", axis=1, tiled=True)
    slot_count = gathered.shape[1]
    stacked = gathered.reshape(step_count * slot_count, gathered.shape[2])
    targets = (
        assign_block.reshape(step_count, row_devices, col_devices, capacity)
        .transpose(0, 2, 1, 3)
        .reshape(step_count, slot_count)
    )
    holdings = counts_block.reshape(step_count, row_devices, col_devices).transpose(0, 2, 1)
    slot_grid = lax.broadcasted_iota(jnp.int32, (step_count, col_devices, row_devices, capacity), 3)
    live_mask = (slot_grid < holdings[..., None]).reshape(step_count, slot_count)
    targets = jnp.where(live_mask, targets, rows_step)
    slot_ids = lax.broadcasted_iota(jnp.int32, (step_count, slot_count), 1)
    step_ids = lax.broadcasted_iota(jnp.int32, (step_count, slot_count), 0)
    inverse = (
        jnp.zeros((step_count, rows_step), jnp.int32)
        .at[step_ids, targets]
        .set(slot_ids, mode="drop")
    )
    grid_shape = (col_devices, row_devices, step_count, MEAN)
    col_ids = lax.broadcasted_iota(jnp.int32, grid_shape, 0)
    row_ids = lax.broadcasted_iota(jnp.int32, grid_shape, 1)
    step_grid = lax.broadcasted_iota(jnp.int32, grid_shape, 2)
    member = lax.broadcasted_iota(jnp.int32, grid_shape, 3)
    row_numbers = (row_ids * col_devices + col_ids) * MEAN + member
    positions = (step_grid * slot_count + inverse[step_grid, row_numbers]).reshape(-1)
    inputs = jnp.take(stacked, positions, axis=0)
    rows_here = inputs
    gate_up = lax.psum_scatter(
        jnp.dot(rows_here, paired, preferred_element_type=jnp.float32).astype(jnp.bfloat16),
        "row",
        scatter_dimension=0,
        tiled=True,
    ).astype(jnp.float32)
    hidden = (jax.nn.silu(gate_up[:, :hidden_cols]) * gate_up[:, hidden_cols:]).astype(jnp.bfloat16)
    hidden_all = lax.all_gather(hidden, "row", axis=0, tiled=True)
    rows_here = hidden_all
    summed = lax.psum_scatter(
        jnp.dot(rows_here, down_w, preferred_element_type=jnp.float32).astype(jnp.bfloat16),
        "col",
        scatter_dimension=0,
        tiled=True,
    )
    finished = lax.all_to_all(summed, "row", split_axis=0, concat_axis=1, tiled=True)
    return finished.reshape(step_count, MEAN, finished.shape[1])


def any_plan(sender_rows, counts, assign, gate_w, up_w, down_w):
    values = sender_rows.astype(jnp.float32)
    normed = (
        values * lax.rsqrt(jnp.mean(values * values, axis=-1, keepdims=True) + epsilon)
    ).astype(jnp.bfloat16)
    paired = jnp.concatenate((gate_w, up_w), axis=1)
    hidden_cols = gate_w.shape[1]
    outputs = []
    for step_index in range(STEPS):
        outputs.append(
            layer_block(
                normed[step_index : step_index + 1],
                counts[step_index : step_index + 1],
                assign[step_index : step_index + 1],
                paired,
                down_w,
                hidden_cols,
            )
        )
    result = jnp.concatenate(outputs, axis=0)
    return result


def solution(mesh):
    near = mesh.shape["row"] == 4 and mesh.shape["col"] == 4
    return jax.shard_map(
        near_plan if near else any_plan,
        mesh=mesh,
        in_specs=(
            P(None, ("groups", "row", "col"), None),
            P(None, "groups"),
            P(None, "groups"),
            P("row", "col"),
            P("row", "col"),
            P("col", "row"),
        ),
        out_specs=P(None, ("groups", "row", "col"), None),
        check_vma=False,
    )
```

```python
import functools

import jax
import jax.numpy as jnp
from jax import lax
from jax.experimental import pallas as pl
from jax.experimental.pallas import tpu as pltpu
from jax.sharding import PartitionSpec as P

STEPS = 2
MEAN = 4

epsilon = 1e-05

BF = jnp.bfloat16
F32 = jnp.float32
MIB = 2**20
PIECES = 2
ARRIVAL = (0, 1, 2, 3, 6, 7, 5, 4)
CUTS = 2
X1 = ((0, 1), (1, 0), (2, 3), (3, 2))
X2 = ((0, 2), (1, 3), (2, 0), (3, 1))
X3 = ((0, 3), (1, 2), (2, 1), (3, 0))


def place():
    row = lax.axis_index("row")
    return row // 2, lax.rem(row, 2), lax.axis_index("col")


def run(body, outs, operands, token, weights=(), scratch=(), cost=1, spec=None):
    count, held = len(operands), len(weights)
    skip = count + held + (token is not None)
    vmem = pl.BlockSpec(memory_space=pltpu.VMEM)
    outs = tuple(outs) + (like((8, 128), F32),)

    def wrapped(*refs):
        results = refs[skip:]
        body(refs[:count], refs[count : count + held], results[: len(outs) - 1], results[len(outs) :])
        results[len(outs) - 1][...] = jnp.zeros((8, 128), F32)

    return pl.pallas_call(
        wrapped,
        out_shape=outs,
        in_specs=[spec or vmem] * count
        + [pl.BlockSpec(memory_space=pltpu.HBM)] * held
        + [pl.BlockSpec(memory_space=pl.ANY)] * (token is not None),
        out_specs=(vmem,) * len(outs),
        scratch_shapes=scratch,
        compiler_params=pltpu.CompilerParams(vmem_limit_bytes=8 * MIB),
        cost_estimate=pl.CostEstimate(flops=0, bytes_accessed=cost, transcendentals=0),
    )(*operands, *(pltpu.with_memory_space_constraint(w, pltpu.HBM) for w in weights), *(() if token is None else (token,)))


def like(shape, dtype=BF):
    return jax.ShapeDtypeStruct(shape, dtype)


def norm_body(ins, _, outs, __):
    (rows_ref,) = ins
    y, c, _ = place()
    width = outs[0].shape[2]
    for step in range(rows_ref.shape[0]):
        total = jnp.sum(jnp.square(rows_ref[step].astype(F32)), axis=-1, keepdims=True)
        scale = lax.rsqrt(total / rows_ref.shape[2] + epsilon)
        for out, (dy, dc) in zip(outs, ((1, 0), (1, 1), (0, 1), (0, 0))):
            block = lax.bitwise_xor(y, dy) * 2 + lax.bitwise_xor(c, dc)
            at = pl.ds(pl.multiple_of(block * width, width), width)
            out[step] = (rows_ref[step, :, at].astype(F32) * scale).astype(BF)


def normed_blocks(sender_rows):
    steps, slots, width = sender_rows.shape
    return run(norm_body, (like((steps, slots, width // 4)),) * 4, (sender_rows,), None)


def pick_body(ins, _, outs, __):
    counts_ref, assign_ref = ins[:2]
    (pick_ref,) = outs
    y, c, z = place()
    rows = pick_ref.shape[0] // 2
    slots = assign_ref.shape[1]
    arrivals = pick_ref.shape[1]
    spread = (
        lax.broadcasted_iota(jnp.int32, (slots // 8, slots), 1) // 8
        == lax.broadcasted_iota(jnp.int32, (slots // 8, slots), 0)
    ).astype(F32)
    held = jnp.dot(counts_ref[...].astype(F32), spread, preferred_element_type=F32)
    slot = lax.rem(lax.broadcasted_iota(jnp.int32, (1, slots), 1), 8).astype(F32)
    at = lax.broadcasted_iota(jnp.int32, (rows, slots), 0)
    target = (lax.rem(at, 16) // 4) * 16 + lax.bitwise_xor(at // 16, z) * 4 + lax.rem(at, 4)
    p = lax.broadcasted_iota(jnp.int32, (slots, arrivals), 1)
    bit = lambda shift: lax.rem(lax.shift_right_logical(p, shift), 2)
    row = lax.bitwise_xor(bit(5), y) * 2 + lax.bitwise_xor(bit(4), c)
    sender = row * 4 + lax.bitwise_xor(lax.shift_right_logical(p, 6), z)
    source = sender * 8 + lax.rem(p, 8)
    entry = lax.broadcasted_iota(jnp.int32, (slots, arrivals), 0)
    for step in range(2):
        live = slot < held[step : step + 1]
        chosen = jnp.where(live, assign_ref[step : step + 1, :], -1)
        placed = (chosen == target).astype(F32).astype(BF)
        moved = ((entry == source) & (bit(3) == step)).astype(F32).astype(BF)
        pick_ref[step * rows : (step + 1) * rows, :] = jnp.dot(
            placed, moved, preferred_element_type=F32
        ).astype(BF)


def quarter_copies(dy, dc, weights, out_ref, sems):
    y, c, _ = place()
    width = out_ref.shape[1] // 2
    start = (lax.bitwise_xor(c, dc) * 2 + lax.bitwise_xor(y, dy)) * width
    at = pl.ds(pl.multiple_of(start, 128), width)
    return [
        pltpu.make_async_copy(w.at[:, at], out_ref.at[:, pl.ds(i * width, width)], sems.at[i])
        for i, w in enumerate(weights)
    ]


def quarter_body(dy, dc, ins, weights, outs, scratch):
    copies = quarter_copies(dy, dc, weights, outs[0], scratch[0])
    for copy in copies:
        copy.start()
    for copy in copies:
        copy.wait()


def dot_and_quarter_body(dy, dc, ins, weights, outs, scratch):
    copies = quarter_copies(dy, dc, weights, outs[-1], scratch[0])
    for copy in copies:
        copy.start()
    x_ref, w_ref = ins
    rows = outs[0].shape[0]

    @pl.loop(0, w_ref.shape[1] // 256)
    def _(i):
        at = pl.ds(pl.multiple_of(i * 256, 256), 256)
        total = jnp.dot(x_ref[...], w_ref[:, at], preferred_element_type=F32).astype(BF)
        for k, out in enumerate(outs[:-1]):
            out[:, at] = total[k * rows : (k + 1) * rows]

    for copy in copies:
        copy.wait()


def fetch_quarter(gate_w, up_w, dy, dc, token):
    shape = pltpu.VMEM((gate_w.shape[0], gate_w.shape[1] // 2), BF)
    return run(
        functools.partial(quarter_body, dy, dc),
        (shape,),
        (),
        token,
        (gate_w, up_w),
        (pltpu.SemaphoreType.DMA((2,)),),
    )


def down_rows_body(dy, ins, _, outs, scratch):
    y, c, _ = place()
    (out_ref,) = outs
    height = out_ref.shape[0] // 2
    copies = []
    for dc in range(2):
        start = (lax.bitwise_xor(c, dc) * 2 + lax.bitwise_xor(y, dy)) * height
        copies.append(
            pltpu.make_async_copy(
                ins[0].at[pl.ds(pl.multiple_of(start, 16), height), :],
                out_ref.at[pl.ds(dc * height, height), :],
                scratch[0].at[dc],
            )
        )
    for copy in copies:
        copy.start()
    for copy in copies:
        copy.wait()


def stack_body(ins, _, outs, __):
    for i, piece in enumerate(ins):
        joined = jnp.concatenate([piece[step].astype(F32) for step in range(2)], axis=0)
        outs[0][i * 16 : (i + 1) * 16, :] = joined.astype(BF)


def after_body(ins, _, outs, __):
    rows = outs[0].shape[0]
    for i, out in enumerate(outs):
        out[...] = ins[0][i * rows : (i + 1) * rows, :]


def halves_dot(x_ref, w_refs):
    total = 0.0
    height = w_refs[0].shape[0]
    for i, w_ref in enumerate(w_refs):
        at = slice(i * height, (i + 1) * height)
        total = total + jnp.dot(x_ref[:, at], w_ref[...], preferred_element_type=F32)
    return total


def store_rows(outs, value):
    rows = outs[0].shape[0]
    for i, out in enumerate(outs):
        out[...] = value[i * rows : (i + 1) * rows].astype(out.dtype)


def load_rows(refs):
    return jnp.concatenate([ref[...].astype(F32) for ref in refs], axis=0)


def first_body(ins, _, outs, scratch):
    pieces, pick_ref, w_refs = ins[:8], ins[8], ins[9:]
    batch_ref, pieces_out = outs[0], outs[1:]
    slots = scratch[0]
    height = pieces[0].shape[0]
    for i, piece in zip(ARRIVAL, pieces):
        slots[i * height : (i + 1) * height, :] = piece[...]
    batch_ref[...] = jnp.dot(pick_ref[...], slots[...], preferred_element_type=F32).astype(BF)
    store_rows(pieces_out, halves_dot(batch_ref, w_refs))


def dot_body(ins, _, outs, __):
    store_rows(outs, halves_dot(ins[0], ins[1:]))


def far_body(ins, _, outs, __):
    store_rows(outs, ins[0][...] + load_rows(ins[1:]))


def hidden_body(step, ins, _, outs, __):
    rows, width = outs[0].shape
    total = ins[0][step * rows : (step + 1) * rows, :] + ins[1][...].astype(F32) + load_rows(ins[2:])
    gate, up = total[:, :width], total[:, width:]
    outs[0][...] = (gate / (1.0 + jnp.exp(-gate)) * up).astype(BF)


def down_part_body(ins, _, outs, __):
    w_ref, own_ref, core_ref = ins
    height = w_ref.shape[0] // 2
    total = jnp.dot(own_ref[...], w_ref[:height, :], preferred_element_type=F32)
    outs[0][...] = total + jnp.dot(core_ref[...], w_ref[height:, :], preferred_element_type=F32)


def down_rest_body(count, ins, _, outs, __):
    w_ref, part_ref, y_ref = ins[:3]
    rows = outs[0].shape[0]
    height = w_ref.shape[0] // 2
    total = part_ref[...] + jnp.dot(y_ref[...], w_ref[:height, :], preferred_element_type=F32)
    yd = load_rows(ins[3 + count :]).astype(BF)
    total = total + jnp.dot(yd, w_ref[height:, :], preferred_element_type=F32)
    for i, out in enumerate(outs[:4]):
        out[...] = total[i * rows : (i + 1) * rows].astype(out.dtype)
    for given, out in zip(ins[3 : 3 + count], outs[4:]):
        out[...] = given[...]


def owner_body(ins, _, outs, __):
    y, c, _ = place()
    at = lax.broadcasted_iota(jnp.int32, (16, 16), 0)
    source = lax.bitwise_xor(at, (y * 2 + c) * 4)
    turn = (lax.broadcasted_iota(jnp.int32, (16, 16), 1) == source).astype(F32).astype(BF)
    for step in range(2):
        total = ins[step * 3][...]
        for got in (ins[step * 3 + 1], ins[step * 3 + 2], ins[7 - step]):
            total = total + got[...].astype(F32)
        turned = jnp.dot(turn, total.astype(BF), preferred_element_type=F32)
        for i, out in enumerate(outs):
            out[step] = turned[i * 4 : (i + 1) * 4].astype(BF)


def output_body(ins, _, outs, __):
    y, c, _ = place()
    width = ins[0].shape[2]
    for dy, dc, block in ((0, 0, ins[0]), (0, 1, ins[1]), (1, 0, ins[2]), (1, 1, ins[3])):
        source = lax.bitwise_xor(y, dy) * 2 + lax.bitwise_xor(c, dc)
        outs[0][:, :, pl.ds(pl.multiple_of(source * width, width), width)] = block[...]


def near_plan(sender_rows, counts, assign, gate_w, up_w, down_w):
    steps, slots, width = sender_rows.shape
    width //= 4
    units = gate_w.shape[1] // 4
    rows = MEAN * counts.shape[1]
    part = rows // 4

    def down_rows(dy, token):
        shape = pltpu.VMEM((down_w.shape[0] // 2, down_w.shape[1]), BF)
        scratch = (pltpu.SemaphoreType.DMA((2,)),)
        spec = pl.BlockSpec(memory_space=pl.ANY)
        return run(functools.partial(down_rows_body, dy), (shape,), (down_w,), token, (), scratch, spec=spec)

    y, yd, core, own, token = normed_blocks(sender_rows)
    y, yd = lax.ppermute(y, "row", X2), lax.ppermute(yd, "row", X3)
    core = lax.ppermute(core, "row", X1)
    quarters = {}

    def bring(dy, dc, token):
        w, token = fetch_quarter(gate_w, up_w, dy, dc, token)
        quarters.setdefault((dy, dc), []).append(w)
        return token

    block = like((4 * slots, width))
    near_block, token = run(stack_body, (block,), (own, core), token)
    near_sent = [lax.ppermute(near_block, "col", X3), lax.ppermute(near_block, "col", X1)]
    far_block, token = run(stack_body, (block,), (y, yd), token)
    far_sent = [lax.ppermute(far_block, "col", pairs) for pairs in (X3, X1, X2)]
    token = bring(1, 1, token)
    passed, token = run(after_body, (block,), (near_sent[0], near_sent[1]), token)
    near_sent.append(lax.ppermute(passed, "col", X1))
    token = bring(1, 0, token)
    pick, token = run(
        pick_body, (like((steps * rows, steps * assign.shape[1])),), (counts, assign), token
    )
    token = bring(0, 1, token)
    pieces = []
    for dz in range(4):
        for own_block, sent in ((near_block, near_sent), (far_block, far_sent)):
            pieces.append((own_block, sent[1], sent[2], sent[0])[dz])
    pieces = [pieces[i] for i in ARRIVAL]

    bits = (like((steps * rows // PIECES, 2 * units)),) * PIECES
    wide = like((steps * rows, 2 * units), F32)
    batch, *out, token = run(
        first_body,
        (like((steps * rows, width)),) + bits,
        tuple(pieces) + (pick, *quarters[1, 1]),
        token,
        (),
        (pltpu.VMEM((32 * slots, width), BF),),
    )
    cores = tuple(lax.ppermute(o, "row", X1) for o in out)
    own_far, token = run(dot_body, (wide,), (batch, *quarters[1, 0]), token)
    *sends, token = run(far_body, (like((rows, 2 * units)),) * steps, (own_far,) + cores, token)
    gots = [lax.ppermute(send, "row", X2) for send in sends]
    last = pltpu.VMEM((gate_w.shape[0], gate_w.shape[1] // 2), BF)
    *out, last, token = run(
        functools.partial(dot_and_quarter_body, 0, 0),
        bits + (last,),
        (batch, *quarters[0, 1]),
        token,
        (gate_w, up_w),
        (pltpu.SemaphoreType.DMA((2,)),),
    )
    cores = tuple(lax.ppermute(o, "row", X1) for o in out)
    own_near, token = run(dot_body, (wide,), (batch, last), token)
    down_near, token = down_rows(0, token)
    hidden = []

    def activate(step, token):
        each = PIECES // steps
        near = cores[step * each : (step + 1) * each]
        operands = (own_near, gots[step]) + near
        body = functools.partial(hidden_body, step)
        result, token = run(body, (like((rows, units)),), operands, token)
        y = lax.ppermute(result, "row", X2)
        hidden.append((result, lax.ppermute(result, "row", X1), y))
        return token

    def shared(step, token):
        cut = (like((rows // CUTS, units)),) * CUTS
        *passed, token = run(after_body, cut, (hidden[step][2],), token)
        return tuple(lax.ppermute(p, "row", X1) for p in passed), token

    def shared(step, token):
        cut = (like((rows // CUTS, units)),) * CUTS
        *passed, token = run(after_body, cut, (hidden[step][2],), token)
        return tuple(lax.ppermute(p, "row", X1) for p in passed), token

    def down_part(step, token):
        own, core, _ = hidden[step]
        return run(down_part_body, (like((rows, width), F32),), (down_near, own, core), token)

    def down_rest(step, part_sum, yd, first, token):
        outs = (like((part, width), F32),) + (like((part, width)),) * (3 + len(first))
        operands = (down_far, part_sum, hidden[step][2]) + first + yd
        body = functools.partial(down_rest_body, len(first))
        keep, send1, send2, send3, *passed, token = run(body, outs, operands, token)
        sent = [keep, lax.ppermute(send3, "col", X3), lax.ppermute(send2, "col", X2)]
        return sent, send1, passed, token

    token = activate(0, token)
    down_far, token = down_rows(1, token)
    part0, token = down_part(0, token)
    token = activate(1, token)
    yd0, token = shared(0, token)
    part1, token = down_part(1, token)
    sums0, first, _, token = down_rest(0, part0, yd0, (), token)
    yd1, token = shared(1, token)
    sums1, second, passed, token = down_rest(1, part1, yd1, (first,), token)
    sums = sums0 + sums1 + [lax.ppermute(s, "col", X1) for s in (second, passed[0])]
    own, core, y, yd, token = run(owner_body, (like((steps, MEAN, width)),) * 4, tuple(sums), token)
    blocks = (own, lax.ppermute(core, "row", X1), lax.ppermute(y, "row", X2), lax.ppermute(yd, "row", X3))
    result, _ = run(output_body, (like((steps, MEAN, 4 * width)),), blocks, token)
    return result


def layer_block(normed_block, counts_block, assign_block, paired, down_w, hidden_cols):
    row_devices = lax.axis_size("row")
    col_devices = lax.axis_size("col")
    step_count = normed_block.shape[0]
    capacity = normed_block.shape[1]
    rows_step = MEAN * counts_block.shape[1]
    spread = lax.all_to_all(normed_block, "row", split_axis=2, concat_axis=1, tiled=True)
    gathered = lax.all_gather(spread, "col", axis=1, tiled=True)
    slot_count = gathered.shape[1]
    stacked = gathered.reshape(step_count * slot_count, gathered.shape[2])
    targets = (
        assign_block.reshape(step_count, row_devices, col_devices, capacity)
        .transpose(0, 2, 1, 3)
        .reshape(step_count, slot_count)
    )
    holdings = counts_block.reshape(step_count, row_devices, col_devices).transpose(0, 2, 1)
    slot_grid = lax.broadcasted_iota(jnp.int32, (step_count, col_devices, row_devices, capacity), 3)
    live_mask = (slot_grid < holdings[..., None]).reshape(step_count, slot_count)
    targets = jnp.where(live_mask, targets, rows_step)
    slot_ids = lax.broadcasted_iota(jnp.int32, (step_count, slot_count), 1)
    step_ids = lax.broadcasted_iota(jnp.int32, (step_count, slot_count), 0)
    inverse = (
        jnp.zeros((step_count, rows_step), jnp.int32)
        .at[step_ids, targets]
        .set(slot_ids, mode="drop")
    )
    grid_shape = (col_devices, row_devices, step_count, MEAN)
    col_ids = lax.broadcasted_iota(jnp.int32, grid_shape, 0)
    row_ids = lax.broadcasted_iota(jnp.int32, grid_shape, 1)
    step_grid = lax.broadcasted_iota(jnp.int32, grid_shape, 2)
    member = lax.broadcasted_iota(jnp.int32, grid_shape, 3)
    row_numbers = (row_ids * col_devices + col_ids) * MEAN + member
    positions = (step_grid * slot_count + inverse[step_grid, row_numbers]).reshape(-1)
    inputs = jnp.take(stacked, positions, axis=0)
    rows_here = inputs
    gate_up = lax.psum_scatter(
        jnp.dot(rows_here, paired, preferred_element_type=jnp.float32).astype(jnp.bfloat16),
        "row",
        scatter_dimension=0,
        tiled=True,
    ).astype(jnp.float32)
    hidden = (jax.nn.silu(gate_up[:, :hidden_cols]) * gate_up[:, hidden_cols:]).astype(jnp.bfloat16)
    hidden_all = lax.all_gather(hidden, "row", axis=0, tiled=True)
    rows_here = hidden_all
    summed = lax.psum_scatter(
        jnp.dot(rows_here, down_w, preferred_element_type=jnp.float32).astype(jnp.bfloat16),
        "col",
        scatter_dimension=0,
        tiled=True,
    )
    finished = lax.all_to_all(summed, "row", split_axis=0, concat_axis=1, tiled=True)
    return finished.reshape(step_count, MEAN, finished.shape[1])


def any_plan(sender_rows, counts, assign, gate_w, up_w, down_w):
    values = sender_rows.astype(jnp.float32)
    normed = (
        values * lax.rsqrt(jnp.mean(values * values, axis=-1, keepdims=True) + epsilon)
    ).astype(jnp.bfloat16)
    paired = jnp.concatenate((gate_w, up_w), axis=1)
    hidden_cols = gate_w.shape[1]
    outputs = []
    for step_index in range(STEPS):
        outputs.append(
            layer_block(
                normed[step_index : step_index + 1],
                counts[step_index : step_index + 1],
                assign[step_index : step_index + 1],
                paired,
                down_w,
                hidden_cols,
            )
        )
    result = jnp.concatenate(outputs, axis=0)
    return result


def solution(mesh):
    near = mesh.shape["row"] == 4 and mesh.shape["col"] == 4
    return jax.shard_map(
        near_plan if near else any_plan,
        mesh=mesh,
        in_specs=(
            P(None, ("groups", "row", "col"), None),
            P(None, "groups"),
            P(None, "groups"),
            P("row", "col"),
            P("row", "col"),
            P("col", "row"),
        ),
        out_specs=P(None, ("groups", "row", "col"), None),
        check_vma=False,
    )
```

```python
import functools

import jax
import jax.numpy as jnp
from jax import lax
from jax.experimental import pallas as pl
from jax.experimental.pallas import tpu as pltpu
from jax.sharding import PartitionSpec as P

STEPS = 2
MEAN = 4

epsilon = 1e-05

BF = jnp.bfloat16
F32 = jnp.float32
MIB = 2**20
PIECES = 2
CUTS = 2
X1 = ((0, 1), (1, 0), (2, 3), (3, 2))
X2 = ((0, 2), (1, 3), (2, 0), (3, 1))
X3 = ((0, 3), (1, 2), (2, 1), (3, 0))


def place():
    row = lax.axis_index("row")
    return row // 2, lax.rem(row, 2), lax.axis_index("col")


def run(body, outs, operands, token, weights=(), scratch=(), cost=1, spec=None):
    count, held = len(operands), len(weights)
    skip = count + held + (token is not None)
    vmem = pl.BlockSpec(memory_space=pltpu.VMEM)
    outs = tuple(outs) + (like((8, 128), F32),)

    def wrapped(*refs):
        results = refs[skip:]
        body(refs[:count], refs[count : count + held], results[: len(outs) - 1], results[len(outs) :])
        results[len(outs) - 1][...] = jnp.zeros((8, 128), F32)

    return pl.pallas_call(
        wrapped,
        out_shape=outs,
        in_specs=[spec or vmem] * count
        + [pl.BlockSpec(memory_space=pltpu.HBM)] * held
        + [pl.BlockSpec(memory_space=pl.ANY)] * (token is not None),
        out_specs=(vmem,) * len(outs),
        scratch_shapes=scratch,
        compiler_params=pltpu.CompilerParams(vmem_limit_bytes=8 * MIB),
        cost_estimate=pl.CostEstimate(flops=0, bytes_accessed=cost, transcendentals=0),
    )(*operands, *(pltpu.with_memory_space_constraint(w, pltpu.HBM) for w in weights), *(() if token is None else (token,)))


def like(shape, dtype=BF):
    return jax.ShapeDtypeStruct(shape, dtype)


def norm_body(ins, _, outs, __):
    (rows_ref,) = ins
    y, c, _ = place()
    width = outs[0].shape[2]
    for step in range(rows_ref.shape[0]):
        total = jnp.sum(jnp.square(rows_ref[step].astype(F32)), axis=-1, keepdims=True)
        scale = lax.rsqrt(total / rows_ref.shape[2] + epsilon)
        for out, (dy, dc) in zip(outs, ((1, 0), (1, 1), (0, 1), (0, 0))):
            block = lax.bitwise_xor(y, dy) * 2 + lax.bitwise_xor(c, dc)
            at = pl.ds(pl.multiple_of(block * width, width), width)
            out[step] = (rows_ref[step, :, at].astype(F32) * scale).astype(BF)


def normed_blocks(sender_rows):
    steps, slots, width = sender_rows.shape
    return run(norm_body, (like((steps, slots, width // 4)),) * 4, (sender_rows,), None)


def pick_body(ins, _, outs, __):
    counts_ref, assign_ref = ins
    (pick_ref,) = outs
    y, c, z = place()
    rows = pick_ref.shape[0] // 2
    slots = assign_ref.shape[1]
    arrivals = pick_ref.shape[1]
    spread = (
        lax.broadcasted_iota(jnp.int32, (slots // 8, slots), 1) // 8
        == lax.broadcasted_iota(jnp.int32, (slots // 8, slots), 0)
    ).astype(F32)
    held = jnp.dot(counts_ref[...].astype(F32), spread, preferred_element_type=F32)
    slot = lax.rem(lax.broadcasted_iota(jnp.int32, (1, slots), 1), 8).astype(F32)
    at = lax.broadcasted_iota(jnp.int32, (rows, slots), 0)
    target = (lax.rem(at, 16) // 4) * 16 + lax.bitwise_xor(at // 16, z) * 4 + lax.rem(at, 4)
    p = lax.broadcasted_iota(jnp.int32, (slots, arrivals), 1)
    bit = lambda shift: lax.rem(lax.shift_right_logical(p, shift), 2)
    row = lax.bitwise_xor(bit(5), y) * 2 + lax.bitwise_xor(bit(4), c)
    sender = row * 4 + lax.bitwise_xor(lax.shift_right_logical(p, 6), z)
    source = sender * 8 + lax.rem(p, 8)
    entry = lax.broadcasted_iota(jnp.int32, (slots, arrivals), 0)
    for step in range(2):
        live = slot < held[step : step + 1]
        chosen = jnp.where(live, assign_ref[step : step + 1, :], -1)
        placed = (chosen == target).astype(F32).astype(BF)
        moved = ((entry == source) & (bit(3) == step)).astype(F32).astype(BF)
        pick_ref[step * rows : (step + 1) * rows, :] = jnp.dot(
            placed, moved, preferred_element_type=F32
        ).astype(BF)


def quarter_copies(dy, dc, weights, out_ref, sems):
    y, c, _ = place()
    width = out_ref.shape[1] // 2
    start = (lax.bitwise_xor(c, dc) * 2 + lax.bitwise_xor(y, dy)) * width
    at = pl.ds(pl.multiple_of(start, 128), width)
    return [
        pltpu.make_async_copy(w.at[:, at], out_ref.at[:, pl.ds(i * width, width)], sems.at[i])
        for i, w in enumerate(weights)
    ]


def quarter_body(dy, dc, ins, weights, outs, scratch):
    copies = quarter_copies(dy, dc, weights, outs[0], scratch[0])
    for copy in copies:
        copy.start()
    for copy in copies:
        copy.wait()


def dot_and_quarter_body(dy, dc, ins, weights, outs, scratch):
    copies = quarter_copies(dy, dc, weights, outs[-1], scratch[0])
    for copy in copies:
        copy.start()
    x_ref, w_ref = ins
    rows = outs[0].shape[0]

    @pl.loop(0, w_ref.shape[1] // 256)
    def _(i):
        at = pl.ds(pl.multiple_of(i * 256, 256), 256)
        total = jnp.dot(x_ref[...], w_ref[:, at], preferred_element_type=F32).astype(BF)
        for k, out in enumerate(outs[:-1]):
            out[:, at] = total[k * rows : (k + 1) * rows]

    for copy in copies:
        copy.wait()


def fetch_quarter(gate_w, up_w, dy, dc, token):
    shape = pltpu.VMEM((gate_w.shape[0], gate_w.shape[1] // 2), BF)
    return run(
        functools.partial(quarter_body, dy, dc),
        (shape,),
        (),
        token,
        (gate_w, up_w),
        (pltpu.SemaphoreType.DMA((2,)),),
    )


def down_rows_body(dy, ins, _, outs, scratch):
    y, c, _ = place()
    (out_ref,) = outs
    height = out_ref.shape[0] // 2
    copies = []
    for dc in range(2):
        start = (lax.bitwise_xor(c, dc) * 2 + lax.bitwise_xor(y, dy)) * height
        copies.append(
            pltpu.make_async_copy(
                ins[0].at[pl.ds(pl.multiple_of(start, 16), height), :],
                out_ref.at[pl.ds(dc * height, height), :],
                scratch[0].at[dc],
            )
        )
    for copy in copies:
        copy.start()
    for copy in copies:
        copy.wait()


def stack_body(ins, _, outs, __):
    for i, piece in enumerate(ins):
        joined = jnp.concatenate([piece[step].astype(F32) for step in range(2)], axis=0)
        outs[0][i * 16 : (i + 1) * 16, :] = joined.astype(BF)


def after_body(ins, _, outs, __):
    rows = outs[0].shape[0]
    for i, out in enumerate(outs):
        out[...] = ins[0][i * rows : (i + 1) * rows, :]


def halves_dot(x_ref, w_refs):
    total = 0.0
    height = w_refs[0].shape[0]
    for i, w_ref in enumerate(w_refs):
        at = slice(i * height, (i + 1) * height)
        total = total + jnp.dot(x_ref[:, at], w_ref[...], preferred_element_type=F32)
    return total


def store_rows(outs, value):
    rows = outs[0].shape[0]
    for i, out in enumerate(outs):
        out[...] = value[i * rows : (i + 1) * rows].astype(out.dtype)


def load_rows(refs):
    return jnp.concatenate([ref[...].astype(F32) for ref in refs], axis=0)


def first_body(ins, _, outs, scratch):
    pieces, pick_ref, w_refs = ins[:8], ins[8], ins[9:]
    batch_ref, pieces_out = outs[0], outs[1:]
    slots = scratch[0]
    height = pieces[0].shape[0]
    for i, piece in enumerate(pieces):
        slots[i * height : (i + 1) * height, :] = piece[...]
    batch_ref[...] = jnp.dot(pick_ref[...], slots[...], preferred_element_type=F32).astype(BF)
    store_rows(pieces_out, halves_dot(batch_ref, w_refs))


def dot_body(ins, _, outs, __):
    store_rows(outs, halves_dot(ins[0], ins[1:]))


def far_body(ins, _, outs, __):
    store_rows(outs, ins[0][...] + load_rows(ins[1:]))


def hidden_body(step, ins, _, outs, __):
    rows, width = outs[0].shape
    total = ins[0][step * rows : (step + 1) * rows, :] + ins[1][...].astype(F32) + load_rows(ins[2:])
    gate, up = total[:, :width], total[:, width:]
    outs[0][...] = (gate / (1.0 + jnp.exp(-gate)) * up).astype(BF)


def down_part_body(ins, _, outs, __):
    w_ref, own_ref, core_ref = ins
    height = w_ref.shape[0] // 2
    total = jnp.dot(own_ref[...], w_ref[:height, :], preferred_element_type=F32)
    outs[0][...] = total + jnp.dot(core_ref[...], w_ref[height:, :], preferred_element_type=F32)


def down_rest_body(count, ins, _, outs, __):
    w_ref, part_ref, y_ref = ins[:3]
    rows = outs[0].shape[0]
    height = w_ref.shape[0] // 2
    total = part_ref[...] + jnp.dot(y_ref[...], w_ref[:height, :], preferred_element_type=F32)
    yd = load_rows(ins[3 + count :]).astype(BF)
    total = total + jnp.dot(yd, w_ref[height:, :], preferred_element_type=F32)
    for i, out in enumerate(outs[:4]):
        out[...] = total[i * rows : (i + 1) * rows].astype(out.dtype)
    for given, out in zip(ins[3 : 3 + count], outs[4:]):
        out[...] = given[...]


def owner_body(ins, _, outs, __):
    y, c, _ = place()
    at = lax.broadcasted_iota(jnp.int32, (16, 16), 0)
    source = lax.bitwise_xor(at, (y * 2 + c) * 4)
    turn = (lax.broadcasted_iota(jnp.int32, (16, 16), 1) == source).astype(F32).astype(BF)
    for step in range(2):
        total = ins[step * 3][...]
        for got in (ins[step * 3 + 1], ins[step * 3 + 2], ins[7 - step]):
            total = total + got[...].astype(F32)
        turned = jnp.dot(turn, total.astype(BF), preferred_element_type=F32)
        for i, out in enumerate(outs):
            out[step] = turned[i * 4 : (i + 1) * 4].astype(BF)


def output_body(ins, _, outs, __):
    y, c, _ = place()
    width = ins[0].shape[2]
    for dy, dc, block in ((0, 0, ins[0]), (0, 1, ins[1]), (1, 0, ins[2]), (1, 1, ins[3])):
        source = lax.bitwise_xor(y, dy) * 2 + lax.bitwise_xor(c, dc)
        outs[0][:, :, pl.ds(pl.multiple_of(source * width, width), width)] = block[...]


def near_plan(sender_rows, counts, assign, gate_w, up_w, down_w):
    steps, slots, width = sender_rows.shape
    width //= 4
    units = gate_w.shape[1] // 4
    rows = MEAN * counts.shape[1]
    part = rows // 4

    def down_rows(dy, token):
        shape = pltpu.VMEM((down_w.shape[0] // 2, down_w.shape[1]), BF)
        scratch = (pltpu.SemaphoreType.DMA((2,)),)
        spec = pl.BlockSpec(memory_space=pl.ANY)
        return run(functools.partial(down_rows_body, dy), (shape,), (down_w,), token, (), scratch, spec=spec)

    y, yd, core, own, token = normed_blocks(sender_rows)
    y, yd = lax.ppermute(y, "row", X2), lax.ppermute(yd, "row", X3)
    core = lax.ppermute(core, "row", X1)
    quarters = {}

    def bring(dy, dc, token):
        w, token = fetch_quarter(gate_w, up_w, dy, dc, token)
        quarters.setdefault((dy, dc), []).append(w)
        return token

    block = like((4 * slots, width))
    near_block, token = run(stack_body, (block,), (own, core), token)
    near_sent = [lax.ppermute(near_block, "col", X3), lax.ppermute(near_block, "col", X1)]
    far_block, token = run(stack_body, (block,), (y, yd), token)
    far_sent = [lax.ppermute(far_block, "col", X3), lax.ppermute(far_block, "col", X1)]
    token = bring(1, 1, token)
    passed, token = run(after_body, (block,), (near_sent[0], near_sent[1]), token)
    near_sent.append(lax.ppermute(passed, "col", X1))
    token = bring(1, 0, token)
    pick, token = run(pick_body, (like((steps * rows, steps * assign.shape[1])),), (counts, assign), token)
    passed, token = run(after_body, (block,), (far_sent[0], far_sent[1]), token)
    far_sent.append(lax.ppermute(passed, "col", X1))
    token = bring(0, 1, token)
    pieces = []
    for dz in range(4):
        for own_block, sent in ((near_block, near_sent), (far_block, far_sent)):
            pieces.append((own_block, sent[1], sent[2], sent[0])[dz])

    bits = (like((steps * rows // PIECES, 2 * units)),) * PIECES
    wide = like((steps * rows, 2 * units), F32)
    batch, *out, token = run(
        first_body,
        (like((steps * rows, width)),) + bits,
        tuple(pieces) + (pick, *quarters[1, 1]),
        token,
        (),
        (pltpu.VMEM((32 * slots, width), BF),),
    )
    cores = tuple(lax.ppermute(o, "row", X1) for o in out)
    own_far, token = run(dot_body, (wide,), (batch, *quarters[1, 0]), token)
    *sends, token = run(far_body, (like((rows, 2 * units)),) * steps, (own_far,) + cores, token)
    gots = [lax.ppermute(send, "row", X2) for send in sends]
    last = pltpu.VMEM((gate_w.shape[0], gate_w.shape[1] // 2), BF)
    *out, last, token = run(
        functools.partial(dot_and_quarter_body, 0, 0),
        bits + (last,),
        (batch, *quarters[0, 1]),
        token,
        (gate_w, up_w),
        (pltpu.SemaphoreType.DMA((2,)),),
    )
    cores = tuple(lax.ppermute(o, "row", X1) for o in out)
    own_near, token = run(dot_body, (wide,), (batch, last), token)
    down_near, token = down_rows(0, token)
    hidden = []

    def activate(step, token):
        each = PIECES // steps
        near = cores[step * each : (step + 1) * each]
        operands = (own_near, gots[step]) + near
        body = functools.partial(hidden_body, step)
        result, token = run(body, (like((rows, units)),), operands, token)
        y = lax.ppermute(result, "row", X2)
        hidden.append((result, lax.ppermute(result, "row", X1), y))
        return token

    def shared(step, token):
        cut = (like((rows // CUTS, units)),) * CUTS
        *passed, token = run(after_body, cut, (hidden[step][2],), token)
        return tuple(lax.ppermute(p, "row", X1) for p in passed), token

    def shared(step, token):
        cut = (like((rows // CUTS, units)),) * CUTS
        *passed, token = run(after_body, cut, (hidden[step][2],), token)
        return tuple(lax.ppermute(p, "row", X1) for p in passed), token

    def down_part(step, token):
        own, core, _ = hidden[step]
        return run(down_part_body, (like((rows, width), F32),), (down_near, own, core), token)

    def down_rest(step, part_sum, yd, first, token):
        outs = (like((part, width), F32),) + (like((part, width)),) * (3 + len(first))
        operands = (down_far, part_sum, hidden[step][2]) + first + yd
        body = functools.partial(down_rest_body, len(first))
        keep, send1, send2, send3, *passed, token = run(body, outs, operands, token)
        sent = [keep, lax.ppermute(send3, "col", X3), lax.ppermute(send2, "col", X2)]
        return sent, send1, passed, token

    token = activate(0, token)
    down_far, token = down_rows(1, token)
    part0, token = down_part(0, token)
    token = activate(1, token)
    yd0, token = shared(0, token)
    part1, token = down_part(1, token)
    sums0, first, _, token = down_rest(0, part0, yd0, (), token)
    yd1, token = shared(1, token)
    sums1, second, passed, token = down_rest(1, part1, yd1, (first,), token)
    sums = sums0 + sums1 + [lax.ppermute(s, "col", X1) for s in (second, passed[0])]
    own, core, y, yd, token = run(owner_body, (like((steps, MEAN, width)),) * 4, tuple(sums), token)
    blocks = (own, lax.ppermute(core, "row", X1), lax.ppermute(y, "row", X2), lax.ppermute(yd, "row", X3))
    result, _ = run(output_body, (like((steps, MEAN, 4 * width)),), blocks, token)
    return result


def layer_block(normed_block, counts_block, assign_block, paired, down_w, hidden_cols):
    row_devices = lax.axis_size("row")
    col_devices = lax.axis_size("col")
    step_count = normed_block.shape[0]
    capacity = normed_block.shape[1]
    rows_step = MEAN * counts_block.shape[1]
    spread = lax.all_to_all(normed_block, "row", split_axis=2, concat_axis=1, tiled=True)
    gathered = lax.all_gather(spread, "col", axis=1, tiled=True)
    slot_count = gathered.shape[1]
    stacked = gathered.reshape(step_count * slot_count, gathered.shape[2])
    targets = (
        assign_block.reshape(step_count, row_devices, col_devices, capacity)
        .transpose(0, 2, 1, 3)
        .reshape(step_count, slot_count)
    )
    holdings = counts_block.reshape(step_count, row_devices, col_devices).transpose(0, 2, 1)
    slot_grid = lax.broadcasted_iota(jnp.int32, (step_count, col_devices, row_devices, capacity), 3)
    live_mask = (slot_grid < holdings[..., None]).reshape(step_count, slot_count)
    targets = jnp.where(live_mask, targets, rows_step)
    slot_ids = lax.broadcasted_iota(jnp.int32, (step_count, slot_count), 1)
    step_ids = lax.broadcasted_iota(jnp.int32, (step_count, slot_count), 0)
    inverse = (
        jnp.zeros((step_count, rows_step), jnp.int32)
        .at[step_ids, targets]
        .set(slot_ids, mode="drop")
    )
    grid_shape = (col_devices, row_devices, step_count, MEAN)
    col_ids = lax.broadcasted_iota(jnp.int32, grid_shape, 0)
    row_ids = lax.broadcasted_iota(jnp.int32, grid_shape, 1)
    step_grid = lax.broadcasted_iota(jnp.int32, grid_shape, 2)
    member = lax.broadcasted_iota(jnp.int32, grid_shape, 3)
    row_numbers = (row_ids * col_devices + col_ids) * MEAN + member
    positions = (step_grid * slot_count + inverse[step_grid, row_numbers]).reshape(-1)
    inputs = jnp.take(stacked, positions, axis=0)
    rows_here = inputs
    gate_up = lax.psum_scatter(
        jnp.dot(rows_here, paired, preferred_element_type=jnp.float32).astype(jnp.bfloat16),
        "row",
        scatter_dimension=0,
        tiled=True,
    ).astype(jnp.float32)
    hidden = (jax.nn.silu(gate_up[:, :hidden_cols]) * gate_up[:, hidden_cols:]).astype(jnp.bfloat16)
    hidden_all = lax.all_gather(hidden, "row", axis=0, tiled=True)
    rows_here = hidden_all
    summed = lax.psum_scatter(
        jnp.dot(rows_here, down_w, preferred_element_type=jnp.float32).astype(jnp.bfloat16),
        "col",
        scatter_dimension=0,
        tiled=True,
    )
    finished = lax.all_to_all(summed, "row", split_axis=0, concat_axis=1, tiled=True)
    return finished.reshape(step_count, MEAN, finished.shape[1])


def any_plan(sender_rows, counts, assign, gate_w, up_w, down_w):
    values = sender_rows.astype(jnp.float32)
    normed = (
        values * lax.rsqrt(jnp.mean(values * values, axis=-1, keepdims=True) + epsilon)
    ).astype(jnp.bfloat16)
    paired = jnp.concatenate((gate_w, up_w), axis=1)
    hidden_cols = gate_w.shape[1]
    outputs = []
    for step_index in range(STEPS):
        outputs.append(
            layer_block(
                normed[step_index : step_index + 1],
                counts[step_index : step_index + 1],
                assign[step_index : step_index + 1],
                paired,
                down_w,
                hidden_cols,
            )
        )
    result = jnp.concatenate(outputs, axis=0)
    return result


def solution(mesh):
    near = mesh.shape["row"] == 4 and mesh.shape["col"] == 4
    return jax.shard_map(
        near_plan if near else any_plan,
        mesh=mesh,
        in_specs=(
            P(None, ("groups", "row", "col"), None),
            P(None, "groups"),
            P(None, "groups"),
            P("row", "col"),
            P("row", "col"),
            P("col", "row"),
        ),
        out_specs=P(None, ("groups", "row", "col"), None),
        check_vma=False,
    )
```

```python
import functools

import jax
import jax.numpy as jnp
from jax import lax
from jax.experimental import pallas as pl
from jax.experimental.pallas import tpu as pltpu
from jax.sharding import PartitionSpec as P

STEPS = 2
MEAN = 4

epsilon = 1e-05

BF = jnp.bfloat16
F32 = jnp.float32
MIB = 2**20
PIECES = 2
CUTS = 2
X1 = ((0, 1), (1, 0), (2, 3), (3, 2))
X2 = ((0, 2), (1, 3), (2, 0), (3, 1))
X3 = ((0, 3), (1, 2), (2, 1), (3, 0))


def place():
    row = lax.axis_index("row")
    return row // 2, lax.rem(row, 2), lax.axis_index("col")


def run(body, outs, operands, token, weights=(), scratch=(), cost=1, spec=None):
    count, held = len(operands), len(weights)
    skip = count + held + (token is not None)
    vmem = pl.BlockSpec(memory_space=pltpu.VMEM)
    outs = tuple(outs) + (like((8, 128), F32),)

    def wrapped(*refs):
        results = refs[skip:]
        body(refs[:count], refs[count : count + held], results[: len(outs) - 1], results[len(outs) :])
        results[len(outs) - 1][...] = jnp.zeros((8, 128), F32)

    return pl.pallas_call(
        wrapped,
        out_shape=outs,
        in_specs=[spec or vmem] * count
        + [pl.BlockSpec(memory_space=pltpu.HBM)] * held
        + [pl.BlockSpec(memory_space=pl.ANY)] * (token is not None),
        out_specs=(vmem,) * len(outs),
        scratch_shapes=scratch,
        compiler_params=pltpu.CompilerParams(vmem_limit_bytes=8 * MIB),
        cost_estimate=pl.CostEstimate(flops=0, bytes_accessed=cost, transcendentals=0),
    )(*operands, *(pltpu.with_memory_space_constraint(w, pltpu.HBM) for w in weights), *(() if token is None else (token,)))


def like(shape, dtype=BF):
    return jax.ShapeDtypeStruct(shape, dtype)


def norm_body(ins, _, outs, __):
    (rows_ref,) = ins
    y, c, _ = place()
    width = outs[0].shape[2]
    for step in range(rows_ref.shape[0]):
        total = jnp.sum(jnp.square(rows_ref[step].astype(F32)), axis=-1, keepdims=True)
        scale = lax.rsqrt(total / rows_ref.shape[2] + epsilon)
        for out, (dy, dc) in zip(outs, ((1, 0), (1, 1), (0, 1), (0, 0))):
            block = lax.bitwise_xor(y, dy) * 2 + lax.bitwise_xor(c, dc)
            at = pl.ds(pl.multiple_of(block * width, width), width)
            out[step] = (rows_ref[step, :, at].astype(F32) * scale).astype(BF)


def normed_blocks(sender_rows):
    steps, slots, width = sender_rows.shape
    return run(norm_body, (like((steps, slots, width // 4)),) * 4, (sender_rows,), None)


def pick_body(ins, _, outs, __):
    counts_ref, assign_ref = ins
    (pick_ref,) = outs
    y, c, z = place()
    rows = pick_ref.shape[0] // 2
    slots = assign_ref.shape[1]
    arrivals = pick_ref.shape[1]
    spread = (
        lax.broadcasted_iota(jnp.int32, (slots // 8, slots), 1) // 8
        == lax.broadcasted_iota(jnp.int32, (slots // 8, slots), 0)
    ).astype(F32)
    held = jnp.dot(counts_ref[...].astype(F32), spread, preferred_element_type=F32)
    slot = lax.rem(lax.broadcasted_iota(jnp.int32, (1, slots), 1), 8).astype(F32)
    at = lax.broadcasted_iota(jnp.int32, (rows, slots), 0)
    target = (lax.rem(at, 16) // 4) * 16 + lax.bitwise_xor(at // 16, z) * 4 + lax.rem(at, 4)
    p = lax.broadcasted_iota(jnp.int32, (slots, arrivals), 1)
    bit = lambda shift: lax.rem(lax.shift_right_logical(p, shift), 2)
    row = lax.bitwise_xor(bit(5), y) * 2 + lax.bitwise_xor(bit(4), c)
    sender = row * 4 + lax.bitwise_xor(lax.shift_right_logical(p, 6), z)
    source = sender * 8 + lax.rem(p, 8)
    entry = lax.broadcasted_iota(jnp.int32, (slots, arrivals), 0)
    for step in range(2):
        live = slot < held[step : step + 1]
        chosen = jnp.where(live, assign_ref[step : step + 1, :], -1)
        placed = (chosen == target).astype(F32).astype(BF)
        moved = ((entry == source) & (bit(3) == step)).astype(F32).astype(BF)
        pick_ref[step * rows : (step + 1) * rows, :] = jnp.dot(
            placed, moved, preferred_element_type=F32
        ).astype(BF)


def quarter_copies(dy, dc, weights, out_ref, sems):
    y, c, _ = place()
    width = out_ref.shape[1] // 2
    start = (lax.bitwise_xor(c, dc) * 2 + lax.bitwise_xor(y, dy)) * width
    at = pl.ds(pl.multiple_of(start, 128), width)
    return [
        pltpu.make_async_copy(w.at[:, at], out_ref.at[:, pl.ds(i * width, width)], sems.at[i])
        for i, w in enumerate(weights)
    ]


def quarter_body(dy, dc, ins, weights, outs, scratch):
    copies = quarter_copies(dy, dc, weights, outs[0], scratch[0])
    for copy in copies:
        copy.start()
    for copy in copies:
        copy.wait()


def dot_and_quarter_body(dy, dc, ins, weights, outs, scratch):
    copies = quarter_copies(dy, dc, weights, outs[-1], scratch[0])
    for copy in copies:
        copy.start()
    x_ref, w_ref = ins
    rows = outs[0].shape[0]

    @pl.loop(0, w_ref.shape[1] // 256)
    def _(i):
        at = pl.ds(pl.multiple_of(i * 256, 256), 256)
        total = jnp.dot(x_ref[...], w_ref[:, at], preferred_element_type=F32).astype(BF)
        for k, out in enumerate(outs[:-1]):
            out[:, at] = total[k * rows : (k + 1) * rows]

    for copy in copies:
        copy.wait()


def fetch_quarter(gate_w, up_w, dy, dc, token):
    shape = pltpu.VMEM((gate_w.shape[0], gate_w.shape[1] // 2), BF)
    return run(
        functools.partial(quarter_body, dy, dc),
        (shape,),
        (),
        token,
        (gate_w, up_w),
        (pltpu.SemaphoreType.DMA((2,)),),
    )


def down_rows_body(dy, ins, _, outs, scratch):
    y, c, _ = place()
    (out_ref,) = outs
    height = out_ref.shape[0] // 2
    copies = []
    for dc in range(2):
        start = (lax.bitwise_xor(c, dc) * 2 + lax.bitwise_xor(y, dy)) * height
        copies.append(
            pltpu.make_async_copy(
                ins[0].at[pl.ds(pl.multiple_of(start, 16), height), :],
                out_ref.at[pl.ds(dc * height, height), :],
                scratch[0].at[dc],
            )
        )
    for copy in copies:
        copy.start()
    for copy in copies:
        copy.wait()


def stack_body(ins, _, outs, __):
    for i, piece in enumerate(ins):
        joined = jnp.concatenate([piece[step].astype(F32) for step in range(2)], axis=0)
        outs[0][i * 16 : (i + 1) * 16, :] = joined.astype(BF)


def after_body(ins, _, outs, __):
    rows = outs[0].shape[0]
    for i, out in enumerate(outs):
        out[...] = ins[0][i * rows : (i + 1) * rows, :]


def halves_dot(x_ref, w_refs):
    total = 0.0
    height = w_refs[0].shape[0]
    for i, w_ref in enumerate(w_refs):
        at = slice(i * height, (i + 1) * height)
        total = total + jnp.dot(x_ref[:, at], w_ref[...], preferred_element_type=F32)
    return total


def store_rows(outs, value):
    rows = outs[0].shape[0]
    for i, out in enumerate(outs):
        out[...] = value[i * rows : (i + 1) * rows].astype(out.dtype)


def load_rows(refs):
    return jnp.concatenate([ref[...].astype(F32) for ref in refs], axis=0)


def first_body(ins, _, outs, scratch):
    pieces, pick_ref, w_refs = ins[:8], ins[8], ins[9:]
    batch_ref, pieces_out = outs[0], outs[1:]
    slots = scratch[0]
    height = pieces[0].shape[0]
    for i, piece in enumerate(pieces):
        slots[i * height : (i + 1) * height, :] = piece[...]
    batch_ref[...] = jnp.dot(pick_ref[...], slots[...], preferred_element_type=F32).astype(BF)
    store_rows(pieces_out, halves_dot(batch_ref, w_refs))


def dot_body(ins, _, outs, __):
    store_rows(outs, halves_dot(ins[0], ins[1:]))


def far_body(ins, _, outs, __):
    store_rows(outs, ins[0][...] + load_rows(ins[1:]))


def hidden_body(step, ins, _, outs, __):
    rows, width = outs[0].shape
    total = ins[0][step * rows : (step + 1) * rows, :] + ins[1][...].astype(F32) + load_rows(ins[2:])
    gate, up = total[:, :width], total[:, width:]
    outs[0][...] = (gate / (1.0 + jnp.exp(-gate)) * up).astype(BF)


def down_part_body(ins, _, outs, __):
    w_ref, own_ref, core_ref = ins
    height = w_ref.shape[0] // 2
    total = jnp.dot(own_ref[...], w_ref[:height, :], preferred_element_type=F32)
    outs[0][...] = total + jnp.dot(core_ref[...], w_ref[height:, :], preferred_element_type=F32)


def down_rest_body(count, ins, _, outs, __):
    w_ref, part_ref, y_ref = ins[:3]
    rows = outs[0].shape[0]
    height = w_ref.shape[0] // 2
    total = part_ref[...] + jnp.dot(y_ref[...], w_ref[:height, :], preferred_element_type=F32)
    yd = load_rows(ins[3 + count :]).astype(BF)
    total = total + jnp.dot(yd, w_ref[height:, :], preferred_element_type=F32)
    for i, out in enumerate(outs[:4]):
        out[...] = total[i * rows : (i + 1) * rows].astype(out.dtype)
    for given, out in zip(ins[3 : 3 + count], outs[4:]):
        out[...] = given[...]


def owner_body(ins, _, outs, __):
    y, c, _ = place()
    at = lax.broadcasted_iota(jnp.int32, (16, 16), 0)
    source = lax.bitwise_xor(at, (y * 2 + c) * 4)
    turn = (lax.broadcasted_iota(jnp.int32, (16, 16), 1) == source).astype(F32).astype(BF)
    for step in range(2):
        total = ins[step * 3][...]
        for got in (ins[step * 3 + 1], ins[step * 3 + 2], ins[7 - step]):
            total = total + got[...].astype(F32)
        turned = jnp.dot(turn, total.astype(BF), preferred_element_type=F32)
        for i, out in enumerate(outs):
            out[step] = turned[i * 4 : (i + 1) * 4].astype(BF)


def output_body(ins, _, outs, __):
    y, c, _ = place()
    width = ins[0].shape[2]
    for dy, dc, block in ((0, 0, ins[0]), (0, 1, ins[1]), (1, 0, ins[2]), (1, 1, ins[3])):
        source = lax.bitwise_xor(y, dy) * 2 + lax.bitwise_xor(c, dc)
        outs[0][:, :, pl.ds(pl.multiple_of(source * width, width), width)] = block[...]


def near_plan(sender_rows, counts, assign, gate_w, up_w, down_w):
    steps, slots, width = sender_rows.shape
    width //= 4
    units = gate_w.shape[1] // 4
    rows = MEAN * counts.shape[1]
    part = rows // 4

    def down_rows(dy, token):
        shape = pltpu.VMEM((down_w.shape[0] // 2, down_w.shape[1]), BF)
        scratch = (pltpu.SemaphoreType.DMA((2,)),)
        spec = pl.BlockSpec(memory_space=pl.ANY)
        return run(functools.partial(down_rows_body, dy), (shape,), (down_w,), token, (), scratch, spec=spec)

    y, yd, core, own, token = normed_blocks(sender_rows)
    y, yd = lax.ppermute(y, "row", X2), lax.ppermute(yd, "row", X3)
    core = lax.ppermute(core, "row", X1)
    quarters = {}

    def bring(dy, dc, token):
        w, token = fetch_quarter(gate_w, up_w, dy, dc, token)
        quarters.setdefault((dy, dc), []).append(w)
        return token

    block = like((4 * slots, width))
    near_block, token = run(stack_body, (block,), (own, core), token)
    near_sent = [lax.ppermute(near_block, "col", X3), lax.ppermute(near_block, "col", X1)]
    far_block, token = run(stack_body, (block,), (y, yd), token)
    far_sent = [lax.ppermute(far_block, "col", X3), lax.ppermute(far_block, "col", X1)]
    token = bring(1, 1, token)
    passed, token = run(after_body, (block,), (near_sent[0], near_sent[1]), token)
    near_sent.append(lax.ppermute(passed, "col", X1))
    token = bring(1, 0, token)
    pick, token = run(pick_body, (like((steps * rows, steps * assign.shape[1])),), (counts, assign), token)
    passed, token = run(after_body, (block,), (far_sent[0], far_sent[1]), token)
    far_sent.append(lax.ppermute(passed, "col", X1))
    token = bring(0, 1, token)
    pieces = []
    for dz in range(4):
        for own_block, sent in ((near_block, near_sent), (far_block, far_sent)):
            pieces.append((own_block, sent[1], sent[2], sent[0])[dz])

    bits = (like((steps * rows // PIECES, 2 * units)),) * PIECES
    wide = like((steps * rows, 2 * units), F32)
    batch, *out, token = run(
        first_body,
        (like((steps * rows, width)),) + bits,
        tuple(pieces) + (pick, *quarters[1, 1]),
        token,
        (),
        (pltpu.VMEM((32 * slots, width), BF),),
    )
    cores = tuple(lax.ppermute(o, "row", X1) for o in out)
    own_far, token = run(dot_body, (wide,), (batch, *quarters[1, 0]), token)
    *sends, token = run(far_body, (like((rows, 2 * units)),) * steps, (own_far,) + cores, token)
    gots = [lax.ppermute(send, "row", X2) for send in sends]
    last = pltpu.VMEM((gate_w.shape[0], gate_w.shape[1] // 2), BF)
    *out, last, token = run(
        functools.partial(dot_and_quarter_body, 0, 0),
        bits + (last,),
        (batch, *quarters[0, 1]),
        token,
        (gate_w, up_w),
        (pltpu.SemaphoreType.DMA((2,)),),
    )
    cores = tuple(lax.ppermute(o, "row", X1) for o in out)
    own_near, token = run(dot_body, (wide,), (batch, last), token)
    down_near, token = down_rows(0, token)
    hidden = []

    def activate(step, token):
        each = PIECES // steps
        near = cores[step * each : (step + 1) * each]
        operands = (own_near, gots[step]) + near
        body = functools.partial(hidden_body, step)
        result, token = run(body, (like((rows, units)),), operands, token)
        y = lax.ppermute(result, "row", X2)
        hidden.append((result, lax.ppermute(result, "row", X1), y))
        return token

    def shared(step, token):
        cut = (like((rows // CUTS, units)),) * CUTS
        *passed, token = run(after_body, cut, (hidden[step][2],), token)
        return tuple(lax.ppermute(p, "row", X1) for p in passed), token

    def shared(step, token):
        cut = (like((rows // CUTS, units)),) * CUTS
        *passed, token = run(after_body, cut, (hidden[step][2],), token)
        return tuple(lax.ppermute(p, "row", X1) for p in passed), token

    def down_part(step, token):
        own, core, _ = hidden[step]
        return run(down_part_body, (like((rows, width), F32),), (down_near, own, core), token)

    def down_rest(step, part_sum, yd, first, token):
        outs = (like((part, width), F32),) + (like((part, width)),) * (3 + len(first))
        operands = (down_far, part_sum, hidden[step][2]) + first + yd
        body = functools.partial(down_rest_body, len(first))
        keep, send1, send2, send3, *passed, token = run(body, outs, operands, token)
        sent = [keep, lax.ppermute(send3, "col", X3), lax.ppermute(send2, "col", X2)]
        return sent, send1, passed, token

    token = activate(0, token)
    down_far, token = down_rows(1, token)
    part0, token = down_part(0, token)
    token = activate(1, token)
    yd0, token = shared(0, token)
    sums0, first, _, token = down_rest(0, part0, yd0, (), token)
    part1, token = down_part(1, token)
    yd1, token = shared(1, token)
    sums1, second, passed, token = down_rest(1, part1, yd1, (first,), token)
    sums = sums0 + sums1 + [lax.ppermute(s, "col", X1) for s in (second, passed[0])]
    own, core, y, yd, token = run(owner_body, (like((steps, MEAN, width)),) * 4, tuple(sums), token)
    blocks = (own, lax.ppermute(core, "row", X1), lax.ppermute(y, "row", X2), lax.ppermute(yd, "row", X3))
    result, _ = run(output_body, (like((steps, MEAN, 4 * width)),), blocks, token)
    return result


def layer_block(normed_block, counts_block, assign_block, paired, down_w, hidden_cols):
    row_devices = lax.axis_size("row")
    col_devices = lax.axis_size("col")
    step_count = normed_block.shape[0]
    capacity = normed_block.shape[1]
    rows_step = MEAN * counts_block.shape[1]
    spread = lax.all_to_all(normed_block, "row", split_axis=2, concat_axis=1, tiled=True)
    gathered = lax.all_gather(spread, "col", axis=1, tiled=True)
    slot_count = gathered.shape[1]
    stacked = gathered.reshape(step_count * slot_count, gathered.shape[2])
    targets = (
        assign_block.reshape(step_count, row_devices, col_devices, capacity)
        .transpose(0, 2, 1, 3)
        .reshape(step_count, slot_count)
    )
    holdings = counts_block.reshape(step_count, row_devices, col_devices).transpose(0, 2, 1)
    slot_grid = lax.broadcasted_iota(jnp.int32, (step_count, col_devices, row_devices, capacity), 3)
    live_mask = (slot_grid < holdings[..., None]).reshape(step_count, slot_count)
    targets = jnp.where(live_mask, targets, rows_step)
    slot_ids = lax.broadcasted_iota(jnp.int32, (step_count, slot_count), 1)
    step_ids = lax.broadcasted_iota(jnp.int32, (step_count, slot_count), 0)
    inverse = (
        jnp.zeros((step_count, rows_step), jnp.int32)
        .at[step_ids, targets]
        .set(slot_ids, mode="drop")
    )
    grid_shape = (col_devices, row_devices, step_count, MEAN)
    col_ids = lax.broadcasted_iota(jnp.int32, grid_shape, 0)
    row_ids = lax.broadcasted_iota(jnp.int32, grid_shape, 1)
    step_grid = lax.broadcasted_iota(jnp.int32, grid_shape, 2)
    member = lax.broadcasted_iota(jnp.int32, grid_shape, 3)
    row_numbers = (row_ids * col_devices + col_ids) * MEAN + member
    positions = (step_grid * slot_count + inverse[step_grid, row_numbers]).reshape(-1)
    inputs = jnp.take(stacked, positions, axis=0)
    rows_here = inputs
    gate_up = lax.psum_scatter(
        jnp.dot(rows_here, paired, preferred_element_type=jnp.float32).astype(jnp.bfloat16),
        "row",
        scatter_dimension=0,
        tiled=True,
    ).astype(jnp.float32)
    hidden = (jax.nn.silu(gate_up[:, :hidden_cols]) * gate_up[:, hidden_cols:]).astype(jnp.bfloat16)
    hidden_all = lax.all_gather(hidden, "row", axis=0, tiled=True)
    rows_here = hidden_all
    summed = lax.psum_scatter(
        jnp.dot(rows_here, down_w, preferred_element_type=jnp.float32).astype(jnp.bfloat16),
        "col",
        scatter_dimension=0,
        tiled=True,
    )
    finished = lax.all_to_all(summed, "row", split_axis=0, concat_axis=1, tiled=True)
    return finished.reshape(step_count, MEAN, finished.shape[1])


def any_plan(sender_rows, counts, assign, gate_w, up_w, down_w):
    values = sender_rows.astype(jnp.float32)
    normed = (
        values * lax.rsqrt(jnp.mean(values * values, axis=-1, keepdims=True) + epsilon)
    ).astype(jnp.bfloat16)
    paired = jnp.concatenate((gate_w, up_w), axis=1)
    hidden_cols = gate_w.shape[1]
    outputs = []
    for step_index in range(STEPS):
        outputs.append(
            layer_block(
                normed[step_index : step_index + 1],
                counts[step_index : step_index + 1],
                assign[step_index : step_index + 1],
                paired,
                down_w,
                hidden_cols,
            )
        )
    result = jnp.concatenate(outputs, axis=0)
    return result


def solution(mesh):
    near = mesh.shape["row"] == 4 and mesh.shape["col"] == 4
    return jax.shard_map(
        near_plan if near else any_plan,
        mesh=mesh,
        in_specs=(
            P(None, ("groups", "row", "col"), None),
            P(None, "groups"),
            P(None, "groups"),
            P("row", "col"),
            P("row", "col"),
            P("col", "row"),
        ),
        out_specs=P(None, ("groups", "row", "col"), None),
        check_vma=False,
    )
```
